32 devices in a mesh: dp: 8 (over z, x), mp: 4 (over y, core).
Axes of the slice: x: 2, y: 2, z: 4, core: 2. Of those that a mesh axis runs over, the one named last changes fastest.
Arguments:
- frames: bfloat16 [16384, 1024], P('dp'), may hold values from -6 to 6
- clip_lengths: int32 [16, 8], P('dp'), may hold values from 0 to 250, as said below
- query_weight: bfloat16 [1024, 1024], P(None, 'mp'), may hold values from -0.1875 to 0.1875
- key_weight: bfloat16 [1024, 1024], P(None, 'mp'), may hold values from -0.1875 to 0.1875
- value_weight: bfloat16 [1024, 1024], P(None, 'mp'), may hold values from -0.1875 to 0.1875
- output_weight: bfloat16 [1024, 1024], P('mp'), may hold values from -1 to 1
- gate_weight: bfloat16 [1024, 4096], P(None, 'mp'), may hold values from -0.1875 to 0.1875
- up_weight: bfloat16 [1024, 4096], P(None, 'mp'), may hold values from -0.1875 to 0.1875
- down_weight: bfloat16 [4096, 1024], P('mp'), may hold values from -0.09375 to 0.09375
- attn_gain: float32 [1024], replicated, may hold values from 0.1 to 1.9
- attn_bias: float32 [1024], replicated, may hold values from -1.2 to 1.2
- mlp_gain: float32 [1024], replicated, may hold values from 0.1 to 1.9
- mlp_bias: float32 [1024], replicated, may hold values from -1.2 to 1.2
- attn_scale: float32 [1024], replicated, may hold values from 0.5 to 2
- mlp_scale: float32 [1024], replicated, may hold values from 0.5 to 2
- cotangent: bfloat16 [16384, 1024], P('dp'), may hold values from -6 to 6
Outputs:
- out_frames: bfloat16 [16384, 1024], P('dp')
- frames_grad: bfloat16 [16384, 1024], P('dp')
- query_weight_grad: float32 [1024, 1024], P('dp', 'mp')
- key_weight_grad: float32 [1024, 1024], P('dp', 'mp')
- value_weight_grad: float32 [1024, 1024], P('dp', 'mp')
- output_weight_grad: float32 [1024, 1024], P('mp', 'dp')
- gate_weight_grad: float32 [1024, 4096], P('dp', 'mp')
- up_weight_grad: float32 [1024, 4096], P('dp', 'mp')
- down_weight_grad: float32 [4096, 1024], P('mp', 'dp')
- attn_gain_grad: float32 [1024], P('dp')
- attn_bias_grad: float32 [1024], P('dp')
- mlp_gain_grad: float32 [1024], P('dp')
- mlp_bias_grad: float32 [1024], P('dp')
- attn_scale_grad: float32 [1024], P('dp')
- mlp_scale_grad: float32 [1024], P('dp')
The draws below stay inside these ranges and needn't reach their ends.
Inputs may be any that keep to these rules, and one draw needn't show every extreme that they name: `clip_lengths`: each entry is 0, 125 or 250; the first entry of every row is 250; the entries of a row sum to at most 1024; the frames of a row past that sum form one more segment.
All inputs are finite; a program needn't handle non-finite values.
Results may differ from the reference program's by a relative error of at most 0.02.
Values may be sent and summed in bfloat16 or wider, within the bound.
A program may use at most 192 MiB of HBM per device.

```python
import math
import jax
import jax.numpy as jnp
from jax import lax

D = 1024
HEADS = 16
HEAD_DIM = 64
FF = 4096
WINDOW = 128
ROW_LEN = 1024
BLOCK = 512
LONG_CLIP = 250
SHORT_CLIP = 125
SLOTS = 8
ROWS = 16
TOKENS = 16384
N_MP = 4


def draw_clip_lengths(key, part):
    key = jax.random.fold_in(key, 7)
    classes = jax.random.randint(key, (ROWS, SLOTS), 0, 2)
    wanted = jnp.where(classes == 0, LONG_CLIP, SHORT_CLIP).astype(jnp.int32)
    wanted = wanted.at[:, 0].set(LONG_CLIP)
    filled = jnp.zeros((ROWS,), jnp.int32)
    columns = []
    for column in range(SLOTS):
        taken = jnp.where(filled + wanted[:, column] <= ROW_LEN, wanted[:, column], 0).astype(jnp.int32)
        filled = filled + taken
        columns.append(taken)
    return jnp.stack(columns, 1).astype(jnp.int32)


def strengthened(entries, stream_key, source, target, parts, factor):
    owner, partner = [(jnp.arange(entries.shape[dim]) // (entries.shape[dim] // parts)).reshape([-1 if axis == dim else 1 for axis in range(entries.ndim)]) for dim in (source, target)]
    chosen = jax.random.permutation(stream_key, parts)[partner]
    strong = (owner == chosen) | (owner == (partner + parts // 2) % parts)
    return jnp.where(strong, factor * entries, entries)


def steps_of(key, dims, shards, least, top_value):
    level, own = 1.0, jax.random.fold_in(key, 6)
    for dim, parts in shards:
        heights = jnp.exp(jax.random.uniform(jax.random.fold_in(own, dim), (parts,), jnp.float32, least / len(shards), top_value / len(shards)))
        level = level * jnp.repeat(heights, dims[dim] // parts).reshape([-1 if axis == dim else 1 for axis in range(len(dims))])
    return level


def normal_values(key, shape, deviation, bound, shards=(), kind=jnp.bfloat16):
    values = deviation * jax.random.normal(key, shape, jnp.float32)
    if shards:
        values = values * steps_of(key, shape, shards, -0.22, 0.18)
    return jnp.clip(values, -bound, bound).astype(kind)


def gaussian_with(key, dims, scale, bound, shards, heavy, kind=jnp.bfloat16):
    drawn = scale * jax.random.normal(key, dims, jnp.float32)
    if shards:
        drawn = drawn * steps_of(key, dims, shards, -0.22, 0.18)
    return jnp.clip(strengthened(drawn, jax.random.fold_in(key, 3), *heavy), -bound, bound).astype(kind)


def setup_inputs(seed: int = 0) -> dict:
    streams_of = jax.random.split(jax.random.key(seed), 17)
    return {
        "frames": normal_values(streams_of[0], (TOKENS, D), 1.0, 6.0, ((0, 8),)),
        "clip_lengths": draw_clip_lengths(jax.random.fold_in(streams_of[16], 71), 0),
        "query_weight": normal_values(streams_of[2], (D, D), D ** -0.5, 0.1875, ((1, 4),)),
        "key_weight": normal_values(streams_of[3], (D, D), D ** -0.5, 0.1875, ((1, 4),)),
        "value_weight": normal_values(streams_of[4], (D, D), D ** -0.5, 0.1875, ((1, 4),)),
        "output_weight": normal_values(streams_of[5], (D, D), (D // 32) ** -0.5, 1.0, ((0, 4),)),
        "gate_weight": normal_values(streams_of[6], (D, FF), D ** -0.5, 0.1875, ((1, 4),)),
        "up_weight": normal_values(streams_of[7], (D, FF), D ** -0.5, 0.1875, ((1, 4),)),
        "down_weight": normal_values(streams_of[8], (FF, D), FF ** -0.5, 0.09375, ((0, 4),)),
        "attn_gain": jnp.clip(1.0 + 0.18 * jax.random.normal(streams_of[9], (D,), jnp.float32), 0.1, 1.9),
        "attn_bias": normal_values(streams_of[10], (D,), 0.3, 1.2, (), jnp.float32),
        "mlp_gain": jnp.clip(1.0 + 0.18 * jax.random.normal(streams_of[11], (D,), jnp.float32), 0.1, 1.9),
        "mlp_bias": normal_values(streams_of[12], (D,), 0.3, 1.2, (), jnp.float32),
        "attn_scale": jnp.clip(jnp.exp(jax.random.uniform(streams_of[13], (D,), jnp.float32, math.log(0.5), math.log(2.0))), 0.5, 2.0),
        "mlp_scale": jnp.clip(jnp.exp(jax.random.uniform(streams_of[14], (D,), jnp.float32, math.log(0.5), math.log(2.0))), 0.5, 2.0),
        "cotangent": gaussian_with(streams_of[15], (TOKENS, D), 1.0, 6.0, ((0, 8),), (0, 1, 8, 2.0)),
    }


@jax.custom_vjp
def low(v):
    return lax.optimization_barrier(v.astype(jnp.bfloat16)).astype(jnp.float32)

@jax.custom_vjp
def low_back(v):
    return v

def low_keep(v):
    return (low(v), None)

def low_pass(kept, grad):
    return (grad,)

def back_keep(v):
    return (v, None)

def back_low(kept, grad):
    return (low(grad),)
low.defvjp(low_keep, low_pass)
low_back.defvjp(back_keep, back_low)

def precise_dot(left, right):
    return jnp.dot(left, right, precision=lax.Precision.HIGHEST, preferred_element_type=jnp.float32)

def clip_layout(lengths):
    ends = jnp.cumsum(lengths, axis=-1).astype(jnp.int32)
    frame_ids = jnp.arange(ROW_LEN, dtype=jnp.int32)
    passed = (frame_ids[None, :, None] >= ends[:, None, :]).astype(jnp.int32)
    segment = lax.optimization_barrier(jnp.sum(passed, axis=-1)).astype(jnp.int32)
    start_ids = lax.optimization_barrier(jnp.sum(passed * lengths[:, None, :], axis=-1)).astype(jnp.int32)
    return (segment, (frame_ids[None, :] - start_ids).astype(jnp.int32))

def rotary_tables(position):
    half_dim = HEAD_DIM // 2
    inverse = 10000.0 ** (-jnp.arange(half_dim, dtype=jnp.float32) / half_dim)
    angle = position.astype(jnp.float32)[:, None] * inverse[None, :]
    cosine = jnp.concatenate([jnp.cos(angle), jnp.cos(angle)], -1)
    sine = jnp.concatenate([jnp.sin(angle), jnp.sin(angle)], -1)
    return (cosine, sine)

def rotate(field, cosine, sine, direction):
    half_dim = field.shape[-1] // 2
    turned = jnp.concatenate([-field[..., half_dim:], field[..., :half_dim]], -1)
    return field * cosine[:, None, :] + direction * turned * sine[:, None, :]

def normalize(source, gain_vec, bias_vec):
    centre = lax.optimization_barrier(jnp.mean(source, -1, keepdims=True))
    centred = source - centre
    spread = lax.rsqrt(lax.optimization_barrier(jnp.mean(centred * centred, -1, keepdims=True)) + 1e-05)
    return centred * spread * gain_vec + bias_vec

def band_mask():
    row_ids = jnp.arange(BLOCK)[:, None]
    col_ids = jnp.arange(BLOCK + WINDOW)[None, :]
    return (col_ids > row_ids) & (col_ids <= row_ids + WINDOW)

def key_blocks(field, fill_value):
    row_count = field.shape[0] // ROW_LEN
    shaped = field.reshape((row_count, ROW_LEN) + field.shape[1:])
    widths = [(0, 0), (WINDOW, 0)] + [(0, 0)] * (field.ndim - 1)
    padded = jnp.pad(shaped, widths, constant_values=fill_value)
    block_count = ROW_LEN // BLOCK
    pieces = jnp.stack([padded[:, index_b * BLOCK:index_b * BLOCK + BLOCK + WINDOW] for index_b in range(block_count)], 1)
    return pieces.reshape((row_count * block_count, BLOCK + WINDOW) + field.shape[1:])

def attend_block(query_blk, key_blk, value_blk, seg_query, seg_key, band):
    raw_scores = jnp.einsum('qhd,khd->hqk', query_blk, key_blk, precision=lax.Precision.HIGHEST)
    allowed = band & (seg_query[:, None] == seg_key[None, :])
    logits = jnp.where(allowed[None], low_back(raw_scores) * HEAD_DIM ** (-0.5), -1e+30)
    weights = low(jax.nn.softmax(logits, axis=-1))
    return jnp.einsum('hqk,khd->qhd', weights, value_blk, precision=lax.Precision.HIGHEST)

def windowed_attention(query, keys, values, segment):
    frame_count = query.shape[0]
    band = band_mask()
    query_blocks = query.reshape(frame_count // BLOCK, BLOCK, HEADS, HEAD_DIM)
    seg_query = segment.reshape(frame_count // BLOCK, BLOCK)

    def block_item(element):
        return attend_block(element[0], element[1], element[2], element[3], element[4], band)
    outputs = lax.map(jax.checkpoint(block_item), (query_blocks, key_blocks(keys, 0.0), key_blocks(values, 0.0), seg_query, key_blocks(segment, -1)))
    return outputs.reshape(frame_count, D)

def forward(source, params, segment, position):
    query_weight, key_weight, value_weight, output_weight, gate_weight, up_weight, down_weight, attn_gain, attn_bias, mlp_gain, mlp_bias, attn_scale, mlp_scale = params
    frame_count = source.shape[0]
    low_attn = low(normalize(source, attn_gain, attn_bias))
    cosine, sine = rotary_tables(position)
    width = D // N_MP
    query_parts = []
    key_parts = []
    value_parts = []
    for member in range(N_MP):
        shared = low_back(low_attn)
        lower = member * width
        query_parts.append(low_back(precise_dot(shared, query_weight[:, lower:lower + width])))
        key_parts.append(low_back(precise_dot(shared, key_weight[:, lower:lower + width])))
        value_parts.append(precise_dot(shared, value_weight[:, lower:lower + width]))
    query = jnp.concatenate(query_parts, 1).reshape(frame_count, HEADS, HEAD_DIM)
    query = low(low_back(rotate(query, cosine, sine, 1.0)))
    keys = jnp.concatenate(key_parts, 1).reshape(frame_count, HEADS, HEAD_DIM)
    keys = low(low_back(rotate(keys, cosine, sine, 1.0)))
    values = low(low_back(jnp.concatenate(value_parts, 1))).reshape(frame_count, HEADS, HEAD_DIM)
    attended = low(low_back(windowed_attention(query, keys, values, segment)))
    attn_total = jnp.zeros((frame_count, D), jnp.float32)
    for member in range(N_MP):
        lower = member * width
        attn_total = attn_total + low(precise_dot(attended[:, lower:lower + width], output_weight[lower:lower + width, :]))
    attn_branch = low_back(attn_total)
    midway = source + attn_scale * attn_branch
    low_mlp = low(normalize(midway, mlp_gain, mlp_bias))
    hidden_width = FF // N_MP
    mlp_total = jnp.zeros((frame_count, D), jnp.float32)
    for member in range(N_MP):
        shared = low_back(low_mlp)
        lower = member * hidden_width
        gating = low_back(precise_dot(shared, gate_weight[:, lower:lower + hidden_width]))
        upward = low_back(precise_dot(shared, up_weight[:, lower:lower + hidden_width]))
        hidden = low(jax.nn.silu(gating) * upward)
        mlp_total = mlp_total + low(precise_dot(hidden, down_weight[lower:lower + hidden_width, :]))
    mlp_branch = low_back(mlp_total)
    return midway + mlp_scale * mlp_branch

def reference(frames, clip_lengths, query_weight, key_weight, value_weight, output_weight, gate_weight, up_weight, down_weight, attn_gain, attn_bias, mlp_gain, mlp_bias, attn_scale, mlp_scale, cotangent):
    group_rows = 4 if ROWS % 4 == 0 else 1
    group_count = ROWS // group_rows
    span_frames = group_rows * ROW_LEN
    weights = (query_weight.astype(jnp.float32), key_weight.astype(jnp.float32), value_weight.astype(jnp.float32), output_weight.astype(jnp.float32), gate_weight.astype(jnp.float32), up_weight.astype(jnp.float32), down_weight.astype(jnp.float32), attn_gain.astype(jnp.float32), attn_bias.astype(jnp.float32), mlp_gain.astype(jnp.float32), mlp_bias.astype(jnp.float32), attn_scale.astype(jnp.float32), mlp_scale.astype(jnp.float32))
    source_all = frames.astype(jnp.float32).reshape(group_count, span_frames, D)
    cotan_all = cotangent.astype(jnp.float32).reshape(group_count, span_frames, D)
    length_all = clip_lengths.reshape(group_count, group_rows, SLOTS)

    def group_step(totals, element):
        source, cotan, lengths = element
        segment, position = clip_layout(lengths)
        segment = segment.reshape(span_frames)
        position = position.reshape(span_frames)

        def layer_fn(source_in, *params):
            return forward(source_in, params, segment, position)
        result, pullback = jax.vjp(layer_fn, source, *weights)
        grads = pullback(cotan)
        totals = tuple((running + fresh for running, fresh in zip(totals, grads[1:])))
        return (totals, (result.astype(jnp.bfloat16), grads[0].astype(jnp.bfloat16)))
    zero_grads = tuple((jnp.zeros_like(weight_arr) for weight_arr in weights))
    totals, (results, source_grads) = lax.scan(group_step, zero_grads, (source_all, cotan_all, length_all))
    return (results.reshape(TOKENS, D), source_grads.reshape(TOKENS, D), totals[0], totals[1], totals[2], totals[3], totals[4], totals[5], totals[6], totals[7], totals[8], totals[9], totals[10], totals[11], totals[12])
```

```python
import jax
import jax.numpy as jnp
from jax import lax
from jax.sharding import PartitionSpec as P

HEAD_DIM = 64
WINDOW = 128
ROW_LEN = 1024
BLOCK = 512


def product(left, right, left_dim, right_dim):
    return lax.dot_general(
        left, right, (((left_dim,), (right_dim,)), ((), ())), preferred_element_type=jnp.float32
    )


def clip_layout(lengths):
    ends = jnp.cumsum(lengths, axis=-1)
    frame_ids = jnp.arange(ROW_LEN, dtype=jnp.int32)
    passed = (frame_ids[None, :, None] >= ends[:, None, :]).astype(jnp.int32)
    segment = jnp.sum(passed, axis=-1)
    start_ids = jnp.sum(passed * lengths[:, None, :], axis=-1)
    return (segment, frame_ids[None, :] - start_ids)


def rotary_tables(position):
    half_dim = HEAD_DIM // 2
    inverse = 10000.0 ** (-jnp.arange(half_dim, dtype=jnp.float32) / half_dim)
    angle = position.astype(jnp.float32)[:, None] * inverse[None, :]
    cosine = jnp.concatenate([jnp.cos(angle), jnp.cos(angle)], -1)
    sine = jnp.concatenate([jnp.sin(angle), jnp.sin(angle)], -1)
    return (cosine, sine)


def rotate(field, cosine, sine, direction):
    half_dim = field.shape[-1] // 2
    turned = jnp.concatenate([-field[..., half_dim:], field[..., :half_dim]], -1)
    return field * cosine[:, None, :] + direction * turned * sine[:, None, :]


def normalize(source, gain_vec, bias_vec):
    centre = jnp.mean(source, -1, keepdims=True)
    centred = source - centre
    spread = lax.rsqrt(jnp.mean(centred * centred, -1, keepdims=True) + 1e-05)
    unit_val = centred * spread
    return (unit_val * gain_vec + bias_vec, unit_val, spread)


def normalize_back(grad_in, unit_val, spread, gain_vec):
    scaled = grad_in * gain_vec
    inner = (
        scaled
        - jnp.mean(scaled, -1, keepdims=True)
        - unit_val * jnp.mean(scaled * unit_val, -1, keepdims=True)
    )
    return (inner * spread, jnp.sum(grad_in * unit_val, 0), jnp.sum(grad_in, 0))


def band_mask():
    row_ids = jnp.arange(BLOCK)[:, None]
    col_ids = jnp.arange(BLOCK + WINDOW)[None, :]
    return (col_ids > row_ids) & (col_ids <= row_ids + WINDOW)


def query_blocks(field):
    return field.reshape((field.shape[0] // BLOCK, BLOCK) + field.shape[1:])


def key_blocks(field, fill_value):
    row_count = field.shape[0] // ROW_LEN
    shaped = field.reshape((row_count, ROW_LEN) + field.shape[1:])
    widths = [(0, 0), (WINDOW, 0)] + [(0, 0)] * (field.ndim - 1)
    padded = jnp.pad(shaped, widths, constant_values=fill_value)
    block_count = ROW_LEN // BLOCK
    pieces = jnp.stack(
        [
            padded[:, index_b * BLOCK : index_b * BLOCK + BLOCK + WINDOW]
            for index_b in range(block_count)
        ],
        1,
    )
    return pieces.reshape((row_count * block_count, BLOCK + WINDOW) + field.shape[1:])


def key_blocks_back(extended):
    block_count = ROW_LEN // BLOCK
    row_count = extended.shape[0] // block_count
    trailing = extended.shape[2:]
    shaped = extended.reshape((row_count, block_count) + extended.shape[1:])
    own_part = shaped[:, :, WINDOW:]
    tail_part = shaped[:, 1:, :WINDOW]
    filler = jnp.zeros((row_count, block_count - 1, BLOCK - WINDOW) + trailing, extended.dtype)
    later = jnp.concatenate([filler, tail_part], 2)
    closing = jnp.zeros((row_count, 1, BLOCK) + trailing, extended.dtype)
    own_part = own_part + jnp.concatenate([later, closing], 1)
    return own_part.reshape((row_count * ROW_LEN,) + trailing)


def masked_logits(query_blk, key_blk, seg_query, seg_key, band):
    raw_scores = jnp.einsum("qhd,khd->hqk", query_blk, key_blk, preferred_element_type=jnp.float32)
    allowed = band & (seg_query[:, None] == seg_key[None, :])
    return jnp.where(allowed[None], raw_scores * HEAD_DIM ** (-0.5), -1e30)


def attend(query_blk, key_blk, value_blk, seg_query, seg_key, band):
    logits = masked_logits(query_blk, key_blk, seg_query, seg_key, band)
    highest = jnp.max(logits, -1, keepdims=True)
    expo = jnp.exp(logits - highest)
    summed = jnp.sum(expo, -1, keepdims=True)
    weights = (expo / summed).astype(jnp.bfloat16)
    result = jnp.einsum("hqk,khd->qhd", weights, value_blk, preferred_element_type=jnp.float32)
    return (result, (highest + jnp.log(summed))[..., 0])


def attend_back(query_blk, key_blk, value_blk, seg_query, seg_key, log_total, grad_blk, band):
    logits = masked_logits(query_blk, key_blk, seg_query, seg_key, band)
    probs = jnp.exp(logits - log_total[..., None])
    low_probs = probs.astype(jnp.bfloat16)
    grad_value = jnp.einsum("hqk,qhd->khd", low_probs, grad_blk, preferred_element_type=jnp.float32)
    grad_probs = jnp.einsum("qhd,khd->hqk", grad_blk, value_blk, preferred_element_type=jnp.float32)
    inner = jnp.sum(probs * grad_probs, -1, keepdims=True)
    grad_logits = (probs * (grad_probs - inner) * HEAD_DIM ** (-0.5)).astype(jnp.bfloat16)
    grad_query = jnp.einsum(
        "hqk,khd->qhd", grad_logits, key_blk, preferred_element_type=jnp.float32
    )
    grad_key = jnp.einsum(
        "hqk,qhd->khd", grad_logits, query_blk, preferred_element_type=jnp.float32
    )
    return (grad_query, grad_key, grad_value)


def rounded(field):
    return lax.optimization_barrier(field.astype(jnp.bfloat16)).astype(jnp.float32)


def scattered(field, axis, scatter_dimension, tiled):
    return lax.psum_scatter(
        field.astype(jnp.bfloat16), axis, scatter_dimension=scatter_dimension, tiled=tiled
    ).astype(jnp.float32)


def per_device(
    frames,
    clip_lengths,
    query_weight,
    key_weight,
    value_weight,
    output_weight,
    gate_weight,
    up_weight,
    down_weight,
    attn_gain,
    attn_bias,
    mlp_gain,
    mlp_bias,
    attn_scale,
    mlp_scale,
    cotangent,
):
    frame_count = frames.shape[0]
    local_heads = query_weight.shape[1] // HEAD_DIM
    segment, position = clip_layout(clip_lengths)
    segment = segment.reshape(frame_count)
    position = position.reshape(frame_count)
    cosine, sine = rotary_tables(position)
    band = band_mask()
    source = frames.astype(jnp.float32)
    normed_attn, unit_attn, spread_attn = normalize(source, attn_gain, attn_bias)
    low_attn = normed_attn.astype(jnp.bfloat16)
    query_pre = jnp.dot(low_attn, query_weight, preferred_element_type=jnp.float32).reshape(
        frame_count, local_heads, HEAD_DIM
    )
    key_pre = jnp.dot(low_attn, key_weight, preferred_element_type=jnp.float32).reshape(
        frame_count, local_heads, HEAD_DIM
    )
    query = rotate(query_pre, cosine, sine, 1.0).astype(jnp.bfloat16)
    keys = rotate(key_pre, cosine, sine, 1.0).astype(jnp.bfloat16)
    values = (
        jnp.dot(low_attn, value_weight, preferred_element_type=jnp.float32)
        .astype(jnp.bfloat16)
        .reshape(frame_count, local_heads, HEAD_DIM)
    )
    query_blk = query_blocks(query)
    key_blk = key_blocks(keys, 0.0)
    value_blk = key_blocks(values, 0.0)
    seg_query = query_blocks(segment)
    seg_key = key_blocks(segment, -1)

    def forward_item(element):
        return attend(element[0], element[1], element[2], element[3], element[4], band)

    outputs, log_totals = lax.map(forward_item, (query_blk, key_blk, value_blk, seg_query, seg_key))
    attended = outputs.reshape(frame_count, local_heads * HEAD_DIM).astype(jnp.bfloat16)
    attn_branch = lax.psum(
        jnp.dot(attended, output_weight, preferred_element_type=jnp.float32).astype(jnp.bfloat16),
        "mp",
    ).astype(jnp.float32)
    midway = source + attn_scale * attn_branch
    normed_mlp, unit_mlp, spread_mlp = normalize(midway, mlp_gain, mlp_bias)
    low_mlp = normed_mlp.astype(jnp.bfloat16)
    gating = jnp.dot(low_mlp, gate_weight, preferred_element_type=jnp.float32)
    upward = jnp.dot(low_mlp, up_weight, preferred_element_type=jnp.float32)
    activated = jax.nn.silu(gating)
    hidden = (activated * upward).astype(jnp.bfloat16)
    mlp_branch = lax.psum(
        jnp.dot(hidden, down_weight, preferred_element_type=jnp.float32).astype(jnp.bfloat16), "mp"
    ).astype(jnp.float32)
    out_frames = (midway + mlp_scale * mlp_branch).astype(jnp.bfloat16)
    grad_out = cotangent.astype(jnp.float32)
    mlp_scale_grad = jnp.sum(grad_out * mlp_branch, 0)
    grad_mlp_branch = (mlp_scale * grad_out).astype(jnp.bfloat16)
    down_grad = product(hidden, grad_mlp_branch, 0, 0)
    grad_hidden = product(grad_mlp_branch, down_weight, 1, 1)
    sigma = jax.nn.sigmoid(gating)
    grad_gating = (grad_hidden * upward * sigma * (1.0 + gating * (1.0 - sigma))).astype(
        jnp.bfloat16
    )
    grad_upward = (grad_hidden * activated).astype(jnp.bfloat16)
    gate_grad = product(low_mlp, grad_gating, 0, 0)
    upward_grad = product(low_mlp, grad_upward, 0, 0)
    grad_normed_mlp = lax.psum(
        (product(grad_gating, gate_weight, 1, 1) + product(grad_upward, up_weight, 1, 1)).astype(
            jnp.bfloat16
        ),
        "mp",
    ).astype(jnp.float32)
    grad_mid_norm, mlp_gain_grad, mlp_bias_grad = normalize_back(
        grad_normed_mlp, unit_mlp, spread_mlp, mlp_gain
    )
    grad_midway = grad_out + grad_mid_norm
    attn_scale_grad = jnp.sum(grad_midway * attn_branch, 0)
    grad_attn_branch = (attn_scale * grad_midway).astype(jnp.bfloat16)
    output_grad = product(attended, grad_attn_branch, 0, 0)
    grad_attended = (
        product(grad_attn_branch, output_weight, 1, 1)
        .astype(jnp.bfloat16)
        .reshape(frame_count, local_heads, HEAD_DIM)
    )

    def backward_item(element):
        return attend_back(
            element[0], element[1], element[2], element[3], element[4], element[5], element[6], band
        )

    grad_query_blk, grad_key_blk, grad_value_blk = lax.map(
        backward_item,
        (
            query_blk,
            key_blk,
            value_blk,
            seg_query,
            seg_key,
            log_totals,
            query_blocks(grad_attended),
        ),
    )
    grad_query_turned = rounded(grad_query_blk.reshape(frame_count, local_heads, HEAD_DIM))
    grad_key_turned = rounded(key_blocks_back(grad_key_blk))
    grad_query = (
        rotate(grad_query_turned, cosine, sine, -1.0)
        .reshape(frame_count, local_heads * HEAD_DIM)
        .astype(jnp.bfloat16)
    )
    grad_key = (
        rotate(grad_key_turned, cosine, sine, -1.0)
        .reshape(frame_count, local_heads * HEAD_DIM)
        .astype(jnp.bfloat16)
    )
    grad_value = (
        key_blocks_back(grad_value_blk)
        .reshape(frame_count, local_heads * HEAD_DIM)
        .astype(jnp.bfloat16)
    )
    query_grad = product(low_attn, grad_query, 0, 0)
    key_grad = product(low_attn, grad_key, 0, 0)
    value_grad = product(low_attn, grad_value, 0, 0)
    grad_normed_attn = lax.psum(
        (
            product(grad_query, query_weight, 1, 1)
            + product(grad_key, key_weight, 1, 1)
            + product(grad_value, value_weight, 1, 1)
        ).astype(jnp.bfloat16),
        "mp",
    ).astype(jnp.float32)
    grad_source_norm, attn_gain_grad, attn_bias_grad = normalize_back(
        grad_normed_attn, unit_attn, spread_attn, attn_gain
    )
    frames_grad = (grad_midway + grad_source_norm).astype(jnp.bfloat16)
    all_parts = (
        scattered(query_grad, "dp", scatter_dimension=0, tiled=True),
        scattered(key_grad, "dp", scatter_dimension=0, tiled=True),
        scattered(value_grad, "dp", scatter_dimension=0, tiled=True),
        scattered(output_grad, "dp", scatter_dimension=1, tiled=True),
        scattered(gate_grad, "dp", scatter_dimension=0, tiled=True),
        scattered(upward_grad, "dp", scatter_dimension=0, tiled=True),
        scattered(down_grad, "dp", scatter_dimension=1, tiled=True),
        lax.psum_scatter(attn_gain_grad, "dp", scatter_dimension=0, tiled=True),
        lax.psum_scatter(attn_bias_grad, "dp", scatter_dimension=0, tiled=True),
        lax.psum_scatter(mlp_gain_grad, "dp", scatter_dimension=0, tiled=True),
        lax.psum_scatter(mlp_bias_grad, "dp", scatter_dimension=0, tiled=True),
        lax.psum_scatter(attn_scale_grad, "dp", scatter_dimension=0, tiled=True),
        lax.psum_scatter(mlp_scale_grad, "dp", scatter_dimension=0, tiled=True),
    )
    return (
        out_frames,
        frames_grad,
        all_parts[0],
        all_parts[1],
        all_parts[2],
        all_parts[3],
        all_parts[4],
        all_parts[5],
        all_parts[6],
        all_parts[7],
        all_parts[8],
        all_parts[9],
        all_parts[10],
        all_parts[11],
        all_parts[12],
    )


def solution(mesh):
    in_specs = (
        P("dp", None),
        P("dp", None),
        P(None, "mp"),
        P(None, "mp"),
        P(None, "mp"),
        P("mp", None),
        P(None, "mp"),
        P(None, "mp"),
        P("mp", None),
        P(),
        P(),
        P(),
        P(),
        P(),
        P(),
        P("dp", None),
    )
    out_specs = (
        P("dp", None),
        P("dp", None),
        P("dp", "mp"),
        P("dp", "mp"),
        P("dp", "mp"),
        P("mp", "dp"),
        P("dp", "mp"),
        P("dp", "mp"),
        P("mp", "dp"),
        P("dp"),
        P("dp"),
        P("dp"),
        P("dp"),
        P("dp"),
        P("dp"),
    )
    return jax.shard_map(
        per_device, mesh=mesh, in_specs=in_specs, out_specs=out_specs, check_vma=False
    )
```

```python
import functools

import jax
import jax.numpy as jnp
from jax import lax
from jax.experimental import pallas as pl
from jax.experimental.pallas import tpu as pltpu
from jax.sharding import PartitionSpec as P

HEAD_DIM = 64
WINDOW = 128
ROW_LEN = 1024
QUARTER = 512
PIECE = 256
D = 1024
F32 = jnp.float32
BF16 = jnp.bfloat16
MESH = pl.DeviceIdType.MESH
MIB = 2**20


def product(left, right, left_dim, right_dim):
    return lax.dot_general(
        left, right, (((left_dim,), (right_dim,)), ((), ())), preferred_element_type=F32
    )


def position_tables(lengths):
    ends = jnp.cumsum(lengths, axis=-1)
    frame_ids = jnp.arange(ROW_LEN, dtype=jnp.int32)
    passed = (frame_ids[None, :, None] >= ends[:, None, :]).astype(jnp.int32)
    start_ids = jnp.sum(passed * lengths[:, None, :], axis=-1)
    position = frame_ids[None, :] - start_ids
    half_dim = HEAD_DIM // 2
    inverse = 10000.0 ** (-jnp.arange(half_dim, dtype=F32) / half_dim)
    angle = position.astype(F32)[:, :, None] * inverse
    cosine, sine = jnp.cos(angle), jnp.sin(angle)
    cosine = jnp.concatenate([cosine] * 4, -1)
    sine = jnp.concatenate([-sine, sine] * 2, -1)
    limit = jnp.minimum(position, WINDOW - 1).astype(F32)
    return cosine, sine, jnp.broadcast_to(limit[:, :, None], limit.shape + (128,))


def places():
    data, model = lax.axis_index("dp"), lax.axis_index("mp")
    core, side = model % 2, model // 2
    return data, core, side, (data, model + 1 - 2 * core), (data, model + 2 - 4 * side)


def meet(partners):
    barrier = pltpu.get_barrier_semaphore()
    for partner in partners:
        pl.semaphore_signal(barrier, inc=1, device_id=partner, device_id_type=MESH)
    pl.semaphore_wait(barrier, len(partners))


class Sends:
    def __init__(self, send_sems, recv_sems):
        self.send_sems, self.recv_sems, self.made = send_sems, recv_sems, []

    def copy(self, index, source, target, partner):
        return pltpu.make_async_remote_copy(
            src_ref=source,
            dst_ref=target,
            send_sem=self.send_sems.at[index],
            recv_sem=self.recv_sems.at[index],
            device_id=partner,
            device_id_type=MESH,
        )

    def start(self, index, source, target, partner):
        made = self.copy(index, source, target, partner)
        made.start()
        self.made.append(made)
        return made


def turned_by(field, cosine, sine):
    lane = lax.broadcasted_iota(jnp.int32, (1, 128), 1)
    lower = lane % HEAD_DIM < HEAD_DIM // 2
    halves = []
    for pair in range(field.shape[1] // 128):
        part = field[:, pair * 128 : pair * 128 + 128]
        swapped = jnp.where(lower, pltpu.roll(part, 96, 1), pltpu.roll(part, 32, 1))
        halves.append(part * cosine + swapped * sine)
    return jnp.concatenate(halves, 1)


def norm_of(source):
    centre = jnp.mean(source, -1, keepdims=True)
    centred = source - centre
    spread = lax.rsqrt(jnp.mean(centred * centred, -1, keepdims=True) + 1e-05)
    return centred * spread, spread


def window_bias(limit):
    row_ids = lax.broadcasted_iota(jnp.int32, (WINDOW, 2 * WINDOW), 0)
    col_ids = lax.broadcasted_iota(jnp.int32, (WINDOW, 2 * WINDOW), 1)
    distance = (row_ids - col_ids + WINDOW).astype(F32)
    both = jnp.concatenate([limit, limit], 1)
    return jnp.where((distance >= 0) & (distance <= both), 0.0, -1e30)


def split_heads(pair):
    lane = lax.broadcasted_iota(jnp.int32, pair.shape, 1)
    zero = jnp.zeros_like(pair)
    return jnp.concatenate(
        [jnp.where(lane < HEAD_DIM, pair, zero), jnp.where(lane >= HEAD_DIM, pair, zero)], 0
    )


def join_heads(stacked):
    rows = stacked.shape[0] // 2
    lane = lax.broadcasted_iota(jnp.int32, (rows, 128), 1)
    return jnp.where(lane < HEAD_DIM, stacked[:rows], stacked[rows:])


def attn_forward_kernel(
    frames, wq, wk, wv, wo, gain1, bias1, gain2, bias2, scale1, cosine, sine, limit,
    low_out, q_out, k_out, v_out, att_out, branch_out, mlp_out,
    frame_buf, low_buf, q_buf, k_buf, v_buf, att_buf, part, core_in, side_out, side_in,
    branch_buf, mlp_buf, load_sems, store_sems, send_sems, recv_sems,
):
    data, core, side, core_dev, side_dev = places()
    loads = []
    for index, row in enumerate((1 - side, side)):
        loads.append(
            pltpu.make_async_copy(
                frames.at[pl.ds(pl.multiple_of(row * ROW_LEN, ROW_LEN), ROW_LEN)],
                frame_buf.at[index],
                load_sems.at[index],
            )
        )
        loads[-1].start()
    meet([core_dev, side_dev])
    sends = Sends(send_sems, recv_sems)
    stores = []

    def store(source, target):
        copy = pltpu.make_async_copy(source, target, store_sems.at[len(stores)])
        copy.start()
        stores.append(copy)

    for index in range(2):
        for buf in (q_buf, k_buf, v_buf):
            buf[index, :WINDOW] = jnp.zeros((WINDOW, 256), BF16)

    core_copies, side_copies = [], []
    for index in range(2):
        loads[index].wait()

        @pl.loop(0, ROW_LEN // PIECE)
        def _(step):
            rows = pl.ds(pl.multiple_of(step * PIECE, PIECE), PIECE)
            shifted = pl.ds(pl.multiple_of(step * PIECE + WINDOW, WINDOW), PIECE)
            unit, _spread = norm_of(frame_buf[index, rows].astype(F32))
            low = (unit * gain1[...] + bias1[...]).astype(BF16)
            low_buf[index, rows] = low
            cos_rows, sin_rows = cosine[index, rows], sine[index, rows]
            q_buf[index, shifted] = turned_by(product(low, wq[...], 1, 0), cos_rows, sin_rows).astype(BF16)
            k_buf[index, shifted] = turned_by(product(low, wk[...], 1, 0), cos_rows, sin_rows).astype(BF16)
            v_buf[index, shifted] = product(low, wv[...], 1, 0).astype(BF16)

        store(low_buf.at[index], low_out.at[index])
        store(q_buf.at[index], q_out.at[index])
        store(k_buf.at[index], k_out.at[index])
        store(v_buf.at[index], v_out.at[index])

        for slot in range(2):
            half = (1 - core) if slot == 0 else core

            @pl.loop(0, QUARTER // PIECE)
            def _(step):
                base = pl.multiple_of(half * QUARTER + step * PIECE, PIECE)
                for block in range(PIECE // WINDOW):
                    first = base + block * WINDOW
                    rows = pl.ds(pl.multiple_of(first, WINDOW), WINDOW)
                    own_rows = pl.ds(pl.multiple_of(first + WINDOW, WINDOW), WINDOW)
                    key_rows = pl.ds(pl.multiple_of(first, WINDOW), 2 * WINDOW)
                    bias = window_bias(limit[index, rows])
                    bias = jnp.concatenate([bias, bias], 0)
                    for pair in range(2):
                        lanes = slice(pair * 128, pair * 128 + 128)
                        query = split_heads(q_buf[index, own_rows, lanes])
                        scores = product(query, k_buf[index, key_rows, lanes], 1, 1)
                        scores = scores * HEAD_DIM**-0.5 + bias
                        expo = jnp.exp(scores - jnp.max(scores, -1, keepdims=True))
                        total = jnp.sum(expo, -1, keepdims=True)
                        result = product(expo.astype(BF16), v_buf[index, key_rows, lanes], 1, 0)
                        att_buf[index, rows, lanes] = join_heads(result * (1.0 / total)).astype(BF16)
                rows = pl.ds(base, PIECE)
                here = pl.ds(pl.multiple_of(step * PIECE, PIECE), PIECE)
                part[index, slot, here] = product(att_buf[index, rows], wo[...], 1, 0).astype(BF16)

            if slot == 0:
                core_copies.append(sends.start(index, part.at[index, 0], core_in.at[index], core_dev))
        store(att_buf.at[index], att_out.at[index])
        core_copies[index].wait_recv()
        if index == 0:
            for step in range(2):
                rows = slice(step * PIECE, step * PIECE + PIECE)
                side_out[rows] = (part[0, 1, rows].astype(F32) + core_in[0, rows].astype(F32)).astype(BF16)
                side_copies.append(
                    sends.start(2 + step, side_out.at[pl.ds(step * PIECE, PIECE)], side_in.at[pl.ds(step * PIECE, PIECE)], side_dev)
                )

    side_gathers, core_gathers = [], []
    for step in range(2):
        rows = slice(step * PIECE, step * PIECE + PIECE)
        span = pl.ds(step * PIECE, PIECE)
        side_copies[step].wait_recv()
        branch = part[1, 1, rows].astype(F32) + core_in[1, rows].astype(F32) + side_in[rows].astype(F32)
        branch_buf[rows] = branch
        source = frame_buf[1, pl.ds(pl.multiple_of(core * QUARTER + step * PIECE, PIECE), PIECE)].astype(F32)
        unit, _spread = norm_of(source + scale1[...] * branch)
        mlp_buf[rows] = (unit * gain2[...] + bias2[...]).astype(BF16)
        side_gathers.append(sends.start(4 + step, mlp_buf.at[span], mlp_out.at[0, 1, span], side_dev))
        core_gathers.append(sends.start(6 + step, mlp_buf.at[span], mlp_out.at[1, 0, span], core_dev))
    store(mlp_buf, mlp_out.at[1, 1])
    store(branch_buf, branch_out)
    for step in range(2):
        span = pl.ds(step * PIECE, PIECE)
        side_gathers[step].wait_recv()
        core_gathers.append(sends.start(8 + step, mlp_out.at[0, 1, span], mlp_out.at[0, 0, span], core_dev))
    for copy in core_gathers:
        copy.wait_recv()
    for copy in sends.made:
        copy.wait_send()
    for copy in stores:
        copy.wait()


def vmem():
    return pl.BlockSpec(memory_space=pltpu.VMEM)


def hbm():
    return pl.BlockSpec(memory_space=pl.ANY)


def attn_forward(frames, wq, wk, wv, wo, gain1, bias1, gain2, bias2, scale1, cosine, sine, limit):
    shape = jax.ShapeDtypeStruct
    padded = ROW_LEN + WINDOW
    sems = pltpu.SemaphoreType.DMA
    return pl.pallas_call(
        attn_forward_kernel,
        out_shape=(
            shape((2, ROW_LEN, D), BF16),
            shape((2, padded, 256), BF16),
            shape((2, padded, 256), BF16),
            shape((2, padded, 256), BF16),
            shape((2, ROW_LEN, 256), BF16),
            shape((QUARTER, D), F32),
            shape((2, 2, QUARTER, D), BF16),
        ),
        in_specs=[hbm()] + [vmem()] * 12,
        out_specs=(hbm(),) * 7,
        scratch_shapes=[
            pltpu.VMEM((2, ROW_LEN, D), BF16),
            pltpu.VMEM((2, ROW_LEN, D), BF16),
            pltpu.VMEM((2, padded, 256), BF16),
            pltpu.VMEM((2, padded, 256), BF16),
            pltpu.VMEM((2, padded, 256), BF16),
            pltpu.VMEM((2, ROW_LEN, 256), BF16),
            pltpu.VMEM((2, 2, QUARTER, D), BF16),
            pltpu.VMEM((2, QUARTER, D), BF16),
            pltpu.VMEM((QUARTER, D), BF16),
            pltpu.VMEM((QUARTER, D), BF16),
            pltpu.VMEM((QUARTER, D), F32),
            pltpu.VMEM((QUARTER, D), BF16),
            sems((2,)),
            sems((12,)),
            sems((10,)),
            sems((10,)),
        ],
        compiler_params=pltpu.CompilerParams(
            collective_id=1, has_side_effects=True, vmem_limit_bytes=60 * MIB
        ),
        name="attn_forward",
    )(frames, wq, wk, wv, wo, gain1, bias1, gain2, bias2, scale1, cosine, sine, limit)


def column_sum(field):
    return jnp.sum(field, 0, keepdims=True)


def mlp_kernel(
    low_mlp, frames, cotangent, branch, wg, wu, wd, gain2, scale1, scale2,
    grad_branch_out, grad_mid_out, frames_out, vec_out, weight_out,
    low_buf, grad_buf, hid_buf, gg_buf, gu_buf, part_m, part_g, core_m, core_g, side_m, side_g,
    wg_buf, wu_buf, wd_buf, stage, frame_buf, cot_buf, branch_buf, gb_buf, gm_buf, of_buf,
    load_sems, store_sems, stage_sems, send_sems, recv_sems,
):
    data, core, side, core_dev, side_dev = places()
    loads = []

    def load(source, target):
        copy = pltpu.make_async_copy(source, target, load_sems.at[len(loads)])
        copy.start()
        loads.append(copy)

    def quarter(group, slot):
        row = (1 - side) if group == 0 else side
        half = (1 - core) if slot == 0 else core
        return pl.ds(pl.multiple_of(row * ROW_LEN + half * QUARTER, QUARTER), QUARTER)

    load(wg, wg_buf)
    load(wu, wu_buf)
    load(wd, wd_buf)
    for group in range(2):
        for slot in range(2):
            load(low_mlp.at[group, slot], low_buf.at[group, slot])
            load(cotangent.at[quarter(group, slot)], grad_buf.at[group, slot])
    load(frames.at[quarter(1, 1)], frame_buf)
    load(cotangent.at[quarter(1, 1)], cot_buf)
    load(branch, branch_buf)
    meet([core_dev, side_dev])
    sends = Sends(send_sems, recv_sems)
    for copy in loads[:7]:
        copy.wait()

    def chunk(group, slot, rows):
        low = low_buf[group, slot, rows]
        grad = (scale2[...] * grad_buf[group, slot, rows].astype(F32)).astype(BF16)
        grad_buf[group, slot, rows] = grad
        for tile in range(4):
            cols = slice(tile * 256, tile * 256 + 256)
            gating = product(low, wg_buf[:, cols], 1, 0)
            upward = product(low, wu_buf[:, cols], 1, 0)
            grad_hidden = product(grad, wd_buf[cols], 1, 1)
            sigma = 0.5 * jnp.tanh(0.5 * gating) + 0.5
            active = gating * sigma
            hid_buf[group, slot, rows, cols] = (active * upward).astype(BF16)
            gg_buf[group, slot, rows, cols] = (
                grad_hidden * upward * (sigma + active * (1.0 - sigma))
            ).astype(BF16)
            gu_buf[group, slot, rows, cols] = (grad_hidden * active).astype(BF16)
        for tile in range(4):
            cols = slice(tile * 256, tile * 256 + 256)
            part_g[group, slot, rows, cols] = (
                product(gg_buf[group, slot, rows], wg_buf[cols], 1, 1)
                + product(gu_buf[group, slot, rows], wu_buf[cols], 1, 1)
            ).astype(BF16)
            part_m[group, slot, rows, cols] = product(
                hid_buf[group, slot, rows], wd_buf[:, cols], 1, 0
            ).astype(BF16)

    def core_copies(group, step):
        rows = pl.ds(step * PIECE, PIECE)
        base = group * 4 + step * 2
        return [
            sends.copy(base, part_g.at[group, 0, rows], core_g.at[group, rows], core_dev),
            sends.copy(base + 1, part_m.at[group, 0, rows], core_m.at[group, rows], core_dev),
        ]

    def side_copies(step):
        rows = pl.ds(step * PIECE, PIECE)
        return [
            sends.copy(8 + step * 2, part_g.at[0, 1, rows], side_g.at[rows], side_dev),
            sends.copy(9 + step * 2, part_m.at[0, 1, rows], side_m.at[rows], side_dev),
        ]

    for group in range(2):
        if group == 1:
            for copy in loads[7:11]:
                copy.wait()
        for step in range(2):
            rows = pl.ds(step * PIECE, PIECE)

            for slot in range(2):
                chunk(group, slot, rows)
                if slot == 0:
                    for copy in core_copies(group, step):
                        copy.start()
            if group == 0:
                for part, arrived, copy, way in zip(
                    (part_g, part_m), (core_g, core_m), core_copies(group, step), side_copies(step)
                ):
                    copy.wait_recv()
                    part[0, 1, rows] = (
                        part[0, 1, rows].astype(F32) + arrived[0, rows].astype(F32)
                    ).astype(BF16)
                    way.start()

    stage_copies = []
    for number in range(6):
        which, half = number // 2, number % 2
        left, right = ((low_buf, gg_buf), (low_buf, gu_buf), (grad_buf, hid_buf))[which]
        if number >= 3:
            stage_copies[number - 3].wait()
        slot_s = number % 3

        @pl.loop(0, 2)
        def _(tile):
            cols = pl.ds(pl.multiple_of(tile * 512, 512), 512)
            total = None
            for group in range(2):
                for slot in range(2):
                    fresh = product(
                        left[group, slot, :, half * 512 : half * 512 + 512], right[group, slot, :, cols], 0, 0
                    )
                    total = fresh if total is None else total + fresh
            stage[slot_s, :, cols] = total.astype(BF16)

        copy = pltpu.make_async_copy(
            stage.at[slot_s], weight_out.at[which, pl.ds(half * 512, 512)], stage_sems.at[number]
        )
        copy.start()
        stage_copies.append(copy)

    for copy in loads[11:]:
        copy.wait()
    vec_out[...] = jnp.zeros((8, D), F32)
    stores = []

    def store(source, target):
        copy = pltpu.make_async_copy(source, target, store_sems.at[len(stores)])
        copy.start()
        stores.append(copy)

    for step in range(2):
        rows = pl.ds(step * PIECE, PIECE)
        for copy in core_copies(1, step) + side_copies(step):
            copy.wait_recv()
        grad_out = cot_buf[rows].astype(F32)
        attn_branch = branch_buf[rows]
        midway = frame_buf[rows].astype(F32) + scale1[...] * attn_branch
        mlp_branch = part_m[1, 1, rows].astype(F32) + core_m[1, rows].astype(F32) + side_m[rows].astype(F32)
        of_buf[rows] = (midway + scale2[...] * mlp_branch).astype(BF16)
        vec_out[5:6] += column_sum(grad_out * mlp_branch)
        grad_norm = part_g[1, 1, rows].astype(F32) + core_g[1, rows].astype(F32) + side_g[rows].astype(F32)
        unit, spread = norm_of(midway)
        vec_out[2:3] += column_sum(grad_norm * unit)
        vec_out[3:4] += column_sum(grad_norm)
        scaled = grad_norm * gain2[...]
        inner = scaled - jnp.mean(scaled, -1, keepdims=True) - unit * jnp.mean(scaled * unit, -1, keepdims=True)
        grad_mid = grad_out + inner * spread
        vec_out[4:5] += column_sum(grad_mid * attn_branch)
        gm_buf[rows] = grad_mid
        gb_buf[rows] = (scale1[...] * grad_mid).astype(BF16)
    store(gb_buf, grad_branch_out)
    store(of_buf, frames_out)
    store(gm_buf, grad_mid_out)
    for group in range(2):
        for step in range(2):
            for copy in core_copies(group, step):
                copy.wait_send()
    for step in range(2):
        for copy in side_copies(step):
            copy.wait_send()
    for copy in stage_copies[3:] + stores:
        copy.wait()


def mlp(low_mlp, frames, cotangent, branch, wg, wu, wd, gain2, scale1, scale2):
    shape = jax.ShapeDtypeStruct
    sems = pltpu.SemaphoreType.DMA
    whole = pltpu.VMEM((2, 2, QUARTER, D), BF16)
    row = pltpu.VMEM((2, QUARTER, D), BF16)
    single = pltpu.VMEM((QUARTER, D), BF16)
    square = pltpu.VMEM((D, D), BF16)
    wide = pltpu.VMEM((QUARTER, D), F32)
    return pl.pallas_call(
        mlp_kernel,
        out_shape=(
            shape((QUARTER, D), BF16),
            shape((QUARTER, D), F32),
            shape((QUARTER, D), BF16),
            shape((8, D), F32),
            shape((3, D, D), BF16),
        ),
        in_specs=[hbm()] * 7 + [vmem()] * 3,
        out_specs=(hbm(), hbm(), hbm(), vmem(), hbm()),
        scratch_shapes=[
            whole, whole, whole, whole, whole, whole, whole, row, row, single, single,
            square, square, square, pltpu.VMEM((3, 512, D), BF16), single, single, wide, single, wide, single,
            sems((14,)), sems((3,)), sems((6,)), sems((12,)), sems((12,)),
        ],
        compiler_params=pltpu.CompilerParams(
            collective_id=2, has_side_effects=True, vmem_limit_bytes=62 * MIB
        ),
        name="mlp_both",
    )(low_mlp, frames, cotangent, branch, wg, wu, wd, gain2, scale1, scale2)


def attn_backward_kernel(
    bits, grad_branch, grad_mid, frames_out_q, low, q, k, v, att, frames,
    wq, wk, wv, wo, gain1, cosine, sine, limit, mlp_grads, vec,
    out_frames, frames_grad, attn_grads_out, mlp_grads_out, vec_out,
    gab, low_buf, q_buf, k_buf, v_buf, att_buf, ga_buf, dq_buf, dk_buf, dv_buf, dk_sum, dv_sum,
    part, core_in, side_in, gm_buf, frame_buf, fg_buf, vec_in, own_mlp, own_attn, *rest,
):
    steps = len(bits)
    in_mlp, in_attn = rest[:steps], rest[steps : 2 * steps]
    cur_mlp, cur_attn = rest[2 * steps : 3 * steps - 1], rest[3 * steps - 1 : 4 * steps - 2]
    out_attn, out_mlp, load_sems, store_sems, send_sems, recv_sems, mlp_send, mlp_recv, attn_send, attn_recv, vec_send, vec_recv = rest[4 * steps - 2 :]
    data, core, side, core_dev, side_dev = places()
    model = 2 * side + core
    mine, data_dev = [], []
    for bit in bits:
        own_bit = (data // bit) % 2
        mine.append(own_bit)
        data_dev.append((data + bit * (1 - 2 * own_bit), model))
    loads = []

    def load(source, target):
        copy = pltpu.make_async_copy(source, target, load_sems.at[len(loads)])
        copy.start()
        loads.append(copy)
        return copy

    load(grad_branch, gab.at[1, 1])
    for source, target in ((q, q_buf), (k, k_buf), (v, v_buf), (att, att_buf)):
        load(source, target)
    early = list(loads)
    low_load = load(low, low_buf)
    late = [
        load(grad_mid, gm_buf),
        load(frames.at[pl.ds(pl.multiple_of(model * QUARTER, QUARTER), QUARTER)], frame_buf),
    ]
    own_loads = [load(mlp_grads.at[which, :, mine[0]], own_mlp.at[which]) for which in range(3)]
    meet([core_dev, side_dev] + data_dev)
    sends = Sends(send_sems, recv_sems)
    mlp_sends = Sends(mlp_send, mlp_recv)
    attn_sends = Sends(attn_send, attn_recv)
    vec_sends = Sends(vec_send, vec_recv)
    stores = []

    def store(source, target):
        copy = pltpu.make_async_copy(source, target, store_sems.at[len(stores)])
        copy.start()
        stores.append(copy)

    spans = [pl.ds(step * PIECE, PIECE) for step in range(2)]

    def place(owner_model, step):
        return pl.ds(pl.multiple_of(owner_model * QUARTER + step * PIECE, PIECE), PIECE)

    side_model = model + 2 - 4 * side

    core_first = [sends.start(step, grad_branch.at[spans[step]], gab.at[1, 0, spans[step]], core_dev) for step in range(2)]
    side_first = [sends.start(2 + step, grad_branch.at[spans[step]], gab.at[0, 1, spans[step]], side_dev) for step in range(2)]
    mlp_copies = [{} for _level in bits]
    for which in range(3):
        mlp_copies[0][which] = mlp_sends.start(
            which, mlp_grads.at[which, :, 1 - mine[0]], in_mlp[0].at[which], data_dev[0]
        )
    store(frames_out_q, out_frames.at[pl.ds(pl.multiple_of(model * QUARTER, QUARTER), QUARTER)])

    for copy in early:
        copy.wait()
    for index in range(2):
        for buf in (dk_sum, dv_sum):
            buf[index, :WINDOW] = jnp.zeros((WINDOW, 256), F32)

    def half_of(slot):
        return (1 - core) if slot == 0 else core

    def row_back(index):
        for slot in range(2):
            base = half_of(slot) * QUARTER

            @pl.loop(0, QUARTER // PIECE)
            def _(step):
                rows = pl.ds(pl.multiple_of(base + step * PIECE, PIECE), PIECE)
                here = pl.ds(pl.multiple_of(step * PIECE, PIECE), PIECE)
                ga_buf[rows] = product(gab[index, slot, here], wo[...], 1, 1).astype(BF16)

        @pl.loop(0, ROW_LEN // PIECE)
        def _(step):
            for block in range(PIECE // WINDOW):
                first = step * PIECE + block * WINDOW
                rows = pl.ds(pl.multiple_of(first, WINDOW), WINDOW)
                own_rows = pl.ds(pl.multiple_of(first + WINDOW, WINDOW), WINDOW)
                key_rows = pl.ds(pl.multiple_of(first, WINDOW), 2 * WINDOW)
                bias = window_bias(limit[index, rows])
                bias = jnp.concatenate([bias, bias], 0)
                for pair in range(2):
                    lanes = slice(pair * 128, pair * 128 + 128)
                    query = split_heads(q_buf[index, own_rows, lanes])
                    keys = k_buf[index, key_rows, lanes]
                    values = v_buf[index, key_rows, lanes]
                    grad = split_heads(ga_buf[rows, lanes])
                    scores = product(query, keys, 1, 1) * HEAD_DIM**-0.5 + bias
                    expo = jnp.exp(scores - jnp.max(scores, -1, keepdims=True))
                    probs = expo * (1.0 / jnp.sum(expo, -1, keepdims=True))
                    grad_probs = product(grad, values, 1, 1)
                    inner = jnp.sum(probs * grad_probs, -1, keepdims=True)
                    grad_logits = (probs * (grad_probs - inner) * HEAD_DIM**-0.5).astype(BF16)
                    dq_buf[index, rows, lanes] = join_heads(product(grad_logits, keys, 1, 0)).astype(BF16)
                    fresh_k = product(grad_logits, query, 0, 0)
                    fresh_v = product(probs.astype(BF16), grad, 0, 0)
                    dk_sum[index, rows, lanes] += fresh_k[:WINDOW]
                    dk_sum[index, own_rows, lanes] = fresh_k[WINDOW:]
                    dv_sum[index, rows, lanes] += fresh_v[:WINDOW]
                    dv_sum[index, own_rows, lanes] = fresh_v[WINDOW:]

        for slot in range(2):
            base = half_of(slot) * QUARTER

            @pl.loop(0, QUARTER // PIECE)
            def _(step):
                first = base + step * PIECE
                rows = pl.ds(pl.multiple_of(first, PIECE), PIECE)
                shifted = pl.ds(pl.multiple_of(first + WINDOW, WINDOW), PIECE)
                here = pl.ds(pl.multiple_of(step * PIECE, PIECE), PIECE)
                cos_rows, sin_rows = cosine[index, rows], -sine[index, rows]
                grad_q = turned_by(dq_buf[index, rows].astype(F32), cos_rows, sin_rows).astype(BF16)
                grad_k = turned_by(
                    dk_sum[index, shifted].astype(BF16).astype(F32), cos_rows, sin_rows
                ).astype(BF16)
                grad_v = dv_sum[index, shifted].astype(BF16)
                dq_buf[index, rows] = grad_q
                dk_buf[index, rows] = grad_k
                dv_buf[index, rows] = grad_v
                part[index, slot, here] = (
                    product(grad_q, wq[...], 1, 1) + product(grad_k, wk[...], 1, 1) + product(grad_v, wv[...], 1, 1)
                ).astype(BF16)

            if slot == 0:
                core_parts.append(sends.start(4 + index, part.at[index, 0], core_in.at[index], core_dev))

    core_parts = []

    def mlp_step(level, which):
        mlp_copies[level][which].wait_recv()
        if level == 0:
            own_loads[which].wait()
        count = in_mlp[level].shape[1]
        for number in range(count):
            own = own_mlp[which, number] if level == 0 else cur_mlp[level - 1][which, number, mine[level]]
            fresh = own.astype(F32) + in_mlp[level][which, number].astype(F32)
            if level == steps - 1:
                out_mlp[which] = fresh
            else:
                cur_mlp[level][which, number // 2, number % 2] = fresh.astype(BF16)
        if level < steps - 1:
            mlp_copies[level + 1][which] = mlp_sends.start(
                (level + 1) * 3 + which,
                cur_mlp[level].at[which, :, 1 - mine[level + 1]],
                in_mlp[level + 1].at[which],
                data_dev[level + 1],
            )

    attn_copies = [{} for _level in bits]

    def attn_first(which):
        attn_copies[0][which] = attn_sends.start(
            which, own_attn.at[which, :, 1 - mine[0]], in_attn[0].at[which], data_dev[0]
        )

    def attn_step(level, which):
        attn_copies[level][which].wait_recv()
        count = in_attn[level].shape[1]
        for number in range(count):
            own = own_attn[which, number, mine[0]] if level == 0 else cur_attn[level - 1][which, number, mine[level]]
            fresh = own.astype(F32) + in_attn[level][which, number].astype(F32)
            if level == steps - 1:
                out_attn[which] = fresh
            else:
                cur_attn[level][which, number // 2, number % 2] = fresh.astype(BF16)
        if level < steps - 1:
            attn_copies[level + 1][which] = attn_sends.start(
                (level + 1) * 4 + which,
                cur_attn[level].at[which, :, 1 - mine[level + 1]],
                in_attn[level + 1].at[which],
                data_dev[level + 1],
            )

    def attn_grad(which):
        count, block = own_attn.shape[1], own_attn.shape[3]

        @pl.loop(0, 2)
        def _(tile):
            cols = pl.ds(pl.multiple_of(tile * 512, 512), 512)
            total = None
            for index in range(2):
                if which < 3:
                    right = (dq_buf, dk_buf, dv_buf)[which]
                    fresh = product(low_buf[index, :, cols], right[index], 0, 0)
                    total = fresh if total is None else total + fresh
                else:
                    for slot in range(2):
                        rows = pl.ds(pl.multiple_of(half_of(slot) * QUARTER, QUARTER), QUARTER)
                        fresh = product(gab[index, slot, :, cols], att_buf[index, rows], 0, 0)
                        total = fresh if total is None else total + fresh
            spread = total.astype(BF16).reshape(count // 2, 2, block, 256)
            own_attn[which, pl.ds(tile * (count // 2), count // 2)] = spread

        attn_first(which)

    for copy in core_first:
        copy.wait_recv()
    row_back(1)
    core_again, side_frames = [], []
    for step in range(2):
        side_first[step].wait_recv()
        core_again.append(sends.start(6 + step, gab.at[0, 1, spans[step]], gab.at[0, 0, spans[step]], core_dev))
    for step in range(2):
        side_frames.append(sends.start(8 + step, frames_out_q.at[spans[step]], out_frames.at[place(model, step)], side_dev))
    core_frames = [sends.start(10 + step, frames_out_q.at[spans[step]], out_frames.at[place(model, step)], core_dev) for step in range(2)]
    for copy in core_again:
        copy.wait_recv()
    row_back(0)
    core_parts[1].wait_recv()
    side_parts = []
    for step in range(2):
        rows = slice(step * PIECE, step * PIECE + PIECE)
        part[0, 1, rows] = (part[0, 1, rows].astype(F32) + core_in[0, rows].astype(F32)).astype(BF16)
        side_parts.append(sends.start(12 + step, part.at[0, 1, spans[step]], side_in.at[spans[step]], side_dev))
    attn_grad(3)
    mlp_step(0, 0)
    low_load.wait()
    for which in range(3):
        attn_grad(which)
    for step in range(2):
        side_frames[step].wait_recv()
        core_frames.append(
            sends.start(14 + step, out_frames.at[place(side_model, step)], out_frames.at[place(side_model, step)], core_dev)
        )
    mlp_step(0, 1)
    for copy in late:
        copy.wait()
    core_parts[0].wait_recv()
    vec_out[...] = vec[...]
    side_grads, core_grads = [], []
    for step in range(2):
        rows = slice(step * PIECE, step * PIECE + PIECE)
        side_parts[step].wait_recv()
        grad_norm = part[1, 1, rows].astype(F32) + core_in[1, rows].astype(F32) + side_in[rows].astype(F32)
        unit, spread = norm_of(frame_buf[rows].astype(F32))
        vec_out[0:1] += column_sum(grad_norm * unit)
        vec_out[1:2] += column_sum(grad_norm)
        scaled = grad_norm * gain1[...]
        inner = scaled - jnp.mean(scaled, -1, keepdims=True) - unit * jnp.mean(scaled * unit, -1, keepdims=True)
        fg_buf[rows] = (gm_buf[rows] + inner * spread).astype(BF16)
        side_grads.append(sends.start(16 + step, fg_buf.at[spans[step]], frames_grad.at[place(model, step)], side_dev))
        core_grads.append(sends.start(18 + step, fg_buf.at[spans[step]], frames_grad.at[place(model, step)], core_dev))
    store(fg_buf, frames_grad.at[pl.ds(pl.multiple_of(model * QUARTER, QUARTER), QUARTER)])
    vec_devs = [core_dev, side_dev] + data_dev
    vec_copies = []

    def vec_step(level):
        if level > 0:
            vec_copies[level - 1].wait_recv()
            vec_copies[level - 1].wait_send()
            vec_out[...] += vec_in[level - 1]
        if level < len(vec_devs):
            vec_copies.append(vec_sends.start(level, vec_out, vec_in.at[level], vec_devs[level]))

    vec_step(0)
    mlp_step(0, 2)
    vec_step(1)
    for level in range(1, steps):
        for which in range(3):
            mlp_step(level, which)
        for which in range(4):
            attn_step(level - 1, which)
        if level == steps - 1:
            for which in range(3):
                store(out_mlp.at[which], mlp_grads_out.at[which])
    for level in range(2, len(vec_devs) + 1):
        vec_step(level)
    for step in range(2):
        side_grads[step].wait_recv()
        core_grads.append(
            sends.start(20 + step, frames_grad.at[place(side_model, step)], frames_grad.at[place(side_model, step)], core_dev)
        )
    for which in range(4):
        attn_step(steps - 1, which)
    store(out_attn, attn_grads_out)
    for copy in core_frames + core_grads:
        copy.wait_recv()
    for group in (sends, mlp_sends, attn_sends):
        for copy in group.made:
            copy.wait_send()
    for copy in stores:
        copy.wait()


def attn_backward(parts, grad_branch, grad_mid, frames_out_q, low, q, k, v, att, frames, wq, wk, wv, wo, gain1, cosine, sine, limit, mlp_grads, vec):
    shape = jax.ShapeDtypeStruct
    sems = pltpu.SemaphoreType.DMA
    padded = ROW_LEN + WINDOW
    block = D // parts
    bits = []
    while 2 ** len(bits) < parts:
        bits.append(2 ** len(bits))
    steps = len(bits)
    ins_mlp = [pltpu.VMEM((3, parts // 2 ** (level + 1), block, D), BF16) for level in range(steps)]
    ins_attn = [pltpu.VMEM((4, parts // 2 ** (level + 1), block, 256), BF16) for level in range(steps)]
    cur_mlp = [pltpu.VMEM((3, parts // 2 ** (level + 2), 2, block, D), BF16) for level in range(steps - 1)]
    cur_attn = [pltpu.VMEM((4, parts // 2 ** (level + 2), 2, block, 256), BF16) for level in range(steps - 1)]
    single = pltpu.VMEM((QUARTER, D), BF16)
    padded_buf = pltpu.VMEM((2, padded, 256), BF16)
    head_buf = pltpu.VMEM((2, ROW_LEN, 256), BF16)
    return pl.pallas_call(
        functools.partial(attn_backward_kernel, bits),
        out_shape=(
            shape((2 * ROW_LEN, D), BF16),
            shape((2 * ROW_LEN, D), BF16),
            shape((4, block, 256), F32),
            shape((3, block, D), F32),
            shape((8, D), F32),
        ),
        in_specs=[hbm()] * 9 + [vmem()] * 8 + [hbm(), vmem()],
        out_specs=(hbm(), hbm(), hbm(), hbm(), vmem()),
        scratch_shapes=[
            pltpu.VMEM((2, 2, QUARTER, D), BF16),
            pltpu.VMEM((2, ROW_LEN, D), BF16),
            padded_buf, padded_buf, padded_buf, head_buf,
            pltpu.VMEM((ROW_LEN, 256), BF16),
            head_buf, head_buf, head_buf,
            pltpu.VMEM((2, padded, 256), F32),
            pltpu.VMEM((2, padded, 256), F32),
            pltpu.VMEM((2, 2, QUARTER, D), BF16),
            pltpu.VMEM((2, QUARTER, D), BF16),
            single,
            pltpu.VMEM((QUARTER, D), F32),
            single, single,
            pltpu.VMEM((steps + 2, 8, D), F32),
            pltpu.VMEM((3, parts // 2, block, D), BF16),
            pltpu.VMEM((4, parts // 2, 2, block, 256), BF16),
            *ins_mlp, *ins_attn, *cur_mlp, *cur_attn,
            pltpu.VMEM((4, block, 256), F32),
            pltpu.VMEM((3, block, D), F32),
            sems((11,)), sems((6,)), sems((22,)), sems((22,)),
            sems((3 * steps,)), sems((3 * steps,)), sems((4 * steps,)), sems((4 * steps,)),
            sems((steps + 2,)), sems((steps + 2,)),
        ],
        compiler_params=pltpu.CompilerParams(
            collective_id=3, has_side_effects=True, vmem_limit_bytes=62 * MIB
        ),
        name="attn_backward",
    )(grad_branch, grad_mid, frames_out_q, low, q, k, v, att, frames, wq, wk, wv, wo, gain1, cosine, sine, limit,
      mlp_grads.reshape(3, parts // 2, 2, block, D), vec)


def per_device(
    parts, frames, clip_lengths, query_weight, key_weight, value_weight, output_weight, gate_weight, up_weight,
    down_weight, attn_gain, attn_bias, mlp_gain, mlp_bias, attn_scale, mlp_scale, cotangent,
):
    side = lax.axis_index("mp") // 2
    lengths = jnp.where(side == 0, clip_lengths[::-1], clip_lengths)
    cosine, sine, limit = position_tables(lengths)
    row = lambda vector: vector.reshape(1, D)
    low, q, k, v, att, branch, low_mlp = attn_forward(
        frames, query_weight, key_weight, value_weight, output_weight, row(attn_gain), row(attn_bias),
        row(mlp_gain), row(mlp_bias), row(attn_scale), cosine, sine, limit,
    )
    grad_branch, grad_mid, frames_q, vec, mlp_grads = mlp(
        low_mlp, frames, cotangent, branch, gate_weight, up_weight, down_weight, row(mlp_gain), row(attn_scale), row(mlp_scale)
    )
    out_frames, frames_grad, attn_part, mlp_part, vec = attn_backward(
        parts, grad_branch, grad_mid, frames_q, low, q, k, v, att, frames,
        query_weight, key_weight, value_weight, output_weight, row(attn_gain), cosine, sine, limit, mlp_grads, vec,
    )
    block = D // parts
    vec = lax.dynamic_slice_in_dim(vec, lax.axis_index("dp") * block, block, 1)
    return (
        out_frames, frames_grad, attn_part[0], attn_part[1], attn_part[2], attn_part[3].T,
        mlp_part[0], mlp_part[1], mlp_part[2].T, vec[0], vec[1], vec[2], vec[3], vec[4], vec[5],
    )


def solution(mesh):
    rows, whole = P("dp", None), P()
    in_weight, out_weight = P(None, "mp"), P("mp", None)
    in_specs = (rows, rows, in_weight, in_weight, in_weight, out_weight, in_weight, in_weight, out_weight) + (whole,) * 6 + (rows,)
    scattered, turned = P("dp", "mp"), P("mp", "dp")
    out_specs = (rows, rows, scattered, scattered, scattered, turned, scattered, scattered, turned) + (P("dp"),) * 6
    return jax.shard_map(
        functools.partial(per_device, mesh.shape["dp"]), mesh=mesh, in_specs=in_specs, out_specs=out_specs, check_vma=False
    )
```

```python
import functools

import jax
import jax.numpy as jnp
import numpy as np
from jax import lax
from jax.experimental import pallas as pl
from jax.experimental.pallas import tpu as pltpu
from jax.sharding import PartitionSpec as P

HEAD_DIM = 64
WINDOW = 128
ROW_LEN = 1024
QUARTER = 512
PIECE = 256
SMALL = 64
SLOTS = 8
CLIP_UNIT = 125
D = 1024
HEADS_WIDE = 256
F32 = jnp.float32
BF16 = jnp.bfloat16
MESH = pl.DeviceIdType.MESH
MIB = 2**20


def product(left, right, left_dim, right_dim):
    return lax.dot_general(
        left, right, (((left_dim,), (right_dim,)), ((), ())), preferred_element_type=F32
    )


def rotary_constants():
    half_dim = HEAD_DIM // 2
    inverse = 10000.0 ** (-np.arange(half_dim) / half_dim)
    inverse = np.concatenate([inverse] * 4)[None, :]
    frame_angle = np.arange(ROW_LEN)[:, None] * inverse
    start_angle = (CLIP_UNIT * np.arange(SLOTS + 1))[:, None] * inverse
    filler = np.zeros((16 - SLOTS - 1, 128))
    starts = np.stack(
        [np.concatenate([np.cos(start_angle), filler]), np.concatenate([np.sin(start_angle), filler])]
    )
    frame = np.stack([np.cos(frame_angle), np.sin(frame_angle)])
    return jnp.asarray(frame, F32), jnp.asarray(starts, F32)


class Copies:
    def __init__(self, sems):
        self.sems, self.count = sems, 0

    def start(self, source, target):
        copy = pltpu.make_async_copy(source, target, self.sems.at[self.count])
        self.count += 1
        copy.start()
        return copy


class Sends:
    def __init__(self, send_sems, recv_sems):
        self.send_sems, self.recv_sems, self.made = send_sems, recv_sems, []

    def start(self, source, target, partner):
        index = len(self.made)
        copy = pltpu.make_async_remote_copy(
            src_ref=source,
            dst_ref=target,
            send_sem=self.send_sems.at[index],
            recv_sem=self.recv_sems.at[index],
            device_id=partner,
            device_id_type=MESH,
        )
        copy.start()
        self.made.append([copy, False])
        return len(self.made) - 1

    def sent(self, *numbers):
        for number in numbers:
            if not self.made[number][1]:
                self.made[number][0].wait_send()
                self.made[number][1] = True

    def arrived(self, *numbers):
        for number in numbers:
            self.made[number][0].wait_recv()


def turned_by(field, cosine, sine):
    lane = lax.broadcasted_iota(jnp.int32, (1, 128), 1)
    lower = lane % HEAD_DIM < HEAD_DIM // 2
    halves = []
    for pair in range(field.shape[1] // 128):
        part = field[:, pair * 128 : pair * 128 + 128]
        swapped = jnp.where(lower, pltpu.roll(part, 96, 1), pltpu.roll(part, 32, 1))
        halves.append(part * cosine + swapped * sine)
    return jnp.concatenate(halves, 1)


def norm_of(source):
    centre = jnp.mean(source, -1, keepdims=True)
    centred = source - centre
    spread = lax.rsqrt(jnp.mean(centred * centred, -1, keepdims=True) + 1e-05)
    return centred * spread, spread


def norm_back(grad, unit, spread, gain):
    scaled = grad * gain
    inner = scaled - jnp.mean(scaled, -1, keepdims=True) - unit * jnp.mean(scaled * unit, -1, keepdims=True)
    return inner * spread


def column_sum(field):
    return jnp.sum(field, 0, keepdims=True)


def split_heads(pair):
    lane = lax.broadcasted_iota(jnp.int32, pair.shape, 1)
    zero = jnp.zeros_like(pair)
    return jnp.concatenate(
        [jnp.where(lane < HEAD_DIM, pair, zero), jnp.where(lane >= HEAD_DIM, pair, zero)], 0
    )


def join_heads(stacked):
    rows = stacked.shape[0] // 2
    lane = lax.broadcasted_iota(jnp.int32, (rows, 128), 1)
    return jnp.where(lane < HEAD_DIM, stacked[:rows], stacked[rows:])


def span(start, size):
    return pl.ds(pl.multiple_of(start, size), size)


def layer_kernel(
    bits,
    lengths, frames, cotangent, wq, wk, wv, wo, wg, wu, wd,
    gain1, bias1, gain2, bias2, scale1, scale2, rotary, rotary_start,
    out_frames, frames_grad, attn_grads_out, mlp_grads_out, vec_out, low_spill, head_spill, branch_spill,
    x0, x1, x2, x3, x4, x5, x6, x7, core_g, core_m, side_g, side_m, wide, dk_sum, dv_sum,
    wg_buf, wu_buf, wd_buf, vec, vec_in, *rest,
):
    steps = len(bits)
    in_mlp, in_attn = rest[:steps], rest[steps : 2 * steps]
    load_sems, store_sems, send_sems, recv_sems = rest[2 * steps :]
    data, model = lax.axis_index("dp"), lax.axis_index("mp")
    core, side = model % 2, model // 2
    side_model = model + 2 - 4 * side
    core_dev, side_dev = (data, model + 1 - 2 * core), (data, side_model)
    mine, data_dev = [], []
    for bit in bits:
        own_bit = (data // bit) % 2
        mine.append(own_bit)
        data_dev.append((data + bit * (1 - 2 * own_bit), model))
    loads, stores, sends = Copies(load_sems), Copies(store_sems), Sends(send_sems, recv_sems)
    block = D // 2**steps

    rows_of = (1 - side, side)
    halves = (1 - core, core)

    def quarter_rows(group, slot):
        return span(rows_of[group] * ROW_LEN + halves[slot] * QUARTER, QUARTER)

    def own_rows(owner, step):
        return span(owner * QUARTER + step * PIECE, PIECE)

    def at_slot(slot, step):
        return pl.ds(slot * QUARTER + step * PIECE, PIECE)

    def piece(step):
        return pl.ds(step * PIECE, PIECE)

    frame_loads = []
    for index in range(2):
        for part in range(4):
            frame_loads.append(
                loads.start(
                    frames.at[span(rows_of[index] * ROW_LEN + part * PIECE, PIECE)],
                    x0.at[index, pl.ds(part * PIECE, PIECE)],
                )
            )
    weight_loads = [loads.start(wg, wg_buf), loads.start(wu, wu_buf), loads.start(wd, wd_buf)]
    cot_loads = {}
    for group in range(2):
        for slot in range(2):
            cot_loads[group, slot] = loads.start(
                cotangent.at[quarter_rows(group, slot)], x4.at[group, pl.ds(slot * QUARTER, QUARTER)]
            )
    barrier = pltpu.get_barrier_semaphore()
    partners = [core_dev, side_dev] + data_dev
    for partner in partners:
        pl.semaphore_signal(barrier, inc=1, device_id=partner, device_id_type=MESH)
    pl.semaphore_wait(barrier, len(partners))

    def clip_facts(index, first, count):
        frame_ids = lax.broadcasted_iota(jnp.int32, (count, 128), 0) + first
        start_ids = jnp.zeros((count, 128), jnp.int32)
        end = 0
        for slot in range(SLOTS):
            length = lengths[rows_of[index], slot]
            end = end + length
            start_ids = start_ids + jnp.where(frame_ids >= end, length, 0)
        return frame_ids, start_ids

    def angles(index, first, count, direction):
        _frame_ids, start_ids = clip_facts(index, first, count)
        start_cos = jnp.broadcast_to(rotary_start[0, 0:1], (count, 128))
        start_sin = jnp.broadcast_to(rotary_start[1, 0:1], (count, 128))
        for number in range(1, SLOTS + 1):
            here = start_ids == number * CLIP_UNIT
            start_cos = jnp.where(here, rotary_start[0, number : number + 1], start_cos)
            start_sin = jnp.where(here, rotary_start[1, number : number + 1], start_sin)
        frame_cos, frame_sin = rotary[0, pl.ds(first, count)], rotary[1, pl.ds(first, count)]
        lane = lax.broadcasted_iota(jnp.int32, (count, 128), 1)
        cosine = frame_cos * start_cos + frame_sin * start_sin
        sine = frame_sin * start_cos - frame_cos * start_sin
        sign = jnp.where(lane % HEAD_DIM < HEAD_DIM // 2, -direction, direction)
        return cosine, sine * sign

    def window(index, number):
        lead = 1 - (7 - number) // 7
        first = pl.multiple_of(number * WINDOW, WINDOW)
        key_first = pl.multiple_of((number - lead) * WINDOW, WINDOW)
        frame_ids, start_ids = clip_facts(index, first, WINDOW)
        limit = jnp.minimum(frame_ids - start_ids, WINDOW - 1)
        limit = jnp.concatenate([limit, limit], 1)
        row_ids = lax.broadcasted_iota(jnp.int32, (WINDOW, 2 * WINDOW), 0)
        col_ids = lax.broadcasted_iota(jnp.int32, (WINDOW, 2 * WINDOW), 1)
        distance = row_ids - col_ids + lead * WINDOW
        bias = jnp.where((distance >= 0) & (distance <= limit), 0.0, -1e30)
        return pl.ds(first, WINDOW), pl.ds(key_first, 2 * WINDOW), jnp.concatenate([bias, bias], 0)

    def columns(kind, pair=None):
        if pair is None:
            return slice(kind * HEADS_WIDE, kind * HEADS_WIDE + HEADS_WIDE)
        return slice(kind * HEADS_WIDE + pair * 128, kind * HEADS_WIDE + pair * 128 + 128)

    core_sent, side_sent, spills = [], [], []
    for index in range(2):
        for part in range(4):
            frame_loads[index * 4 + part].wait()

        @pl.loop(0, ROW_LEN // PIECE)
        def _(step):
            rows = span(step * PIECE, PIECE)
            unit, _spread = norm_of(x0[index, rows].astype(F32))
            low = (unit * gain1[...] + bias1[...]).astype(BF16)
            x1[index, rows] = low
            cosine, sine = angles(index, pl.multiple_of(step * PIECE, PIECE), PIECE, 1.0)
            x2[index, rows, columns(0)] = turned_by(product(low, wq[...], 1, 0), cosine, sine).astype(BF16)
            x2[index, rows, columns(1)] = turned_by(product(low, wk[...], 1, 0), cosine, sine).astype(BF16)
            x2[index, rows, columns(2)] = product(low, wv[...], 1, 0).astype(BF16)

        spills.append(stores.start(x1.at[index], low_spill.at[index]))
        for slot in range(2):

            @pl.loop(0, QUARTER // PIECE)
            def _(step):
                base = halves[slot] * QUARTER + step * PIECE
                for inner in range(PIECE // WINDOW):
                    rows, key_rows, bias = window(index, halves[slot] * 4 + step * 2 + inner)
                    for pair in range(2):
                        query = split_heads(x2[index, rows, columns(0, pair)])
                        scores = product(query, x2[index, key_rows, columns(1, pair)], 1, 1)
                        scores = scores * HEAD_DIM**-0.5 + bias
                        expo = jnp.exp(scores - jnp.max(scores, -1, keepdims=True))
                        total = jnp.sum(expo, -1, keepdims=True)
                        result = product(expo.astype(BF16), x2[index, key_rows, columns(2, pair)], 1, 0)
                        x2[index, rows, columns(3, pair)] = join_heads(result * (1.0 / total)).astype(BF16)
                x5[index, span(slot * QUARTER + step * PIECE, PIECE)] = product(
                    x2[index, span(base, PIECE), columns(3)], wo[...], 1, 0
                ).astype(BF16)

            if slot == 0:
                core_sent.append(sends.start(x5.at[index, pl.ds(0, QUARTER)], core_g.at[index], core_dev))
        spills.append(stores.start(x2.at[index], head_spill.at[index]))
        sends.arrived(core_sent[index])
        if index == 0:
            for step in range(2):
                rows = at_slot(1, step)
                x5[0, rows] = (x5[0, rows].astype(F32) + core_g[0, piece(step)].astype(F32)).astype(BF16)
                side_sent.append(sends.start(x5.at[0, rows], side_g.at[piece(step)], side_dev))

    side_low, core_low = [], []
    for step in range(2):
        sends.arrived(side_sent[step])

        @pl.loop(0, PIECE // SMALL)
        def _(small):
            here = span(step * PIECE + small * SMALL, SMALL)
            there = span(QUARTER + step * PIECE + small * SMALL, SMALL)
            branch = x5[1, there].astype(F32) + core_g[1, here].astype(F32) + side_g[here].astype(F32)
            wide[here] = branch
            source = x0[1, span(core * QUARTER + step * PIECE + small * SMALL, SMALL)].astype(F32)
            unit, _spread = norm_of(source + scale1[...] * branch)
            x3[1, there] = (unit * gain2[...] + bias2[...]).astype(BF16)

        rows = at_slot(1, step)
        side_low.append(sends.start(x3.at[1, rows], x3.at[0, rows], side_dev))
        core_low.append(sends.start(x3.at[1, rows], x3.at[1, at_slot(0, step)], core_dev))

    spills.append(stores.start(wide, branch_spill))
    for copy in spills + weight_loads:
        copy.wait()
    sends.sent(*core_sent, *side_sent)
    vec[...] = jnp.zeros((8, D), F32)

    def chunk(group, slot, step):
        rows = at_slot(slot, step)
        low = x3[group, rows]
        grad = (scale2[...] * x4[group, rows].astype(F32)).astype(BF16)
        x4[group, rows] = grad
        for tile in range(4):
            cols = slice(tile * 256, tile * 256 + 256)
            gating = product(low, wg_buf[:, cols], 1, 0)
            upward = product(low, wu_buf[:, cols], 1, 0)
            grad_hidden = product(grad, wd_buf[cols], 1, 1)
            sigma = 0.5 * jnp.tanh(0.5 * gating) + 0.5
            active = gating * sigma
            x0[group, rows, cols] = (active * upward).astype(BF16)
            x1[group, rows, cols] = (grad_hidden * upward * (sigma + active * (1.0 - sigma))).astype(BF16)
            x2[group, rows, cols] = (grad_hidden * active).astype(BF16)
        for tile in range(4):
            cols = slice(tile * 256, tile * 256 + 256)
            x5[group, rows, cols] = (
                product(x1[group, rows], wg_buf[cols], 1, 1) + product(x2[group, rows], wu_buf[cols], 1, 1)
            ).astype(BF16)
            x6[group, rows, cols] = product(x0[group, rows], wd_buf[:, cols], 1, 0).astype(BF16)

    core_grad, core_part, side_grad, core_again = {}, {}, [], []
    for group, step in ((1, 0), (1, 1), (0, 0), (0, 1)):
        if group == 1:
            sends.arrived(core_low[step])
        else:
            sends.arrived(side_low[step])
            core_again.append(sends.start(x3.at[0, at_slot(1, step)], x3.at[0, at_slot(0, step)], core_dev))
            sends.arrived(core_again[step])
        for slot in range(2):
            if step == 0:
                cot_loads[group, slot].wait()
            chunk(group, slot, step)
            if slot == 0:
                rows = at_slot(0, step)
                core_grad[group, step] = sends.start(x5.at[group, rows], core_g.at[group, piece(step)], core_dev)
                core_part[group, step] = sends.start(x6.at[group, rows], core_m.at[group, piece(step)], core_dev)
        if group == 0:
            rows = at_slot(1, step)
            sends.arrived(core_grad[0, step])
            x5[0, rows] = (x5[0, rows].astype(F32) + core_g[0, piece(step)].astype(F32)).astype(BF16)
            side_grad.append(sends.start(x5.at[0, rows], side_g.at[piece(step)], side_dev))
            sends.arrived(core_part[0, step])
            x6[0, rows] = (x6[0, rows].astype(F32) + core_m[0, piece(step)].astype(F32)).astype(BF16)

    quarter_loads = [
        loads.start(frames.at[span(model * QUARTER, QUARTER)], wd_buf.at[pl.ds(0, QUARTER)]),
        loads.start(cotangent.at[span(model * QUARTER, QUARTER)], wd_buf.at[pl.ds(QUARTER, QUARTER)]),
    ]
    low_loads = [loads.start(low_spill.at[0], wg_buf), loads.start(low_spill.at[1], wu_buf)]

    def kept(which, half, start, size):
        if which == 0:
            return x6.at[half, pl.ds(start, size)]
        if which == 1:
            return x1.at[0, pl.ds(half * QUARTER + start, size)]
        if which == 2:
            return x3.at[0, pl.ds(half * QUARTER + start, size)]
        return x3.at[1, pl.ds(half * QUARTER + start, size), columns(which - 3)]

    def arriving(level, which):
        return in_mlp[level].at[which] if which < 3 else in_attn[level].at[which - 3]

    data_sent = {}

    def place_blocks(which, tile, total, cols):
        fresh = total.astype(BF16)
        for number in range(QUARTER // block):
            whole = tile * (QUARTER // block) + number
            target = kept(which, whole % 2, (whole // 2) * block, block)
            target[:, cols] = fresh[number * block : number * block + block]

    def send_half(which):
        data_sent[0, which] = sends.start(
            kept(which, 1 - mine[0], 0, QUARTER), arriving(0, which), data_dev[0]
        )

    def mlp_grad(which):
        left, right = ((x3, x1), (x3, x2), (x4, x0))[which]
        for tile in range(2):

            @pl.loop(0, 2)
            def _(part):
                cols = span(part * 512, 512)
                total = None
                for group in range(2):
                    fresh = product(left[group, :, tile * 512 : tile * 512 + 512], right[group, :, cols], 0, 0)
                    total = fresh if total is None else total + fresh
                place_blocks(which, tile, total, cols)

        send_half(which)

    def data_step(level, which):
        copy = data_sent[level, which]
        sends.arrived(copy)
        sends.sent(copy)
        size = QUARTER >> level
        source_half = mine[0] if level % 2 == 0 else 1 - mine[0]
        offset = 0 if level == 0 else mine[level] * size
        come = arriving(level, which)
        for number in range(size // block):
            own = kept(which, source_half, offset + number * block, block)[...]
            fresh = own.astype(F32) + come[number * block : number * block + block].astype(F32)
            if level == steps - 1:
                if which < 3:
                    wide[which * block : which * block + block] = fresh
                else:
                    wide[3 * block : 4 * block, columns(which - 3)] = fresh
            else:
                target = kept(
                    which, 1 - source_half, (number % 2) * (size // 2) + (number // 2) * block, block
                )
                target[...] = fresh.astype(BF16)
        if level < steps - 1:
            away = 1 - mine[level + 1]
            data_sent[level + 1, which] = sends.start(
                kept(which, 1 - source_half, away * (size // 2), size // 2),
                arriving(level + 1, which),
                data_dev[level + 1],
            )

    side_branch, core_branch, side_mlp = [], [], []

    def own_backward(step):
        sends.arrived(core_grad[1, step], side_grad[step])

        @pl.loop(0, PIECE // SMALL)
        def _(small):
            here = span(step * PIECE + small * SMALL, SMALL)
            there = span(QUARTER + step * PIECE + small * SMALL, SMALL)
            branch = wide[here]
            grad_out = wd_buf[there].astype(F32)
            midway = wd_buf[here].astype(F32) + scale1[...] * branch
            grad_norm = x5[1, there].astype(F32) + core_g[1, here].astype(F32) + side_g[here].astype(F32)
            unit, spread = norm_of(midway)
            vec[2:3] += column_sum(grad_norm * unit)
            vec[3:4] += column_sum(grad_norm)
            grad_mid = grad_out + norm_back(grad_norm, unit, spread, gain2[...])
            vec[4:5] += column_sum(grad_mid * branch)
            x7[1, there] = (scale1[...] * grad_mid).astype(BF16)
            wide[here] = grad_mid

        rows = at_slot(1, step)
        core_branch.append(sends.start(x7.at[1, rows], x7.at[1, at_slot(0, step)], core_dev))
        side_branch.append(sends.start(x7.at[1, rows], x7.at[0, rows], side_dev))

    def row_back(index):
        for slot in range(2):

            @pl.loop(0, QUARTER // PIECE)
            def _(step):
                rows = span(halves[slot] * QUARTER + step * PIECE, PIECE)
                x4[index, rows, columns(3)] = product(
                    x7[index, span(slot * QUARTER + step * PIECE, PIECE)], wo[...], 1, 1
                ).astype(BF16)

        dk_sum[...] = jnp.zeros(dk_sum.shape, F32)
        dv_sum[...] = jnp.zeros(dv_sum.shape, F32)

        @pl.loop(0, ROW_LEN // PIECE)
        def _(step):
            for inner in range(PIECE // WINDOW):
                rows, key_rows, bias = window(index, step * 2 + inner)
                for pair in range(2):
                    lanes = slice(pair * 128, pair * 128 + 128)
                    query = split_heads(x2[index, rows, columns(0, pair)])
                    keys = x2[index, key_rows, columns(1, pair)]
                    values = x2[index, key_rows, columns(2, pair)]
                    grad = split_heads(x4[index, rows, columns(3, pair)])
                    scores = product(query, keys, 1, 1) * HEAD_DIM**-0.5 + bias
                    expo = jnp.exp(scores - jnp.max(scores, -1, keepdims=True))
                    probs = expo * (1.0 / jnp.sum(expo, -1, keepdims=True))
                    grad_probs = product(grad, values, 1, 1)
                    inside = jnp.sum(probs * grad_probs, -1, keepdims=True)
                    grad_logits = (probs * (grad_probs - inside) * HEAD_DIM**-0.5).astype(BF16)
                    x4[index, rows, columns(0, pair)] = join_heads(product(grad_logits, keys, 1, 0)).astype(BF16)
                    dk_sum[key_rows, lanes] += product(grad_logits, query, 0, 0)
                    dv_sum[key_rows, lanes] += product(probs.astype(BF16), grad, 0, 0)

        for slot in range(2):

            @pl.loop(0, QUARTER // PIECE)
            def _(step):
                first = pl.multiple_of(halves[slot] * QUARTER + step * PIECE, PIECE)
                rows = pl.ds(first, PIECE)
                cosine, sine = angles(index, first, PIECE, -1.0)
                grad_q = turned_by(x4[index, rows, columns(0)].astype(F32), cosine, sine).astype(BF16)
                grad_k = turned_by(dk_sum[rows].astype(BF16).astype(F32), cosine, sine).astype(BF16)
                grad_v = dv_sum[rows].astype(BF16)
                x4[index, rows, columns(0)] = grad_q
                x4[index, rows, columns(1)] = grad_k
                x4[index, rows, columns(2)] = grad_v
                x5[index, span(slot * QUARTER + step * PIECE, PIECE)] = (
                    product(grad_q, wq[...], 1, 1) + product(grad_k, wk[...], 1, 1) + product(grad_v, wv[...], 1, 1)
                ).astype(BF16)

            if slot == 0:
                return_sent[index] = sends.start(x5.at[index, pl.ds(0, QUARTER)], core_g.at[index], core_dev)

    return_sent = {}

    def attn_grad(which):
        kind = which - 3
        for tile in range(2):
            cols = slice(tile * 512, tile * 512 + 512)
            total = None
            for index in range(2):
                if kind < 3:
                    left = (wg_buf, wu_buf)[index]
                    pairs = [(left[:, cols], x4[index, :, columns(kind)])]
                else:
                    pairs = [
                        (
                            x7[index, pl.ds(slot * QUARTER, QUARTER), cols],
                            x2[index, span(halves[slot] * QUARTER, QUARTER), columns(3)],
                        )
                        for slot in range(2)
                    ]
                for left, right in pairs:
                    fresh = product(left, right, 0, 0)
                    total = fresh if total is None else total + fresh
            place_blocks(which, tile, total, slice(None))
        send_half(which)

    sends.sent(*core_part.values())
    mlp_grad(0)
    for copy in quarter_loads:
        copy.wait()
    own_backward(0)
    mlp_grad(1)
    head_load = loads.start(head_spill, x2)
    own_backward(1)
    sends.sent(*core_low, *side_low, *core_again)
    mlp_grad(2)
    sends.arrived(*core_branch)
    head_load.wait()
    sends.sent(*core_grad.values(), *side_grad)
    row_back(1)
    data_step(0, 0)
    gathered = []
    for step in range(2):
        sends.arrived(side_branch[step])
        gathered.append(sends.start(x7.at[0, at_slot(1, step)], x7.at[0, at_slot(0, step)], core_dev))
    for step in range(2):
        rows = at_slot(1, step)
        side_mlp.append(sends.start(x6.at[0, rows], side_m.at[piece(step)], side_dev))
    sends.arrived(*gathered)
    row_back(0)
    sends.arrived(return_sent[0])
    side_return = []
    for step in range(2):
        rows = at_slot(1, step)
        x5[0, rows] = (x5[0, rows].astype(F32) + core_g[0, piece(step)].astype(F32)).astype(BF16)
        side_return.append(sends.start(x5.at[0, rows], side_g.at[piece(step)], side_dev))
    for copy in low_loads:
        copy.wait()
    branch_loads = []
    for part in range(4):
        target = (dk_sum, dv_sum)[part // 2].at[pl.ds((part % 2) * QUARTER, QUARTER)]
        branch_loads.append(loads.start(branch_spill.at[:, pl.ds(part * 256, 256)], target))
    attn_grad(6)
    data_step(0, 1)
    for which in range(3, 6):
        attn_grad(which)

    for copy in branch_loads:
        copy.wait()
    core_frames, side_frames = [], []
    for step in range(2):
        sends.arrived(core_part[1, step], side_mlp[step])
        for part in range(4):
            cols = slice(part * 256, part * 256 + 256)
            here, there = piece(step), at_slot(1, step)
            branch = (dk_sum, dv_sum)[part // 2][pl.ds((part % 2) * QUARTER + step * PIECE, PIECE)]
            mlp_branch = x6[1, there, cols].astype(F32) + core_m[1, here, cols].astype(F32) + side_m[here, cols].astype(F32)
            vec[5:6, cols] += column_sum(wd_buf[there, cols].astype(F32) * mlp_branch)
            midway = wd_buf[here, cols].astype(F32) + scale1[:, cols] * branch
            x6[1, there, cols] = (midway + scale2[:, cols] * mlp_branch).astype(BF16)
        core_frames.append(sends.start(x6.at[1, at_slot(1, step)], out_frames.at[own_rows(model, step)], core_dev))
    final_stores = [stores.start(x6.at[1, pl.ds(QUARTER, QUARTER)], out_frames.at[span(model * QUARTER, QUARTER)])]

    sends.arrived(return_sent[1])
    core_out, side_out = [], []
    for step in range(2):
        sends.arrived(side_return[step])

        @pl.loop(0, PIECE // SMALL)
        def _(small):
            here = span(step * PIECE + small * SMALL, SMALL)
            there = span(QUARTER + step * PIECE + small * SMALL, SMALL)
            grad_norm = x5[1, there].astype(F32) + core_g[1, here].astype(F32) + side_g[here].astype(F32)
            unit, spread = norm_of(wd_buf[here].astype(F32))
            vec[0:1] += column_sum(grad_norm * unit)
            vec[1:2] += column_sum(grad_norm)
            x5[1, there] = (wide[here] + norm_back(grad_norm, unit, spread, gain1[...])).astype(BF16)

        rows = at_slot(1, step)
        side_out.append(sends.start(x5.at[1, rows], frames_grad.at[own_rows(model, step)], side_dev))
        core_out.append(sends.start(x5.at[1, rows], frames_grad.at[own_rows(model, step)], core_dev))
    for step in range(2):
        side_frames.append(sends.start(x6.at[1, at_slot(1, step)], out_frames.at[own_rows(model, step)], side_dev))
    final_stores.append(stores.start(x5.at[1, pl.ds(QUARTER, QUARTER)], frames_grad.at[span(model * QUARTER, QUARTER)]))

    vec_devs, vec_sent = partners, []

    def vec_step():
        level = len(vec_sent)
        if level > 0:
            sends.arrived(vec_sent[-1])
            sends.sent(vec_sent[-1])
            vec[...] += vec_in[level - 1]
        if level < len(vec_devs):
            vec_sent.append(sends.start(vec, vec_in.at[level], vec_devs[level]))

    vec_step()
    data_step(0, 2)
    vec_step()
    for level in range(1, steps):
        for which in range(3):
            data_step(level, which)
        if level < 3:
            vec_step()
        for which in (6, 3, 4, 5):
            data_step(level - 1, which)
    while len(vec_sent) < len(vec_devs):
        vec_step()
    last = []
    for step in range(2):
        sends.arrived(side_out[step])
        last.append(sends.start(frames_grad.at[own_rows(side_model, step)], frames_grad.at[own_rows(side_model, step)], core_dev))
    for which in (6, 3, 4, 5):
        data_step(steps - 1, which)
    sends.arrived(vec_sent[-1])
    sends.sent(vec_sent[-1])
    vec_out[...] = vec[...] + vec_in[len(vec_devs) - 1]
    for which in range(3):
        final_stores.append(stores.start(wide.at[pl.ds(which * block, block)], mlp_grads_out.at[which]))
    final_stores.append(stores.start(wide.at[pl.ds(3 * block, block)], attn_grads_out))
    for step in range(2):
        sends.arrived(side_frames[step])
        last.append(sends.start(out_frames.at[own_rows(side_model, step)], out_frames.at[own_rows(side_model, step)], core_dev))
    sends.arrived(*core_frames, *core_out, *last)
    sends.sent(*range(len(sends.made)))
    for copy in final_stores:
        copy.wait()


def layer(parts, lengths, frames, cotangent, wq, wk, wv, wo, wg, wu, wd, gain1, bias1, gain2, bias2, scale1, scale2):
    shape = jax.ShapeDtypeStruct
    sems = pltpu.SemaphoreType.DMA
    block = D // parts
    bits = []
    while 2 ** len(bits) < parts:
        bits.append(2 ** len(bits))
    steps = len(bits)
    rotary, rotary_start = rotary_constants()
    whole = pltpu.VMEM((2, ROW_LEN, D), BF16)
    row = pltpu.VMEM((2, QUARTER, D), BF16)
    single = pltpu.VMEM((QUARTER, D), BF16)
    square = pltpu.VMEM((D, D), BF16)
    sums = pltpu.VMEM((ROW_LEN, HEADS_WIDE), F32)
    ins_mlp = [pltpu.VMEM((3, QUARTER >> level, D), BF16) for level in range(steps)]
    ins_attn = [pltpu.VMEM((4, QUARTER >> level, HEADS_WIDE), BF16) for level in range(steps)]
    vmem, hbm = pl.BlockSpec(memory_space=pltpu.VMEM), pl.BlockSpec(memory_space=pl.ANY)
    smem = pl.BlockSpec(memory_space=pltpu.SMEM)
    send_count = 48 + 8 * steps
    return pl.pallas_call(
        functools.partial(layer_kernel, bits),
        out_shape=(
            shape((2 * ROW_LEN, D), BF16),
            shape((2 * ROW_LEN, D), BF16),
            shape((block, 4 * HEADS_WIDE), F32),
            shape((3, block, D), F32),
            shape((8, D), F32),
            shape((2, ROW_LEN, D), BF16),
            shape((2, ROW_LEN, D), BF16),
            shape((QUARTER, D), F32),
        ),
        in_specs=[smem, hbm, hbm] + [vmem] * 4 + [hbm] * 3 + [vmem] * 8,
        out_specs=(hbm, hbm, hbm, hbm, vmem, hbm, hbm, hbm),
        scratch_shapes=[
            *[whole] * 8,
            row, row, single, single,
            pltpu.VMEM((QUARTER, D), F32),
            sums, sums, square, square, square,
            pltpu.VMEM((8, D), F32),
            pltpu.VMEM((steps + 2, 8, D), F32),
            *ins_mlp, *ins_attn,
            sems((32,)), sems((16,)), sems((send_count,)), sems((send_count,)),
        ],
        compiler_params=pltpu.CompilerParams(
            collective_id=1, has_side_effects=True, vmem_limit_bytes=64 * MIB
        ),
        name="layer",
    )(lengths, frames, cotangent, wq, wk, wv, wo, wg, wu, wd, gain1, bias1, gain2, bias2, scale1, scale2, rotary, rotary_start)


def per_device(
    parts, frames, clip_lengths, query_weight, key_weight, value_weight, output_weight, gate_weight, up_weight,
    down_weight, attn_gain, attn_bias, mlp_gain, mlp_bias, attn_scale, mlp_scale, cotangent,
):
    out_frames, frames_grad, attn_part, mlp_part, vec = layer(
        parts, clip_lengths, frames, cotangent, query_weight, key_weight, value_weight, output_weight,
        gate_weight, up_weight, down_weight,
        *[vector.reshape(1, D) for vector in (attn_gain, attn_bias, mlp_gain, mlp_bias, attn_scale, mlp_scale)],
    )[:5]
    block = D // parts
    vec = lax.dynamic_slice_in_dim(vec, lax.axis_index("dp") * block, block, 1)
    query, key, value, output = [attn_part[:, kind * HEADS_WIDE : (kind + 1) * HEADS_WIDE] for kind in range(4)]
    return (
        out_frames, frames_grad, query, key, value, output.T,
        mlp_part[0], mlp_part[1], mlp_part[2].T, vec[0], vec[1], vec[2], vec[3], vec[4], vec[5],
    )


def solution(mesh):
    rows, whole = P("dp", None), P()
    in_weight, out_weight = P(None, "mp"), P("mp", None)
    in_specs = (
        (rows, rows, in_weight, in_weight, in_weight, out_weight, in_weight, in_weight, out_weight)
        + (whole,) * 6
        + (rows,)
    )
    scattered, turned = P("dp", "mp"), P("mp", "dp")
    out_specs = (
        rows, rows, scattered, scattered, scattered, turned, scattered, scattered, turned,
    ) + (P("dp"),) * 6
    return jax.shard_map(
        functools.partial(per_device, mesh.shape["dp"]),
        mesh=mesh,
        in_specs=in_specs,
        out_specs=out_specs,
        check_vma=False,
    )
```

```python
import functools

import jax
import jax.numpy as jnp
import numpy as np
from jax import lax
from jax.experimental import pallas as pl
from jax.experimental.pallas import tpu as pltpu
from jax.sharding import PartitionSpec as P

HEAD_DIM = 64
WINDOW = 128
ROW_LEN = 1024
QUARTER = 512
PIECE = 256
SMALL = 64
SLOTS = 8
CLIP_UNIT = 125
D = 1024
HEADS_WIDE = 256
F32 = jnp.float32
BF16 = jnp.bfloat16
MESH = pl.DeviceIdType.MESH
MIB = 2**20


def product(left, right, left_dim, right_dim):
    return lax.dot_general(
        left, right, (((left_dim,), (right_dim,)), ((), ())), preferred_element_type=F32
    )


def rotary_constants():
    half_dim = HEAD_DIM // 2
    inverse = 10000.0 ** (-np.arange(half_dim) / half_dim)
    inverse = np.concatenate([inverse] * 4)[None, :]
    frame_angle = np.arange(ROW_LEN)[:, None] * inverse
    start_angle = (CLIP_UNIT * np.arange(SLOTS + 1))[:, None] * inverse
    filler = np.zeros((16 - SLOTS - 1, 128))
    starts = np.stack(
        [np.concatenate([np.cos(start_angle), filler]), np.concatenate([np.sin(start_angle), filler])]
    )
    frame = np.stack([np.cos(frame_angle), np.sin(frame_angle)])
    return jnp.asarray(frame, F32), jnp.asarray(starts, F32)


class Copies:
    def __init__(self, sems):
        self.sems, self.count = sems, 0

    def start(self, source, target):
        copy = pltpu.make_async_copy(source, target, self.sems.at[self.count])
        self.count += 1
        copy.start()
        return copy


class Sends:
    def __init__(self, send_sems, recv_sems):
        self.send_sems, self.recv_sems, self.made = send_sems, recv_sems, []

    def start(self, source, target, partner):
        index = len(self.made)
        copy = pltpu.make_async_remote_copy(
            src_ref=source,
            dst_ref=target,
            send_sem=self.send_sems.at[index],
            recv_sem=self.recv_sems.at[index],
            device_id=partner,
            device_id_type=MESH,
        )
        copy.start()
        self.made.append([copy, False])
        return len(self.made) - 1

    def sent(self, *numbers):
        for number in numbers:
            if not self.made[number][1]:
                self.made[number][0].wait_send()
                self.made[number][1] = True

    def arrived(self, *numbers):
        for number in numbers:
            self.made[number][0].wait_recv()


def turned_by(field, cosine, sine):
    lane = lax.broadcasted_iota(jnp.int32, (1, 128), 1)
    lower = lane % HEAD_DIM < HEAD_DIM // 2
    halves = []
    for pair in range(field.shape[1] // 128):
        part = field[:, pair * 128 : pair * 128 + 128]
        swapped = jnp.where(lower, pltpu.roll(part, 96, 1), pltpu.roll(part, 32, 1))
        halves.append(part * cosine + swapped * sine)
    return jnp.concatenate(halves, 1)


def norm_of(source):
    centre = jnp.mean(source, -1, keepdims=True)
    centred = source - centre
    spread = lax.rsqrt(jnp.mean(centred * centred, -1, keepdims=True) + 1e-05)
    return centred * spread, spread


def norm_back(grad, unit, spread, gain):
    scaled = grad * gain
    inner = scaled - jnp.mean(scaled, -1, keepdims=True) - unit * jnp.mean(scaled * unit, -1, keepdims=True)
    return inner * spread


def column_sum(field):
    return jnp.sum(field, 0, keepdims=True)


def split_heads(pair):
    lane = lax.broadcasted_iota(jnp.int32, pair.shape, 1)
    zero = jnp.zeros_like(pair)
    return jnp.concatenate(
        [jnp.where(lane < HEAD_DIM, pair, zero), jnp.where(lane >= HEAD_DIM, pair, zero)], 0
    )


def join_heads(stacked):
    rows = stacked.shape[0] // 2
    lane = lax.broadcasted_iota(jnp.int32, (rows, 128), 1)
    return jnp.where(lane < HEAD_DIM, stacked[:rows], stacked[rows:])


def span(start, size):
    return pl.ds(pl.multiple_of(start, size), size)


def layer_kernel(
    bits,
    lengths, frames, cotangent, wq, wk, wv, wo, wg, wu, wd,
    gain1, bias1, gain2, bias2, scale1, scale2, rotary, rotary_start,
    out_frames, frames_grad, attn_grads_out, mlp_grads_out, vec_out, low_spill, head_spill, branch_spill,
    x0, x1, x2, x3, x4, x5, x6, x7, wo_other, att_other, core_g, core_m, side_g, side_m, wide, dk_sum, dv_sum,
    wg_buf, wu_buf, wd_buf, vec, vec_in, *rest,
):
    steps = len(bits)
    in_mlp, in_attn = rest[:steps], rest[steps : 2 * steps]
    load_sems, store_sems, send_sems, recv_sems = rest[2 * steps :]
    data, model = lax.axis_index("dp"), lax.axis_index("mp")
    core, side = model % 2, model // 2
    side_model = model + 2 - 4 * side
    core_dev, side_dev = (data, model + 1 - 2 * core), (data, side_model)
    own_bit = {bit: (data // bit) % 2 for bit in bits}
    bit_dev = {bit: (data + bit * (1 - 2 * own_bit[bit]), model) for bit in bits}
    data_dev = [bit_dev[bit] for bit in bits]

    def order_of(which):
        if which in (1, 4, 6) and steps > 1:
            return [bits[1], bits[0]] + bits[2:]
        return bits

    loads, stores, sends = Copies(load_sems), Copies(store_sems), Sends(send_sems, recv_sems)
    block = D // 2**steps

    rows_of = (1 - side, side)
    halves = (1 - core, core)

    def quarter_rows(group, slot):
        return span(rows_of[group] * ROW_LEN + halves[slot] * QUARTER, QUARTER)

    def own_rows(owner, step):
        return span(owner * QUARTER + step * PIECE, PIECE)

    def at_slot(slot, step):
        return pl.ds(slot * QUARTER + step * PIECE, PIECE)

    def piece(step):
        return pl.ds(step * PIECE, PIECE)

    frame_loads = []
    for index in range(2):
        for part in range(4):
            frame_loads.append(
                loads.start(
                    frames.at[span(rows_of[index] * ROW_LEN + part * PIECE, PIECE)],
                    x0.at[index, pl.ds(part * PIECE, PIECE)],
                )
            )
    weight_loads = [loads.start(wg, wg_buf), loads.start(wu, wu_buf), loads.start(wd, wd_buf)]
    cot_loads = {}
    for group in range(2):
        for slot in range(2):
            cot_loads[group, slot] = loads.start(
                cotangent.at[quarter_rows(group, slot)], x4.at[group, pl.ds(slot * QUARTER, QUARTER)]
            )
    barrier = pltpu.get_barrier_semaphore()
    partners = [core_dev, side_dev] + data_dev
    for partner in partners:
        pl.semaphore_signal(barrier, inc=1, device_id=partner, device_id_type=MESH)
    pl.semaphore_wait(barrier, len(partners))

    def clip_facts(index, first, count):
        frame_ids = lax.broadcasted_iota(jnp.int32, (count, 128), 0) + first
        start_ids = jnp.zeros((count, 128), jnp.int32)
        end = 0
        for slot in range(SLOTS):
            length = lengths[rows_of[index], slot]
            end = end + length
            start_ids = start_ids + jnp.where(frame_ids >= end, length, 0)
        return frame_ids, start_ids

    def angles(index, first, count, direction):
        frame_ids = lax.broadcasted_iota(jnp.int32, (count, 128), 0) + first
        start_cos = jnp.broadcast_to(rotary_start[0, 0:1], (count, 128))
        start_sin = jnp.broadcast_to(rotary_start[1, 0:1], (count, 128))
        end = 0
        for slot in range(SLOTS):
            end = end + lengths[rows_of[index], slot]
            number = lax.div(end, jnp.int32(CLIP_UNIT))
            passed = frame_ids >= end
            start_cos = jnp.where(passed, rotary_start[0, pl.ds(number, 1)], start_cos)
            start_sin = jnp.where(passed, rotary_start[1, pl.ds(number, 1)], start_sin)
        frame_cos, frame_sin = rotary[0, pl.ds(first, count)], rotary[1, pl.ds(first, count)]
        lane = lax.broadcasted_iota(jnp.int32, (count, 128), 1)
        cosine = frame_cos * start_cos + frame_sin * start_sin
        sine = frame_sin * start_cos - frame_cos * start_sin
        sign = jnp.where(lane % HEAD_DIM < HEAD_DIM // 2, -direction, direction)
        return cosine, sine * sign

    def window(index, number):
        lead = 1 - (7 - number) // 7
        first = pl.multiple_of(number * WINDOW, WINDOW)
        key_first = pl.multiple_of((number - lead) * WINDOW, WINDOW)
        frame_ids, start_ids = clip_facts(index, first, WINDOW)
        limit = jnp.minimum(frame_ids - start_ids, WINDOW - 1)
        limit = jnp.concatenate([limit, limit], 1)
        row_ids = lax.broadcasted_iota(jnp.int32, (WINDOW, 2 * WINDOW), 0)
        col_ids = lax.broadcasted_iota(jnp.int32, (WINDOW, 2 * WINDOW), 1)
        distance = row_ids - col_ids + lead * WINDOW
        bias = jnp.where((distance >= 0) & (distance <= limit), 0.0, -1e30)
        return pl.ds(first, WINDOW), pl.ds(key_first, 2 * WINDOW), jnp.concatenate([bias, bias], 0)

    def columns(kind, pair=None):
        if pair is None:
            return slice(kind * HEADS_WIDE, kind * HEADS_WIDE + HEADS_WIDE)
        return slice(kind * HEADS_WIDE + pair * 128, kind * HEADS_WIDE + pair * 128 + 128)

    other_weight = sends.start(wo, wo_other, side_dev)
    att_sent, spills = [], []
    ones = jnp.ones((2 * WINDOW, 128), BF16)
    for index in range(2):
        for part in range(4):
            frame_loads[index * 4 + part].wait()

        @pl.loop(0, ROW_LEN // PIECE)
        def _(step):
            rows = span(step * PIECE, PIECE)
            unit, _spread = norm_of(x0[index, rows].astype(F32))
            low = (unit * gain1[...] + bias1[...]).astype(BF16)
            x1[index, rows] = low
            cosine, sine = angles(index, pl.multiple_of(step * PIECE, PIECE), PIECE, 1.0)
            x2[index, rows, columns(0)] = turned_by(product(low, wq[...], 1, 0), cosine, sine).astype(BF16)
            x2[index, rows, columns(1)] = turned_by(product(low, wk[...], 1, 0), cosine, sine).astype(BF16)
            x2[index, rows, columns(2)] = product(low, wv[...], 1, 0).astype(BF16)

        spills.append(stores.start(x1.at[index], low_spill.at[index]))
        for half in range(2):

            @pl.loop(0, QUARTER // PIECE)
            def _(step):
                for inner in range(PIECE // WINDOW):
                    rows, key_rows, bias = window(index, half * 4 + step * 2 + inner)
                    for pair in range(2):
                        query = split_heads(x2[index, rows, columns(0, pair)])
                        scores = product(query, x2[index, key_rows, columns(1, pair)], 1, 1)
                        scores = scores * HEAD_DIM**-0.5 + bias
                        expo = jnp.exp(scores - jnp.max(scores, -1, keepdims=True)).astype(BF16)
                        values = jnp.concatenate([x2[index, key_rows, columns(2, pair)], ones], 1)
                        result = product(expo, values, 1, 0)
                        x2[index, rows, columns(3, pair)] = (
                            join_heads(result[:, :128]) / join_heads(result[:, 128:])
                        ).astype(BF16)

            if index == 0:
                rows = pl.ds(half * QUARTER, QUARTER)
                att_sent.append(sends.start(x2.at[0, rows, columns(3)], att_other.at[rows], side_dev))
        spills.append(stores.start(x2.at[index], head_spill.at[index]))

    sends.arrived(other_weight, *att_sent)
    for slot in range(2):

        @pl.loop(0, QUARTER // PIECE)
        def _(step):
            rows = span(halves[slot] * QUARTER + step * PIECE, PIECE)
            fresh = product(x2[1, rows, columns(3)], wo[...], 1, 0) + product(att_other[rows], wo_other[...], 1, 0)
            if slot == 0:
                x5[1, span(step * PIECE, PIECE)] = fresh.astype(BF16)
            else:
                wide[span(step * PIECE, PIECE)] = fresh

        if slot == 0:
            core_sent = [
                sends.start(x5.at[1, piece(step)], core_g.at[1, piece(step)], core_dev) for step in range(2)
            ]

    side_low, core_low = [], []
    for step in range(2):
        sends.arrived(core_sent[step])

        @pl.loop(0, PIECE // SMALL)
        def _(small):
            here = span(step * PIECE + small * SMALL, SMALL)
            there = span(QUARTER + step * PIECE + small * SMALL, SMALL)
            branch = wide[here] + core_g[1, here].astype(F32)
            wide[here] = branch
            source = x0[1, span(core * QUARTER + step * PIECE + small * SMALL, SMALL)].astype(F32)
            unit, _spread = norm_of(source + scale1[...] * branch)
            x3[1, there] = (unit * gain2[...] + bias2[...]).astype(BF16)

        rows = at_slot(1, step)
        side_low.append(sends.start(x3.at[1, rows], x3.at[0, rows], side_dev))
        core_low.append(sends.start(x3.at[1, rows], x3.at[1, at_slot(0, step)], core_dev))

    spills.append(stores.start(wide, branch_spill))
    for copy in spills + weight_loads:
        copy.wait()
    sends.sent(*core_sent, *att_sent)
    vec[...] = jnp.zeros((8, D), F32)

    def chunk(group, slot, step):
        rows = at_slot(slot, step)
        low = x3[group, rows]
        grad = (scale2[...] * x4[group, rows].astype(F32)).astype(BF16)
        x4[group, rows] = grad
        for tile in range(4):
            cols = slice(tile * 256, tile * 256 + 256)
            gating = product(low, wg_buf[:, cols], 1, 0)
            upward = product(low, wu_buf[:, cols], 1, 0)
            grad_hidden = product(grad, wd_buf[cols], 1, 1)
            sigma = 0.5 * jnp.tanh(0.5 * gating) + 0.5
            active = gating * sigma
            x0[group, rows, cols] = (active * upward).astype(BF16)
            x1[group, rows, cols] = (grad_hidden * upward * (sigma + active * (1.0 - sigma))).astype(BF16)
            x2[group, rows, cols] = (grad_hidden * active).astype(BF16)
        for tile in range(4):
            cols = slice(tile * 256, tile * 256 + 256)
            x5[group, rows, cols] = (
                product(x1[group, rows], wg_buf[cols], 1, 1) + product(x2[group, rows], wu_buf[cols], 1, 1)
            ).astype(BF16)
            x6[group, rows, cols] = product(x0[group, rows], wd_buf[:, cols], 1, 0).astype(BF16)

    core_grad, core_part, side_grad, core_again, side_mlp = {}, {}, [], [], []
    for group, step in ((1, 0), (0, 0), (0, 1), (1, 1)):
        if group == 1:
            sends.arrived(core_low[step])
        else:
            sends.arrived(side_low[step])
            core_again.append(sends.start(x3.at[0, at_slot(1, step)], x3.at[0, at_slot(0, step)], core_dev))
            sends.arrived(core_again[step])
        for slot in range(2):
            if step == 0:
                cot_loads[group, slot].wait()
            chunk(group, slot, step)
            if slot == 0:
                rows = at_slot(0, step)
                core_grad[group, step] = sends.start(x5.at[group, rows], core_g.at[group, piece(step)], core_dev)
                core_part[group, step] = sends.start(x6.at[group, rows], core_m.at[group, piece(step)], core_dev)
        if group == 0:
            rows = at_slot(1, step)
            sends.arrived(core_grad[0, step])
            x5[0, rows] = (x5[0, rows].astype(F32) + core_g[0, piece(step)].astype(F32)).astype(BF16)
            side_grad.append(sends.start(x5.at[0, rows], side_g.at[piece(step)], side_dev))
            sends.arrived(core_part[0, step])
            x6[0, rows] = (x6[0, rows].astype(F32) + core_m[0, piece(step)].astype(F32)).astype(BF16)
            if step == 1:
                side_mlp.append(sends.start(x6.at[0, at_slot(1, 0)], side_m.at[piece(0)], side_dev))

    quarter_loads = [
        loads.start(frames.at[span(model * QUARTER, QUARTER)], wd_buf.at[pl.ds(0, QUARTER)]),
        loads.start(cotangent.at[span(model * QUARTER, QUARTER)], wd_buf.at[pl.ds(QUARTER, QUARTER)]),
    ]
    low_loads = [loads.start(low_spill.at[0], wg_buf), loads.start(low_spill.at[1], wu_buf)]

    def kept(which, half, start, size):
        if which == 0:
            return x6.at[half, pl.ds(start, size)]
        if which == 1:
            return x1.at[0, pl.ds(half * QUARTER + start, size)]
        if which == 2:
            return x3.at[0, pl.ds(half * QUARTER + start, size)]
        return x3.at[1, pl.ds(half * QUARTER + start, size), columns(which - 3)]

    def arriving(level, which):
        return in_mlp[level].at[which] if which < 3 else in_attn[level].at[which - 3]

    data_sent = {}

    def place_blocks(which, tile, total, cols):
        fresh = total.astype(BF16)
        for number in range(QUARTER // block):
            natural = tile * (QUARTER // block) + number
            whole = sum(((natural // bit) % 2) << place for place, bit in enumerate(order_of(which)))
            target = kept(which, whole % 2, (whole // 2) * block, block)
            target[:, cols] = fresh[number * block : number * block + block]

    def send_half(which):
        data_sent[0, which] = sends.start(
            kept(which, 1 - own_bit[order_of(which)[0]], 0, QUARTER),
            arriving(0, which),
            bit_dev[order_of(which)[0]],
        )

    def mlp_grad(which):
        left, right = ((x3, x1), (x3, x2), (x4, x0))[which]
        for tile in range(2):

            @pl.loop(0, 2)
            def _(part):
                cols = span(part * 512, 512)
                total = None
                for group in range(2):
                    fresh = product(left[group, :, tile * 512 : tile * 512 + 512], right[group, :, cols], 0, 0)
                    total = fresh if total is None else total + fresh
                place_blocks(which, tile, total, cols)

        send_half(which)

    def data_step(level, which):
        copy = data_sent[level, which]
        order = order_of(which)
        mine = [own_bit[bit] for bit in order]
        sends.arrived(copy)
        sends.sent(copy)
        size = QUARTER >> level
        source_half = mine[0] if level % 2 == 0 else 1 - mine[0]
        offset = 0 if level == 0 else mine[level] * size
        come = arriving(level, which)
        for number in range(size // block):
            own = kept(which, source_half, offset + number * block, block)[...]
            fresh = own.astype(F32) + come[number * block : number * block + block].astype(F32)
            if level == steps - 1:
                if which < 3:
                    wide[which * block : which * block + block] = fresh
                else:
                    wide[3 * block : 4 * block, columns(which - 3)] = fresh
            else:
                target = kept(
                    which, 1 - source_half, (number % 2) * (size // 2) + (number // 2) * block, block
                )
                target[...] = fresh.astype(BF16)
        if level < steps - 1:
            away = 1 - mine[level + 1]
            data_sent[level + 1, which] = sends.start(
                kept(which, 1 - source_half, away * (size // 2), size // 2),
                arriving(level + 1, which),
                bit_dev[order[level + 1]],
            )

    side_branch, core_branch = [], []

    def own_backward(step):
        sends.arrived(core_grad[1, step], side_grad[step])

        @pl.loop(0, PIECE // SMALL)
        def _(small):
            here = span(step * PIECE + small * SMALL, SMALL)
            there = span(QUARTER + step * PIECE + small * SMALL, SMALL)
            branch = wide[here]
            grad_out = wd_buf[there].astype(F32)
            midway = wd_buf[here].astype(F32) + scale1[...] * branch
            grad_norm = x5[1, there].astype(F32) + core_g[1, here].astype(F32) + side_g[here].astype(F32)
            unit, spread = norm_of(midway)
            vec[2:3] += column_sum(grad_norm * unit)
            vec[3:4] += column_sum(grad_norm)
            grad_mid = grad_out + norm_back(grad_norm, unit, spread, gain2[...])
            vec[4:5] += column_sum(grad_mid * branch)
            x7[1, there] = (scale1[...] * grad_mid).astype(BF16)
            wide[here] = grad_mid

        rows = at_slot(1, step)
        core_branch.append(sends.start(x7.at[1, rows], x7.at[1, at_slot(0, step)], core_dev))
        side_branch.append(sends.start(x7.at[1, rows], x7.at[0, rows], side_dev))

    def row_back(index):
        for slot in range(2):

            @pl.loop(0, QUARTER // PIECE)
            def _(step):
                rows = span(halves[slot] * QUARTER + step * PIECE, PIECE)
                x4[index, rows, columns(3)] = product(
                    x7[index, span(slot * QUARTER + step * PIECE, PIECE)], wo[...], 1, 1
                ).astype(BF16)

        dk_sum[...] = jnp.zeros(dk_sum.shape, F32)
        dv_sum[...] = jnp.zeros(dv_sum.shape, F32)

        @pl.loop(0, ROW_LEN // PIECE)
        def _(step):
            for inner in range(PIECE // WINDOW):
                rows, key_rows, bias = window(index, step * 2 + inner)
                for pair in range(2):
                    lanes = slice(pair * 128, pair * 128 + 128)
                    query = split_heads(x2[index, rows, columns(0, pair)])
                    keys = x2[index, key_rows, columns(1, pair)]
                    values = x2[index, key_rows, columns(2, pair)]
                    grad = split_heads(x4[index, rows, columns(3, pair)])
                    scores = product(query, keys, 1, 1) * HEAD_DIM**-0.5 + bias
                    expo = jnp.exp(scores - jnp.max(scores, -1, keepdims=True))
                    inverse = 1.0 / product(expo.astype(BF16), ones, 1, 0)
                    probs = expo * jnp.concatenate([inverse, inverse], 1)
                    grad_probs = product(grad, values, 1, 1)
                    inside = grad.astype(F32) * split_heads(x2[index, rows, columns(3, pair)]).astype(F32)
                    inside = product(inside.astype(BF16), ones[:128], 1, 0)
                    inside = jnp.concatenate([inside, inside], 1)
                    grad_logits = (probs * (grad_probs - inside) * HEAD_DIM**-0.5).astype(BF16)
                    x4[index, rows, columns(0, pair)] = join_heads(product(grad_logits, keys, 1, 0)).astype(BF16)
                    dk_sum[key_rows, lanes] += product(grad_logits, query, 0, 0)
                    dv_sum[key_rows, lanes] += product(probs.astype(BF16), grad, 0, 0)

        for slot in range(2):

            @pl.loop(0, QUARTER // PIECE)
            def _(step):
                first = pl.multiple_of(halves[slot] * QUARTER + step * PIECE, PIECE)
                rows = pl.ds(first, PIECE)
                cosine, sine = angles(index, first, PIECE, -1.0)
                grad_q = turned_by(x4[index, rows, columns(0)].astype(F32), cosine, sine).astype(BF16)
                grad_k = turned_by(dk_sum[rows].astype(BF16).astype(F32), cosine, sine).astype(BF16)
                grad_v = dv_sum[rows].astype(BF16)
                x4[index, rows, columns(0)] = grad_q
                x4[index, rows, columns(1)] = grad_k
                x4[index, rows, columns(2)] = grad_v
                x5[index, span(slot * QUARTER + step * PIECE, PIECE)] = (
                    product(grad_q, wq[...], 1, 1) + product(grad_k, wk[...], 1, 1) + product(grad_v, wv[...], 1, 1)
                ).astype(BF16)

            if slot == 0:
                return_sent[index] = sends.start(x5.at[index, pl.ds(0, QUARTER)], core_g.at[index], core_dev)

    return_sent = {}

    def attn_grad(which):
        kind = which - 3
        for tile in range(2):
            cols = slice(tile * 512, tile * 512 + 512)
            total = None
            for index in range(2):
                if kind < 3:
                    left = (wg_buf, wu_buf)[index]
                    pairs = [(left[:, cols], x4[index, :, columns(kind)])]
                else:
                    pairs = [
                        (
                            x7[index, pl.ds(slot * QUARTER, QUARTER), cols],
                            x2[index, span(halves[slot] * QUARTER, QUARTER), columns(3)],
                        )
                        for slot in range(2)
                    ]
                for left, right in pairs:
                    fresh = product(left, right, 0, 0)
                    total = fresh if total is None else total + fresh
            place_blocks(which, tile, total, slice(None))
        send_half(which)

    sends.sent(*core_part.values())
    mlp_grad(0)
    for copy in quarter_loads:
        copy.wait()
    own_backward(0)
    mlp_grad(1)
    head_load = loads.start(head_spill, x2)
    own_backward(1)
    sends.sent(*core_low, *side_low, *core_again)
    mlp_grad(2)
    side_mlp.append(sends.start(x6.at[0, at_slot(1, 1)], side_m.at[piece(1)], side_dev))
    sends.arrived(*core_branch)
    head_load.wait()
    sends.sent(*core_grad.values(), *side_grad)
    row_back(1)
    branch_loads = []
    for part in range(4):
        target = (dk_sum, dv_sum)[part // 2].at[pl.ds((part % 2) * QUARTER, QUARTER)]
        branch_loads.append(loads.start(branch_spill.at[:, pl.ds(part * 256, 256)], target))
    gathered = []
    for step in range(2):
        sends.arrived(side_branch[step])
        gathered.append(sends.start(x7.at[0, at_slot(1, step)], x7.at[0, at_slot(0, step)], core_dev))
    data_step(0, 0)
    data_step(0, 1)

    for copy in branch_loads:
        copy.wait()
    core_frames, side_frames = [], []
    for step in range(2):
        sends.arrived(core_part[1, step], side_mlp[step])
        for part in range(4):
            cols = slice(part * 256, part * 256 + 256)
            here, there = piece(step), at_slot(1, step)
            branch = (dk_sum, dv_sum)[part // 2][pl.ds((part % 2) * QUARTER + step * PIECE, PIECE)]
            mlp_branch = x6[1, there, cols].astype(F32) + core_m[1, here, cols].astype(F32) + side_m[here, cols].astype(F32)
            vec[5:6, cols] += column_sum(wd_buf[there, cols].astype(F32) * mlp_branch)
            midway = wd_buf[here, cols].astype(F32) + scale1[:, cols] * branch
            x6[1, there, cols] = (midway + scale2[:, cols] * mlp_branch).astype(BF16)
        core_frames.append(sends.start(x6.at[1, at_slot(1, step)], out_frames.at[own_rows(model, step)], core_dev))
        if step == 0:
            side_frames.append(sends.start(x6.at[1, at_slot(1, 0)], out_frames.at[own_rows(model, 0)], side_dev))
    final_stores = [stores.start(x6.at[1, pl.ds(QUARTER, QUARTER)], out_frames.at[span(model * QUARTER, QUARTER)])]

    sends.arrived(*gathered)
    row_back(0)
    sends.arrived(return_sent[0])
    side_return = []
    for step in range(2):
        rows = at_slot(1, step)
        x5[0, rows] = (x5[0, rows].astype(F32) + core_g[0, piece(step)].astype(F32)).astype(BF16)
        side_return.append(sends.start(x5.at[0, rows], side_g.at[piece(step)], side_dev))
    for copy in low_loads:
        copy.wait()
    for which in (6, 3):
        attn_grad(which)
    data_step(0, 2)
    for which in (4, 5):
        attn_grad(which)
    if steps > 1:
        for which in range(3):
            data_step(1, which)
    for which in (6, 3):
        data_step(0, which)

    sends.arrived(return_sent[1])
    core_out, side_out = [], []
    for step in range(2):
        sends.arrived(side_return[step])

        @pl.loop(0, PIECE // SMALL)
        def _(small):
            here = span(step * PIECE + small * SMALL, SMALL)
            there = span(QUARTER + step * PIECE + small * SMALL, SMALL)
            grad_norm = x5[1, there].astype(F32) + core_g[1, here].astype(F32) + side_g[here].astype(F32)
            unit, spread = norm_of(wd_buf[here].astype(F32))
            vec[0:1] += column_sum(grad_norm * unit)
            vec[1:2] += column_sum(grad_norm)
            x5[1, there] = (wide[here] + norm_back(grad_norm, unit, spread, gain1[...])).astype(BF16)

        rows = at_slot(1, step)
        side_out.append(sends.start(x5.at[1, rows], frames_grad.at[own_rows(model, step)], side_dev))
        core_out.append(sends.start(x5.at[1, rows], frames_grad.at[own_rows(model, step)], core_dev))
        if step == 0:
            side_frames.append(sends.start(x6.at[1, at_slot(1, 1)], out_frames.at[own_rows(model, 1)], side_dev))
            for which in (4, 5):
                data_step(0, which)
    final_stores.append(stores.start(x5.at[1, pl.ds(QUARTER, QUARTER)], frames_grad.at[span(model * QUARTER, QUARTER)]))

    vec_devs, vec_sent = partners, []

    def vec_step():
        level = len(vec_sent)
        if level > 0:
            sends.arrived(vec_sent[-1])
            sends.sent(vec_sent[-1])
            vec[...] += vec_in[level - 1]
        if level < len(vec_devs):
            vec_sent.append(sends.start(vec, vec_in.at[level], vec_devs[level]))

    last = []

    def second_hop(arriving_copy, target, step):
        sends.arrived(arriving_copy)
        rows = own_rows(side_model, step)
        last.append(sends.start(target.at[rows], target.at[rows], core_dev))

    vec_step()
    second_hop(side_frames[0], out_frames, 0)
    for level in range(1, steps):
        for which in (6, 3, 4, 5):
            data_step(level, which)
        if level == 1:
            vec_step()
        if level + 1 < steps:
            for which in range(3):
                data_step(level + 1, which)
            vec_step()
    while len(vec_sent) < len(vec_devs):
        vec_step()
    second_hop(side_out[0], frames_grad, 0)
    sends.arrived(vec_sent[-1])
    sends.sent(vec_sent[-1])
    vec_out[...] = vec[...] + vec_in[len(vec_devs) - 1]
    for which in range(3):
        final_stores.append(stores.start(wide.at[pl.ds(which * block, block)], mlp_grads_out.at[which]))
    final_stores.append(stores.start(wide.at[pl.ds(3 * block, block)], attn_grads_out))
    second_hop(side_frames[1], out_frames, 1)
    second_hop(side_out[1], frames_grad, 1)
    sends.arrived(*core_frames, *core_out, *last)
    sends.sent(*range(len(sends.made)))
    for copy in final_stores:
        copy.wait()


def layer(parts, lengths, frames, cotangent, wq, wk, wv, wo, wg, wu, wd, gain1, bias1, gain2, bias2, scale1, scale2):
    shape = jax.ShapeDtypeStruct
    sems = pltpu.SemaphoreType.DMA
    block = D // parts
    bits = []
    while 2 ** len(bits) < parts:
        bits.append(2 ** len(bits))
    steps = len(bits)
    rotary, rotary_start = rotary_constants()
    whole = pltpu.VMEM((2, ROW_LEN, D), BF16)
    row = pltpu.VMEM((2, QUARTER, D), BF16)
    single = pltpu.VMEM((QUARTER, D), BF16)
    square = pltpu.VMEM((D, D), BF16)
    sums = pltpu.VMEM((ROW_LEN, HEADS_WIDE), F32)
    ins_mlp = [pltpu.VMEM((3, QUARTER >> level, D), BF16) for level in range(steps)]
    ins_attn = [pltpu.VMEM((4, QUARTER >> level, HEADS_WIDE), BF16) for level in range(steps)]
    vmem, hbm = pl.BlockSpec(memory_space=pltpu.VMEM), pl.BlockSpec(memory_space=pl.ANY)
    smem = pl.BlockSpec(memory_space=pltpu.SMEM)
    send_count = 48 + 8 * steps
    return pl.pallas_call(
        functools.partial(layer_kernel, bits),
        out_shape=(
            shape((2 * ROW_LEN, D), BF16),
            shape((2 * ROW_LEN, D), BF16),
            shape((block, 4 * HEADS_WIDE), F32),
            shape((3, block, D), F32),
            shape((8, D), F32),
            shape((2, ROW_LEN, D), BF16),
            shape((2, ROW_LEN, D), BF16),
            shape((QUARTER, D), F32),
        ),
        in_specs=[smem, hbm, hbm] + [vmem] * 4 + [hbm] * 3 + [vmem] * 8,
        out_specs=(hbm, hbm, hbm, hbm, vmem, hbm, hbm, hbm),
        scratch_shapes=[
            *[whole] * 8,
            pltpu.VMEM((HEADS_WIDE, D), BF16),
            pltpu.VMEM((ROW_LEN, HEADS_WIDE), BF16),
            row, row, single, single,
            pltpu.VMEM((QUARTER, D), F32),
            sums, sums, square, square, square,
            pltpu.VMEM((8, D), F32),
            pltpu.VMEM((steps + 2, 8, D), F32),
            *ins_mlp, *ins_attn,
            sems((32,)), sems((16,)), sems((send_count,)), sems((send_count,)),
        ],
        compiler_params=pltpu.CompilerParams(
            collective_id=1, has_side_effects=True, vmem_limit_bytes=64 * MIB
        ),
        name="layer",
    )(lengths, frames, cotangent, wq, wk, wv, wo, wg, wu, wd, gain1, bias1, gain2, bias2, scale1, scale2, rotary, rotary_start)


def deliver_kernel(
    frames_in, grad_in, attn_in, mlp_in, frames_to, grad_to, q_to, k_to, v_to, o_to, gate_to, up_to, down_to,
    frames_buf, grad_buf, attn_buf, mlp_buf, o_turned, down_turned, load_sems, store_sems,
):
    loads, stores = Copies(load_sems), Copies(store_sems)
    attn_load, mlp_load = loads.start(attn_in, attn_buf), loads.start(mlp_in, mlp_buf)
    count = frames_in.shape[0] // 4
    moves, waits = [], []
    for source, buf, target in ((frames_in, frames_buf, frames_to), (grad_in, grad_buf, grad_to)):
        for part in range(4):
            rows = pl.ds(part * count, count)
            moves.append((loads.start(source.at[rows], buf.at[rows]), buf.at[rows], target.at[rows]))
    attn_load.wait()
    for kind, target in enumerate((q_to, k_to, v_to)):
        waits.append(stores.start(attn_buf.at[:, pl.ds(kind * HEADS_WIDE, HEADS_WIDE)], target))
    mlp_load.wait()
    waits.append(stores.start(mlp_buf.at[0], gate_to))
    waits.append(stores.start(mlp_buf.at[1], up_to))
    for load, source, target in moves:
        load.wait()
        waits.append(stores.start(source, target))
    o_turned[...] = attn_buf[:, 3 * HEADS_WIDE :].T
    waits.append(stores.start(o_turned, o_to))
    down_turned[...] = mlp_buf[2].T
    waits.append(stores.start(down_turned, down_to))
    for copy in waits:
        copy.wait()


def deliver(frames_in, grad_in, attn_in, mlp_in):
    shape = jax.ShapeDtypeStruct
    block = attn_in.shape[0]
    hbm = pl.BlockSpec(memory_space=pl.ANY)
    small, large = (block, HEADS_WIDE), (block, D)
    return pl.pallas_call(
        deliver_kernel,
        out_shape=(
            shape(frames_in.shape, BF16), shape(grad_in.shape, BF16),
            shape(small, F32), shape(small, F32), shape(small, F32), shape(small[::-1], F32),
            shape(large, F32), shape(large, F32), shape(large[::-1], F32),
        ),
        in_specs=[hbm] * 4,
        out_specs=(hbm,) * 9,
        scratch_shapes=[
            pltpu.VMEM(frames_in.shape, BF16), pltpu.VMEM(grad_in.shape, BF16),
            pltpu.VMEM((block, D), F32), pltpu.VMEM((3, block, D), F32),
            pltpu.VMEM(small[::-1], F32), pltpu.VMEM(large[::-1], F32),
            pltpu.SemaphoreType.DMA((10,)), pltpu.SemaphoreType.DMA((15,)),
        ],
        compiler_params=pltpu.CompilerParams(vmem_limit_bytes=62 * MIB),
        name="deliver",
    )(frames_in, grad_in, attn_in, mlp_in)


def per_device(
    parts, frames, clip_lengths, query_weight, key_weight, value_weight, output_weight, gate_weight, up_weight,
    down_weight, attn_gain, attn_bias, mlp_gain, mlp_bias, attn_scale, mlp_scale, cotangent,
):
    out_frames, frames_grad, attn_part, mlp_part, vec = layer(
        parts, clip_lengths, frames, cotangent, query_weight, key_weight, value_weight, output_weight,
        gate_weight, up_weight, down_weight,
        *[vector.reshape(1, D) for vector in (attn_gain, attn_bias, mlp_gain, mlp_bias, attn_scale, mlp_scale)],
    )[:5]
    block = D // parts
    vec = lax.dynamic_slice_in_dim(vec, lax.axis_index("dp") * block, block, 1)
    arrays = deliver(out_frames, frames_grad, attn_part, mlp_part)
    return tuple(arrays) + tuple(vec[kind] for kind in range(6))


def solution(mesh):
    rows, whole = P("dp", None), P()
    in_weight, out_weight = P(None, "mp"), P("mp", None)
    in_specs = (
        (rows, rows, in_weight, in_weight, in_weight, out_weight, in_weight, in_weight, out_weight)
        + (whole,) * 6
        + (rows,)
    )
    scattered, turned = P("dp", "mp"), P("mp", "dp")
    out_specs = (
        rows, rows, scattered, scattered, scattered, turned, scattered, scattered, turned,
    ) + (P("dp"),) * 6
    return jax.shard_map(
        functools.partial(per_device, mesh.shape["dp"]),
        mesh=mesh,
        in_specs=in_specs,
        out_specs=out_specs,
        check_vma=False,
    )
```

```python
import functools

import jax
import jax.numpy as jnp
import numpy as np
from jax import lax
from jax.experimental import pallas as pl
from jax.experimental.pallas import tpu as pltpu
from jax.sharding import PartitionSpec as P

HEAD_DIM = 64
WINDOW = 128
ROW_LEN = 1024
QUARTER = 512
PIECE = 256
SMALL = 64
SLOTS = 8
CLIP_UNIT = 125
D = 1024
HEADS_WIDE = 256
F32 = jnp.float32
BF16 = jnp.bfloat16
MESH = pl.DeviceIdType.MESH
MIB = 2**20


def product(left, right, left_dim, right_dim):
    return lax.dot_general(
        left, right, (((left_dim,), (right_dim,)), ((), ())), preferred_element_type=F32
    )


def rotary_constants():
    half_dim = HEAD_DIM // 2
    inverse = 10000.0 ** (-np.arange(half_dim) / half_dim)
    inverse = np.concatenate([inverse] * 4)[None, :]
    frame_angle = np.arange(ROW_LEN)[:, None] * inverse
    start_angle = (CLIP_UNIT * np.arange(SLOTS + 1))[:, None] * inverse
    filler = np.zeros((16 - SLOTS - 1, 128))
    starts = np.stack(
        [np.concatenate([np.cos(start_angle), filler]), np.concatenate([np.sin(start_angle), filler])]
    )
    frame = np.stack([np.cos(frame_angle), np.sin(frame_angle)])
    return jnp.asarray(frame, F32), jnp.asarray(starts, F32)


class Copies:
    def __init__(self, sems):
        self.sems, self.count = sems, 0

    def start(self, source, target):
        copy = pltpu.make_async_copy(source, target, self.sems.at[self.count])
        self.count += 1
        copy.start()
        return copy


class Sends:
    def __init__(self, send_sems, recv_sems):
        self.send_sems, self.recv_sems, self.made = send_sems, recv_sems, []

    def start(self, source, target, partner):
        index = len(self.made)
        copy = pltpu.make_async_remote_copy(
            src_ref=source,
            dst_ref=target,
            send_sem=self.send_sems.at[index],
            recv_sem=self.recv_sems.at[index],
            device_id=partner,
            device_id_type=MESH,
        )
        copy.start()
        self.made.append([copy, False])
        return len(self.made) - 1

    def sent(self, *numbers):
        for number in numbers:
            if not self.made[number][1]:
                self.made[number][0].wait_send()
                self.made[number][1] = True

    def arrived(self, *numbers):
        for number in numbers:
            self.made[number][0].wait_recv()


def turned_by(field, cosine, sine):
    lane = lax.broadcasted_iota(jnp.int32, (1, 128), 1)
    lower = lane % HEAD_DIM < HEAD_DIM // 2
    halves = []
    for pair in range(field.shape[1] // 128):
        part = field[:, pair * 128 : pair * 128 + 128]
        swapped = jnp.where(lower, pltpu.roll(part, 96, 1), pltpu.roll(part, 32, 1))
        halves.append(part * cosine + swapped * sine)
    return jnp.concatenate(halves, 1)


def norm_of(source):
    centre = jnp.mean(source, -1, keepdims=True)
    centred = source - centre
    spread = lax.rsqrt(jnp.mean(centred * centred, -1, keepdims=True) + 1e-05)
    return centred * spread, spread


def norm_back(grad, unit, spread, gain):
    scaled = grad * gain
    inner = scaled - jnp.mean(scaled, -1, keepdims=True) - unit * jnp.mean(scaled * unit, -1, keepdims=True)
    return inner * spread


def column_sum(field):
    return jnp.sum(field, 0, keepdims=True)


def split_heads(pair):
    lane = lax.broadcasted_iota(jnp.int32, pair.shape, 1)
    zero = jnp.zeros_like(pair)
    return jnp.concatenate(
        [jnp.where(lane < HEAD_DIM, pair, zero), jnp.where(lane >= HEAD_DIM, pair, zero)], 0
    )


def join_heads(stacked):
    rows = stacked.shape[0] // 2
    lane = lax.broadcasted_iota(jnp.int32, (rows, 128), 1)
    return jnp.where(lane < HEAD_DIM, stacked[:rows], stacked[rows:])


def span(start, size):
    return pl.ds(pl.multiple_of(start, size), size)


def layer_kernel(
    bits,
    lengths, frames, cotangent, wq, wk, wv, wo, wg, wu, wd,
    gain1, bias1, gain2, bias2, scale1, scale2, rotary, rotary_start,
    out_frames, frames_grad, attn_grads_out, mlp_grads_out, vec_out, low_spill, head_spill, branch_spill,
    x0, x1, x2, x3, x4, x5, x6, x7, wo_other, att_other, core_g, core_m, side_g, side_m, wide, dk_sum, dv_sum,
    wg_buf, wu_buf, wd_buf, vec, vec_in, *rest,
):
    steps = len(bits)
    in_mlp, in_attn = rest[:steps], rest[steps : 2 * steps]
    load_sems, store_sems, send_sems, recv_sems = rest[2 * steps :]
    data, model = lax.axis_index("dp"), lax.axis_index("mp")
    core, side = model % 2, model // 2
    side_model = model + 2 - 4 * side
    core_dev, side_dev = (data, model + 1 - 2 * core), (data, side_model)
    own_bit = {bit: (data // bit) % 2 for bit in bits}
    bit_dev = {bit: (data + bit * (1 - 2 * own_bit[bit]), model) for bit in bits}
    data_dev = [bit_dev[bit] for bit in bits]

    def order_of(which):
        if which in (1, 4, 6) and steps > 1:
            return [bits[1], bits[0]] + bits[2:]
        return bits

    loads, stores, sends = Copies(load_sems), Copies(store_sems), Sends(send_sems, recv_sems)
    block = D // 2**steps

    rows_of = (1 - side, side)
    halves = (1 - core, core)

    def quarter_rows(group, slot):
        return span(rows_of[group] * ROW_LEN + halves[slot] * QUARTER, QUARTER)

    def own_rows(owner, step):
        return span(owner * QUARTER + step * PIECE, PIECE)

    def at_slot(slot, step):
        return pl.ds(slot * QUARTER + step * PIECE, PIECE)

    def piece(step):
        return pl.ds(step * PIECE, PIECE)

    frame_loads = []
    for index in range(2):
        for part in range(4):
            frame_loads.append(
                loads.start(
                    frames.at[span(rows_of[index] * ROW_LEN + part * PIECE, PIECE)],
                    x0.at[index, pl.ds(part * PIECE, PIECE)],
                )
            )
    weight_loads = [loads.start(wg, wg_buf), loads.start(wu, wu_buf), loads.start(wd, wd_buf)]
    cot_loads = {}
    for group in range(2):
        for slot in range(2):
            cot_loads[group, slot] = loads.start(
                cotangent.at[quarter_rows(group, slot)], x4.at[group, pl.ds(slot * QUARTER, QUARTER)]
            )
    barrier = pltpu.get_barrier_semaphore()
    partners = [core_dev, side_dev] + data_dev
    for partner in partners:
        pl.semaphore_signal(barrier, inc=1, device_id=partner, device_id_type=MESH)
    pl.semaphore_wait(barrier, len(partners))

    def clip_facts(index, first, count):
        frame_ids = lax.broadcasted_iota(jnp.int32, (count, 128), 0) + first
        start_ids = jnp.zeros((count, 128), jnp.int32)
        end = 0
        for slot in range(SLOTS):
            length = lengths[rows_of[index], slot]
            end = end + length
            start_ids = start_ids + jnp.where(frame_ids >= end, length, 0)
        return frame_ids, start_ids

    def angles(index, first, count, direction):
        frame_ids = lax.broadcasted_iota(jnp.int32, (count, 128), 0) + first
        start_cos = jnp.broadcast_to(rotary_start[0, 0:1], (count, 128))
        start_sin = jnp.broadcast_to(rotary_start[1, 0:1], (count, 128))
        end = 0
        for slot in range(SLOTS):
            end = end + lengths[rows_of[index], slot]
            number = lax.div(end, jnp.int32(CLIP_UNIT))
            passed = frame_ids >= end
            start_cos = jnp.where(passed, rotary_start[0, pl.ds(number, 1)], start_cos)
            start_sin = jnp.where(passed, rotary_start[1, pl.ds(number, 1)], start_sin)
        frame_cos, frame_sin = rotary[0, pl.ds(first, count)], rotary[1, pl.ds(first, count)]
        lane = lax.broadcasted_iota(jnp.int32, (count, 128), 1)
        cosine = frame_cos * start_cos + frame_sin * start_sin
        sine = frame_sin * start_cos - frame_cos * start_sin
        sign = jnp.where(lane % HEAD_DIM < HEAD_DIM // 2, -direction, direction)
        return cosine, sine * sign

    def window(index, number):
        lead = 1 - (7 - number) // 7
        first = pl.multiple_of(number * WINDOW, WINDOW)
        key_first = pl.multiple_of((number - lead) * WINDOW, WINDOW)
        frame_ids, start_ids = clip_facts(index, first, WINDOW)
        limit = jnp.minimum(frame_ids - start_ids, WINDOW - 1)
        limit = jnp.concatenate([limit, limit], 1)
        row_ids = lax.broadcasted_iota(jnp.int32, (WINDOW, 2 * WINDOW), 0)
        col_ids = lax.broadcasted_iota(jnp.int32, (WINDOW, 2 * WINDOW), 1)
        distance = row_ids - col_ids + lead * WINDOW
        bias = jnp.where((distance >= 0) & (distance <= limit), 0.0, -1e30)
        return pl.ds(first, WINDOW), pl.ds(key_first, 2 * WINDOW), jnp.concatenate([bias, bias], 0)

    def columns(kind, pair=None):
        if pair is None:
            return slice(kind * HEADS_WIDE, kind * HEADS_WIDE + HEADS_WIDE)
        return slice(kind * HEADS_WIDE + pair * 128, kind * HEADS_WIDE + pair * 128 + 128)

    other_weight = sends.start(wo, wo_other, side_dev)
    att_sent, spills = [], []
    ones = jnp.ones((2 * WINDOW, 128), BF16)
    for index in range(2):
        for part in range(4):
            frame_loads[index * 4 + part].wait()

        @pl.loop(0, ROW_LEN // PIECE)
        def _(step):
            rows = span(step * PIECE, PIECE)
            unit, _spread = norm_of(x0[index, rows].astype(F32))
            low = (unit * gain1[...] + bias1[...]).astype(BF16)
            x1[index, rows] = low
            cosine, sine = angles(index, pl.multiple_of(step * PIECE, PIECE), PIECE, 1.0)
            x2[index, rows, columns(0)] = turned_by(product(low, wq[...], 1, 0), cosine, sine).astype(BF16)
            x2[index, rows, columns(1)] = turned_by(product(low, wk[...], 1, 0), cosine, sine).astype(BF16)
            x2[index, rows, columns(2)] = product(low, wv[...], 1, 0).astype(BF16)

        spills.append(stores.start(x1.at[index], low_spill.at[index]))
        for half in range(2):

            @pl.loop(0, QUARTER // PIECE)
            def _(step):
                for inner in range(PIECE // WINDOW):
                    rows, key_rows, bias = window(index, half * 4 + step * 2 + inner)
                    for pair in range(2):
                        query = split_heads(x2[index, rows, columns(0, pair)])
                        scores = product(query, x2[index, key_rows, columns(1, pair)], 1, 1)
                        scores = scores * HEAD_DIM**-0.5 + bias
                        expo = jnp.exp(scores - jnp.max(scores, -1, keepdims=True)).astype(BF16)
                        values = jnp.concatenate([x2[index, key_rows, columns(2, pair)], ones], 1)
                        result = product(expo, values, 1, 0)
                        x2[index, rows, columns(3, pair)] = (
                            join_heads(result[:, :128]) / join_heads(result[:, 128:])
                        ).astype(BF16)

            if index == 0:
                rows = pl.ds(half * QUARTER, QUARTER)
                att_sent.append(sends.start(x2.at[0, rows, columns(3)], att_other.at[rows], side_dev))
        spills.append(stores.start(x2.at[index], head_spill.at[index]))

    sends.arrived(other_weight, *att_sent)
    for slot in range(2):

        @pl.loop(0, QUARTER // PIECE)
        def _(step):
            rows = span(halves[slot] * QUARTER + step * PIECE, PIECE)
            fresh = product(x2[1, rows, columns(3)], wo[...], 1, 0) + product(att_other[rows], wo_other[...], 1, 0)
            if slot == 0:
                x5[1, span(step * PIECE, PIECE)] = fresh.astype(BF16)
            else:
                wide[span(step * PIECE, PIECE)] = fresh

        if slot == 0:
            core_sent = [
                sends.start(x5.at[1, piece(step)], core_g.at[1, piece(step)], core_dev) for step in range(2)
            ]

    side_low, core_low = [], []
    for step in range(2):
        sends.arrived(core_sent[step])

        @pl.loop(0, PIECE // SMALL)
        def _(small):
            here = span(step * PIECE + small * SMALL, SMALL)
            there = span(QUARTER + step * PIECE + small * SMALL, SMALL)
            branch = wide[here] + core_g[1, here].astype(F32)
            wide[here] = branch
            source = x0[1, span(core * QUARTER + step * PIECE + small * SMALL, SMALL)].astype(F32)
            unit, _spread = norm_of(source + scale1[...] * branch)
            x3[1, there] = (unit * gain2[...] + bias2[...]).astype(BF16)

        rows = at_slot(1, step)
        side_low.append(sends.start(x3.at[1, rows], x3.at[0, rows], side_dev))
        core_low.append(sends.start(x3.at[1, rows], x3.at[1, at_slot(0, step)], core_dev))

    spills.append(stores.start(wide, branch_spill))
    for copy in spills + weight_loads:
        copy.wait()
    sends.sent(*core_sent, *att_sent)
    vec[...] = jnp.zeros((8, D), F32)

    def chunk(group, slot, step):
        rows = at_slot(slot, step)
        low = x3[group, rows]
        grad = (scale2[...] * x4[group, rows].astype(F32)).astype(BF16)
        x4[group, rows] = grad
        for tile in range(4):
            cols = slice(tile * 256, tile * 256 + 256)
            gating = product(low, wg_buf[:, cols], 1, 0)
            upward = product(low, wu_buf[:, cols], 1, 0)
            grad_hidden = product(grad, wd_buf[cols], 1, 1)
            sigma = 0.5 * jnp.tanh(0.5 * gating) + 0.5
            active = gating * sigma
            x0[group, rows, cols] = (active * upward).astype(BF16)
            x1[group, rows, cols] = (grad_hidden * upward * (sigma + active * (1.0 - sigma))).astype(BF16)
            x2[group, rows, cols] = (grad_hidden * active).astype(BF16)
        for tile in range(4):
            cols = slice(tile * 256, tile * 256 + 256)
            x5[group, rows, cols] = (
                product(x1[group, rows], wg_buf[cols], 1, 1) + product(x2[group, rows], wu_buf[cols], 1, 1)
            ).astype(BF16)
            x6[group, rows, cols] = product(x0[group, rows], wd_buf[:, cols], 1, 0).astype(BF16)

    core_grad, core_part, side_grad, core_again, side_mlp = {}, {}, [], [], []
    for group, step in ((1, 0), (0, 0), (0, 1), (1, 1)):
        if group == 1:
            sends.arrived(core_low[step])
        else:
            sends.arrived(side_low[step])
            core_again.append(sends.start(x3.at[0, at_slot(1, step)], x3.at[0, at_slot(0, step)], core_dev))
            sends.arrived(core_again[step])
        for slot in range(2):
            if step == 0:
                cot_loads[group, slot].wait()
            chunk(group, slot, step)
            if slot == 0:
                rows = at_slot(0, step)
                core_grad[group, step] = sends.start(x5.at[group, rows], core_g.at[group, piece(step)], core_dev)
                core_part[group, step] = sends.start(x6.at[group, rows], core_m.at[group, piece(step)], core_dev)
        if group == 0:
            rows = at_slot(1, step)
            sends.arrived(core_grad[0, step])
            x5[0, rows] = (x5[0, rows].astype(F32) + core_g[0, piece(step)].astype(F32)).astype(BF16)
            side_grad.append(sends.start(x5.at[0, rows], side_g.at[piece(step)], side_dev))
            sends.arrived(core_part[0, step])
            x6[0, rows] = (x6[0, rows].astype(F32) + core_m[0, piece(step)].astype(F32)).astype(BF16)
            if step == 1:
                side_mlp.append(sends.start(x6.at[0, at_slot(1, 0)], side_m.at[piece(0)], side_dev))

    quarter_loads = [
        loads.start(frames.at[span(model * QUARTER, QUARTER)], wd_buf.at[pl.ds(0, QUARTER)]),
        loads.start(cotangent.at[span(model * QUARTER, QUARTER)], wd_buf.at[pl.ds(QUARTER, QUARTER)]),
    ]
    low_loads = [loads.start(low_spill.at[0], wg_buf), loads.start(low_spill.at[1], wu_buf)]

    def kept(which, half, start, size):
        if which == 0:
            return x6.at[half, pl.ds(start, size)]
        if which == 1:
            return x1.at[0, pl.ds(half * QUARTER + start, size)]
        if which == 2:
            return x3.at[0, pl.ds(half * QUARTER + start, size)]
        return x3.at[1, pl.ds(half * QUARTER + start, size), columns(which - 3)]

    def arriving(level, which):
        return in_mlp[level].at[which] if which < 3 else in_attn[level].at[which - 3]

    data_sent = {}

    def place_blocks(which, tile, total, cols):
        fresh = total.astype(BF16)
        for number in range(QUARTER // block):
            natural = tile * (QUARTER // block) + number
            whole = sum(((natural // bit) % 2) << place for place, bit in enumerate(order_of(which)))
            target = kept(which, whole % 2, (whole // 2) * block, block)
            target[:, cols] = fresh[number * block : number * block + block]

    def send_half(which):
        data_sent[0, which] = sends.start(
            kept(which, 1 - own_bit[order_of(which)[0]], 0, QUARTER),
            arriving(0, which),
            bit_dev[order_of(which)[0]],
        )

    def mlp_grad(which):
        left, right = ((x3, x1), (x3, x2), (x4, x0))[which]
        for tile in range(2):

            @pl.loop(0, 2)
            def _(part):
                cols = span(part * 512, 512)
                total = None
                for group in range(2):
                    fresh = product(left[group, :, tile * 512 : tile * 512 + 512], right[group, :, cols], 0, 0)
                    total = fresh if total is None else total + fresh
                place_blocks(which, tile, total, cols)

        send_half(which)

    def data_step(level, which):
        copy = data_sent[level, which]
        order = order_of(which)
        mine = [own_bit[bit] for bit in order]
        sends.arrived(copy)
        sends.sent(copy)
        size = QUARTER >> level
        source_half = mine[0] if level % 2 == 0 else 1 - mine[0]
        offset = 0 if level == 0 else mine[level] * size
        come = arriving(level, which)
        for number in range(size // block):
            own = kept(which, source_half, offset + number * block, block)[...]
            fresh = own.astype(F32) + come[number * block : number * block + block].astype(F32)
            if level == steps - 1:
                if which < 3:
                    wide[which * block : which * block + block] = fresh
                else:
                    wide[3 * block : 4 * block, columns(which - 3)] = fresh
            else:
                target = kept(
                    which, 1 - source_half, (number % 2) * (size // 2) + (number // 2) * block, block
                )
                target[...] = fresh.astype(BF16)
        if level < steps - 1:
            away = 1 - mine[level + 1]
            data_sent[level + 1, which] = sends.start(
                kept(which, 1 - source_half, away * (size // 2), size // 2),
                arriving(level + 1, which),
                bit_dev[order[level + 1]],
            )

    side_branch, core_branch = [], []

    def own_backward(step):
        sends.arrived(core_grad[1, step], side_grad[step])

        @pl.loop(0, PIECE // SMALL)
        def _(small):
            here = span(step * PIECE + small * SMALL, SMALL)
            there = span(QUARTER + step * PIECE + small * SMALL, SMALL)
            branch = wide[here]
            grad_out = wd_buf[there].astype(F32)
            midway = wd_buf[here].astype(F32) + scale1[...] * branch
            grad_norm = x5[1, there].astype(F32) + core_g[1, here].astype(F32) + side_g[here].astype(F32)
            unit, spread = norm_of(midway)
            vec[2:3] += column_sum(grad_norm * unit)
            vec[3:4] += column_sum(grad_norm)
            grad_mid = grad_out + norm_back(grad_norm, unit, spread, gain2[...])
            vec[4:5] += column_sum(grad_mid * branch)
            x7[1, there] = (scale1[...] * grad_mid).astype(BF16)
            wide[here] = grad_mid

        rows = at_slot(1, step)
        core_branch.append(sends.start(x7.at[1, rows], x7.at[1, at_slot(0, step)], core_dev))
        side_branch.append(sends.start(x7.at[1, rows], x7.at[0, rows], side_dev))

    def row_back(index, between):
        for slot in range(2):

            @pl.loop(0, QUARTER // PIECE)
            def _(step):
                rows = span(halves[slot] * QUARTER + step * PIECE, PIECE)
                x4[index, rows, columns(3)] = product(
                    x7[index, span(slot * QUARTER + step * PIECE, PIECE)], wo[...], 1, 1
                ).astype(BF16)

        dk_sum[...] = jnp.zeros(dk_sum.shape, F32)
        dv_sum[...] = jnp.zeros(dv_sum.shape, F32)

        @pl.loop(0, ROW_LEN // PIECE)
        def _(step):
            for inner in range(PIECE // WINDOW):
                rows, key_rows, bias = window(index, step * 2 + inner)
                for pair in range(2):
                    lanes = slice(pair * 128, pair * 128 + 128)
                    query = split_heads(x2[index, rows, columns(0, pair)])
                    keys = x2[index, key_rows, columns(1, pair)]
                    values = x2[index, key_rows, columns(2, pair)]
                    grad = split_heads(x4[index, rows, columns(3, pair)])
                    scores = product(query, keys, 1, 1) * HEAD_DIM**-0.5 + bias
                    expo = jnp.exp(scores - jnp.max(scores, -1, keepdims=True))
                    inverse = 1.0 / product(expo.astype(BF16), ones, 1, 0)
                    probs = expo * jnp.concatenate([inverse, inverse], 1)
                    grad_probs = product(grad, values, 1, 1)
                    inside = grad.astype(F32) * split_heads(x2[index, rows, columns(3, pair)]).astype(F32)
                    inside = product(inside.astype(BF16), ones[:128], 1, 0)
                    inside = jnp.concatenate([inside, inside], 1)
                    grad_logits = (probs * (grad_probs - inside) * HEAD_DIM**-0.5).astype(BF16)
                    x4[index, rows, columns(0, pair)] = join_heads(product(grad_logits, keys, 1, 0)).astype(BF16)
                    dk_sum[key_rows, lanes] += product(grad_logits, query, 0, 0)
                    dv_sum[key_rows, lanes] += product(probs.astype(BF16), grad, 0, 0)

        between()

        for slot in range(2):

            @pl.loop(0, QUARTER // PIECE)
            def _(step):
                first = pl.multiple_of(halves[slot] * QUARTER + step * PIECE, PIECE)
                rows = pl.ds(first, PIECE)
                cosine, sine = angles(index, first, PIECE, -1.0)
                grad_q = turned_by(x4[index, rows, columns(0)].astype(F32), cosine, sine).astype(BF16)
                grad_k = turned_by(dk_sum[rows].astype(BF16).astype(F32), cosine, sine).astype(BF16)
                grad_v = dv_sum[rows].astype(BF16)
                x4[index, rows, columns(0)] = grad_q
                x4[index, rows, columns(1)] = grad_k
                x4[index, rows, columns(2)] = grad_v
                x5[index, span(slot * QUARTER + step * PIECE, PIECE)] = (
                    product(grad_q, wq[...], 1, 1) + product(grad_k, wk[...], 1, 1) + product(grad_v, wv[...], 1, 1)
                ).astype(BF16)

            if slot == 0:
                return_sent[index] = sends.start(x5.at[index, pl.ds(0, QUARTER)], core_g.at[index], core_dev)

    return_sent = {}

    def attn_grad(which):
        kind = which - 3
        for tile in range(2):
            cols = slice(tile * 512, tile * 512 + 512)
            total = None
            for index in range(2):
                if kind < 3:
                    left = (wg_buf, wu_buf)[index]
                    pairs = [(left[:, cols], x4[index, :, columns(kind)])]
                else:
                    pairs = [
                        (
                            x7[index, pl.ds(slot * QUARTER, QUARTER), cols],
                            x2[index, span(halves[slot] * QUARTER, QUARTER), columns(3)],
                        )
                        for slot in range(2)
                    ]
                for left, right in pairs:
                    fresh = product(left, right, 0, 0)
                    total = fresh if total is None else total + fresh
            place_blocks(which, tile, total, slice(None))
        send_half(which)

    sends.sent(*core_part.values())
    mlp_grad(0)
    for copy in quarter_loads:
        copy.wait()
    own_backward(0)
    mlp_grad(1)
    head_load = loads.start(head_spill, x2)
    own_backward(1)
    sends.sent(*core_low, *side_low, *core_again)
    mlp_grad(2)
    side_mlp.append(sends.start(x6.at[0, at_slot(1, 1)], side_m.at[piece(1)], side_dev))
    sends.arrived(*core_branch)
    head_load.wait()
    sends.sent(*core_grad.values(), *side_grad)
    row_back(1, lambda: None)
    core_frames, side_frames = [], []

    def branch_back(step):
        return [
            loads.start(branch_spill.at[piece(step), pl.ds(part * 256, 256)], dk_sum.at[pl.ds(part * PIECE, PIECE)])
            for part in range(4)
        ]

    def own_frames(step, branch_loads):
        sends.arrived(core_part[1, step], side_mlp[step])
        for part in range(4):
            branch_loads[part].wait()
            cols = slice(part * 256, part * 256 + 256)
            here, there = piece(step), at_slot(1, step)
            mlp_branch = x6[1, there, cols].astype(F32) + core_m[1, here, cols].astype(F32) + side_m[here, cols].astype(F32)
            vec[5:6, cols] += column_sum(wd_buf[there, cols].astype(F32) * mlp_branch)
            midway = wd_buf[here, cols].astype(F32) + scale1[:, cols] * dk_sum[pl.ds(part * PIECE, PIECE)]
            x6[1, there, cols] = (midway + scale2[:, cols] * mlp_branch).astype(BF16)
        core_frames.append(sends.start(x6.at[1, at_slot(1, step)], out_frames.at[own_rows(model, step)], core_dev))

    def side_frame(step):
        side_frames.append(sends.start(x6.at[1, at_slot(1, step)], out_frames.at[own_rows(model, step)], side_dev))

    branch_loads = branch_back(0)
    gathered = []
    for step in range(2):
        sends.arrived(side_branch[step])
        gathered.append(sends.start(x7.at[0, at_slot(1, step)], x7.at[0, at_slot(0, step)], core_dev))
    data_step(0, 0)
    own_frames(0, branch_loads)
    side_frame(0)
    data_step(0, 1)
    sends.arrived(*gathered)

    def second_level(*chosen):
        if steps > 1:
            for which in chosen:
                data_step(1, which)

    row_back(0, lambda: second_level(0))
    sends.arrived(return_sent[0])
    side_return = []
    for step in range(2):
        rows = at_slot(1, step)
        x5[0, rows] = (x5[0, rows].astype(F32) + core_g[0, piece(step)].astype(F32)).astype(BF16)
        side_return.append(sends.start(x5.at[0, rows], side_g.at[piece(step)], side_dev))
    branch_loads = branch_back(1)
    for copy in low_loads:
        copy.wait()
    for which in (6, 3):
        attn_grad(which)
    data_step(0, 2)
    second_level(1)
    for which in (4, 5):
        attn_grad(which)
    own_frames(1, branch_loads)
    final_stores = [stores.start(x6.at[1, pl.ds(QUARTER, QUARTER)], out_frames.at[span(model * QUARTER, QUARTER)])]

    sends.arrived(return_sent[1])
    core_out, side_out = [], []
    for step in range(2):
        sends.arrived(side_return[step])

        @pl.loop(0, PIECE // SMALL)
        def _(small):
            here = span(step * PIECE + small * SMALL, SMALL)
            there = span(QUARTER + step * PIECE + small * SMALL, SMALL)
            grad_norm = x5[1, there].astype(F32) + core_g[1, here].astype(F32) + side_g[here].astype(F32)
            unit, spread = norm_of(wd_buf[here].astype(F32))
            vec[0:1] += column_sum(grad_norm * unit)
            vec[1:2] += column_sum(grad_norm)
            x5[1, there] = (wide[here] + norm_back(grad_norm, unit, spread, gain1[...])).astype(BF16)

        rows = at_slot(1, step)
        side_out.append(sends.start(x5.at[1, rows], frames_grad.at[own_rows(model, step)], side_dev))
        core_out.append(sends.start(x5.at[1, rows], frames_grad.at[own_rows(model, step)], core_dev))
        if step == 0:
            side_frame(1)
            second_level(2)
    final_stores.append(stores.start(x5.at[1, pl.ds(QUARTER, QUARTER)], frames_grad.at[span(model * QUARTER, QUARTER)]))

    vec_devs, vec_sent = partners, []

    def vec_step():
        level = len(vec_sent)
        if level == len(vec_devs):
            return
        if level > 0:
            sends.arrived(vec_sent[-1])
            sends.sent(vec_sent[-1])
            vec[...] += vec_in[level - 1]
        if level < len(vec_devs):
            vec_sent.append(sends.start(vec, vec_in.at[level], vec_devs[level]))

    last = []

    def second_hop(arriving_copy, target, step):
        sends.arrived(arriving_copy)
        rows = own_rows(side_model, step)
        last.append(sends.start(target.at[rows], target.at[rows], core_dev))

    vec_step()
    second_hop(side_frames[0], out_frames, 0)
    for which in (6, 3):
        data_step(0, which)
    vec_step()
    for which in (4, 5):
        data_step(0, which)
    vec_step()
    for level in range(2, steps):
        for which in (0, 1, 2):
            data_step(level, which)
        if level == 2:
            second_level(6, 3)
            vec_step()
            second_level(4, 5)
            vec_step()
            second_hop(side_out[0], frames_grad, 0)
        for which in (6, 3, 4, 5):
            data_step(level, which)
    while len(vec_sent) < len(vec_devs):
        vec_step()
    sends.arrived(vec_sent[-1])
    sends.sent(vec_sent[-1])
    vec_out[...] = vec[...] + vec_in[len(vec_devs) - 1]
    for which in range(3):
        final_stores.append(stores.start(wide.at[pl.ds(which * block, block)], mlp_grads_out.at[which]))
    final_stores.append(stores.start(wide.at[pl.ds(3 * block, block)], attn_grads_out))
    second_hop(side_frames[1], out_frames, 1)
    second_hop(side_out[1], frames_grad, 1)
    sends.arrived(*core_frames, *core_out, *last)
    sends.sent(*range(len(sends.made)))
    for copy in final_stores:
        copy.wait()


def layer(parts, lengths, frames, cotangent, wq, wk, wv, wo, wg, wu, wd, gain1, bias1, gain2, bias2, scale1, scale2):
    shape = jax.ShapeDtypeStruct
    sems = pltpu.SemaphoreType.DMA
    block = D // parts
    bits = []
    while 2 ** len(bits) < parts:
        bits.append(2 ** len(bits))
    steps = len(bits)
    rotary, rotary_start = rotary_constants()
    whole = pltpu.VMEM((2, ROW_LEN, D), BF16)
    row = pltpu.VMEM((2, QUARTER, D), BF16)
    single = pltpu.VMEM((QUARTER, D), BF16)
    square = pltpu.VMEM((D, D), BF16)
    sums = pltpu.VMEM((ROW_LEN, HEADS_WIDE), F32)
    ins_mlp = [pltpu.VMEM((3, QUARTER >> level, D), BF16) for level in range(steps)]
    ins_attn = [pltpu.VMEM((4, QUARTER >> level, HEADS_WIDE), BF16) for level in range(steps)]
    vmem, hbm = pl.BlockSpec(memory_space=pltpu.VMEM), pl.BlockSpec(memory_space=pl.ANY)
    smem = pl.BlockSpec(memory_space=pltpu.SMEM)
    send_count = 48 + 8 * steps
    return pl.pallas_call(
        functools.partial(layer_kernel, bits),
        out_shape=(
            shape((2 * ROW_LEN, D), BF16),
            shape((2 * ROW_LEN, D), BF16),
            shape((block, 4 * HEADS_WIDE), F32),
            shape((3, block, D), F32),
            shape((8, D), F32),
            shape((2, ROW_LEN, D), BF16),
            shape((2, ROW_LEN, D), BF16),
            shape((QUARTER, D), F32),
        ),
        in_specs=[smem, hbm, hbm] + [vmem] * 4 + [hbm] * 3 + [vmem] * 8,
        out_specs=(hbm, hbm, hbm, hbm, vmem, hbm, hbm, hbm),
        scratch_shapes=[
            *[whole] * 8,
            pltpu.VMEM((HEADS_WIDE, D), BF16),
            pltpu.VMEM((ROW_LEN, HEADS_WIDE), BF16),
            row, row, single, single,
            pltpu.VMEM((QUARTER, D), F32),
            sums, sums, square, square, square,
            pltpu.VMEM((8, D), F32),
            pltpu.VMEM((steps + 2, 8, D), F32),
            *ins_mlp, *ins_attn,
            sems((32,)), sems((16,)), sems((send_count,)), sems((send_count,)),
        ],
        compiler_params=pltpu.CompilerParams(
            collective_id=1, has_side_effects=True, vmem_limit_bytes=64 * MIB
        ),
        name="layer",
    )(lengths, frames, cotangent, wq, wk, wv, wo, wg, wu, wd, gain1, bias1, gain2, bias2, scale1, scale2, rotary, rotary_start)


def deliver_kernel(
    frames_in, grad_in, attn_in, mlp_in, frames_to, grad_to, q_to, k_to, v_to, o_to, gate_to, up_to, down_to,
    frames_buf, grad_buf, attn_buf, mlp_buf, o_turned, down_turned, load_sems, store_sems,
):
    loads, stores = Copies(load_sems), Copies(store_sems)
    attn_load, mlp_load = loads.start(attn_in, attn_buf), loads.start(mlp_in, mlp_buf)
    count = frames_in.shape[0] // 4
    moves, waits = [], []
    for source, buf, target in ((frames_in, frames_buf, frames_to), (grad_in, grad_buf, grad_to)):
        for part in range(4):
            rows = pl.ds(part * count, count)
            moves.append((loads.start(source.at[rows], buf.at[rows]), buf.at[rows], target.at[rows]))
    attn_load.wait()
    for kind, target in enumerate((q_to, k_to, v_to)):
        waits.append(stores.start(attn_buf.at[:, pl.ds(kind * HEADS_WIDE, HEADS_WIDE)], target))
    mlp_load.wait()
    waits.append(stores.start(mlp_buf.at[0], gate_to))
    waits.append(stores.start(mlp_buf.at[1], up_to))
    for load, source, target in moves:
        load.wait()
        waits.append(stores.start(source, target))
    o_turned[...] = attn_buf[:, 3 * HEADS_WIDE :].T
    waits.append(stores.start(o_turned, o_to))
    down_turned[...] = mlp_buf[2].T
    waits.append(stores.start(down_turned, down_to))
    for copy in waits:
        copy.wait()


def deliver(frames_in, grad_in, attn_in, mlp_in):
    shape = jax.ShapeDtypeStruct
    block = attn_in.shape[0]
    hbm = pl.BlockSpec(memory_space=pl.ANY)
    small, large = (block, HEADS_WIDE), (block, D)
    return pl.pallas_call(
        deliver_kernel,
        out_shape=(
            shape(frames_in.shape, BF16), shape(grad_in.shape, BF16),
            shape(small, F32), shape(small, F32), shape(small, F32), shape(small[::-1], F32),
            shape(large, F32), shape(large, F32), shape(large[::-1], F32),
        ),
        in_specs=[hbm] * 4,
        out_specs=(hbm,) * 9,
        scratch_shapes=[
            pltpu.VMEM(frames_in.shape, BF16), pltpu.VMEM(grad_in.shape, BF16),
            pltpu.VMEM((block, D), F32), pltpu.VMEM((3, block, D), F32),
            pltpu.VMEM(small[::-1], F32), pltpu.VMEM(large[::-1], F32),
            pltpu.SemaphoreType.DMA((10,)), pltpu.SemaphoreType.DMA((15,)),
        ],
        compiler_params=pltpu.CompilerParams(vmem_limit_bytes=62 * MIB),
        name="deliver",
    )(frames_in, grad_in, attn_in, mlp_in)


def per_device(
    parts, frames, clip_lengths, query_weight, key_weight, value_weight, output_weight, gate_weight, up_weight,
    down_weight, attn_gain, attn_bias, mlp_gain, mlp_bias, attn_scale, mlp_scale, cotangent,
):
    out_frames, frames_grad, attn_part, mlp_part, vec = layer(
        parts, clip_lengths, frames, cotangent, query_weight, key_weight, value_weight, output_weight,
        gate_weight, up_weight, down_weight,
        *[vector.reshape(1, D) for vector in (attn_gain, attn_bias, mlp_gain, mlp_bias, attn_scale, mlp_scale)],
    )[:5]
    block = D // parts
    vec = lax.dynamic_slice_in_dim(vec, lax.axis_index("dp") * block, block, 1)
    arrays = deliver(out_frames, frames_grad, attn_part, mlp_part)
    return tuple(arrays) + tuple(vec[kind] for kind in range(6))


def solution(mesh):
    rows, whole = P("dp", None), P()
    in_weight, out_weight = P(None, "mp"), P("mp", None)
    in_specs = (
        (rows, rows, in_weight, in_weight, in_weight, out_weight, in_weight, in_weight, out_weight)
        + (whole,) * 6
        + (rows,)
    )
    scattered, turned = P("dp", "mp"), P("mp", "dp")
    out_specs = (
        rows, rows, scattered, scattered, scattered, turned, scattered, scattered, turned,
    ) + (P("dp"),) * 6
    return jax.shard_map(
        functools.partial(per_device, mesh.shape["dp"]),
        mesh=mesh,
        in_specs=in_specs,
        out_specs=out_specs,
        check_vma=False,
    )
```

```python
import functools

import jax
import jax.numpy as jnp
import numpy as np
from jax import lax
from jax.experimental import pallas as pl
from jax.experimental.pallas import tpu as pltpu
from jax.sharding import PartitionSpec as P

HEAD_DIM = 64
WINDOW = 128
ROW_LEN = 1024
QUARTER = 512
PIECE = 256
SMALL = 64
SLOTS = 8
CLIP_UNIT = 125
D = 1024
HEADS_WIDE = 256
F32 = jnp.float32
BF16 = jnp.bfloat16
MESH = pl.DeviceIdType.MESH
MIB = 2**20


def product(left, right, left_dim, right_dim):
    return lax.dot_general(
        left, right, (((left_dim,), (right_dim,)), ((), ())), preferred_element_type=F32
    )


def rotary_constants():
    half_dim = HEAD_DIM // 2
    inverse = 10000.0 ** (-np.arange(half_dim) / half_dim)
    inverse = np.concatenate([inverse] * 4)[None, :]
    frame_angle = np.arange(ROW_LEN)[:, None] * inverse
    start_angle = (CLIP_UNIT * np.arange(SLOTS + 1))[:, None] * inverse
    filler = np.zeros((16 - SLOTS - 1, 128))
    starts = np.stack(
        [np.concatenate([np.cos(start_angle), filler]), np.concatenate([np.sin(start_angle), filler])]
    )
    frame = np.stack([np.cos(frame_angle), np.sin(frame_angle)])
    return jnp.asarray(frame, F32), jnp.asarray(starts, F32)


class Copies:
    def __init__(self, sems):
        self.sems, self.count = sems, 0

    def start(self, source, target):
        copy = pltpu.make_async_copy(source, target, self.sems.at[self.count])
        self.count += 1
        copy.start()
        return copy


class Sends:
    def __init__(self, send_sems, recv_sems):
        self.send_sems, self.recv_sems, self.made = send_sems, recv_sems, []

    def start(self, source, target, partner):
        index = len(self.made)
        copy = pltpu.make_async_remote_copy(
            src_ref=source,
            dst_ref=target,
            send_sem=self.send_sems.at[index],
            recv_sem=self.recv_sems.at[index],
            device_id=partner,
            device_id_type=MESH,
        )
        copy.start()
        self.made.append([copy, False])
        return len(self.made) - 1

    def sent(self, *numbers):
        for number in numbers:
            if not self.made[number][1]:
                self.made[number][0].wait_send()
                self.made[number][1] = True

    def arrived(self, *numbers):
        for number in numbers:
            self.made[number][0].wait_recv()


def turned_by(field, cosine, sine):
    lane = lax.broadcasted_iota(jnp.int32, (1, 128), 1)
    lower = lane % HEAD_DIM < HEAD_DIM // 2
    halves = []
    for pair in range(field.shape[1] // 128):
        part = field[:, pair * 128 : pair * 128 + 128]
        swapped = jnp.where(lower, pltpu.roll(part, 96, 1), pltpu.roll(part, 32, 1))
        halves.append(part * cosine + swapped * sine)
    return jnp.concatenate(halves, 1)


def norm_of(source):
    centre = jnp.mean(source, -1, keepdims=True)
    centred = source - centre
    spread = lax.rsqrt(jnp.mean(centred * centred, -1, keepdims=True) + 1e-05)
    return centred * spread, spread


def norm_back(grad, unit, spread, gain):
    scaled = grad * gain
    inner = scaled - jnp.mean(scaled, -1, keepdims=True) - unit * jnp.mean(scaled * unit, -1, keepdims=True)
    return inner * spread


def column_sum(field):
    return jnp.sum(field, 0, keepdims=True)


def split_heads(pair):
    lane = lax.broadcasted_iota(jnp.int32, pair.shape, 1)
    zero = jnp.zeros_like(pair)
    return jnp.concatenate(
        [jnp.where(lane < HEAD_DIM, pair, zero), jnp.where(lane >= HEAD_DIM, pair, zero)], 0
    )


def join_heads(stacked):
    rows = stacked.shape[0] // 2
    lane = lax.broadcasted_iota(jnp.int32, (rows, 128), 1)
    return jnp.where(lane < HEAD_DIM, stacked[:rows], stacked[rows:])


def span(start, size):
    return pl.ds(pl.multiple_of(start, size), size)


def layer_kernel(
    bits,
    lengths, frames, cotangent, wq, wk, wv, wo, wg, wu, wd,
    gain1, bias1, gain2, bias2, scale1, scale2, rotary, rotary_start,
    out_frames, frames_grad, attn_grads_out, mlp_grads_out, vec_out, low_spill, head_spill, branch_spill,
    x0, x1, x2, x3, x4, x5, x6, x7, wo_other, att_other, core_g, core_m, side_g, side_m, wide, dk_sum, dv_sum,
    wg_buf, wu_buf, wd_buf, vec, vec_in, *rest,
):
    steps = len(bits)
    in_mlp, in_attn = rest[:steps], rest[steps : 2 * steps]
    load_sems, store_sems, send_sems, recv_sems = rest[2 * steps :]
    data, model = lax.axis_index("dp"), lax.axis_index("mp")
    core, side = model % 2, model // 2
    side_model = model + 2 - 4 * side
    core_dev, side_dev = (data, model + 1 - 2 * core), (data, side_model)
    own_bit = {bit: (data // bit) % 2 for bit in bits}
    bit_dev = {bit: (data + bit * (1 - 2 * own_bit[bit]), model) for bit in bits}
    data_dev = [bit_dev[bit] for bit in bits]

    def order_of(which):
        if which in (1, 4, 6) and steps > 1:
            return [bits[1], bits[0]] + bits[2:]
        return bits

    loads, stores, sends = Copies(load_sems), Copies(store_sems), Sends(send_sems, recv_sems)
    block = D // 2**steps

    rows_of = (1 - side, side)
    halves = (1 - core, core)

    def quarter_rows(group, slot):
        return span(rows_of[group] * ROW_LEN + halves[slot] * QUARTER, QUARTER)

    def own_rows(owner, step):
        return span(owner * QUARTER + step * PIECE, PIECE)

    def at_slot(slot, step):
        return pl.ds(slot * QUARTER + step * PIECE, PIECE)

    def piece(step):
        return pl.ds(step * PIECE, PIECE)

    frame_loads = []
    for index in range(2):
        for part in range(4):
            frame_loads.append(
                loads.start(
                    frames.at[span(rows_of[index] * ROW_LEN + part * PIECE, PIECE)],
                    x0.at[index, pl.ds(part * PIECE, PIECE)],
                )
            )
    weight_loads = [loads.start(wg, wg_buf), loads.start(wu, wu_buf), loads.start(wd, wd_buf)]
    cot_loads = {}
    for group in range(2):
        for slot in range(2):
            cot_loads[group, slot] = loads.start(
                cotangent.at[quarter_rows(group, slot)], x4.at[group, pl.ds(slot * QUARTER, QUARTER)]
            )
    barrier = pltpu.get_barrier_semaphore()
    partners = [core_dev, side_dev] + data_dev
    for partner in partners:
        pl.semaphore_signal(barrier, inc=1, device_id=partner, device_id_type=MESH)
    pl.semaphore_wait(barrier, len(partners))

    def clip_facts(index, first, count):
        frame_ids = lax.broadcasted_iota(jnp.int32, (count, 128), 0) + first
        start_ids = jnp.zeros((count, 128), jnp.int32)
        end = 0
        for slot in range(SLOTS):
            length = lengths[rows_of[index], slot]
            end = end + length
            start_ids = start_ids + jnp.where(frame_ids >= end, length, 0)
        return frame_ids, start_ids

    def angles(index, first, count, direction):
        frame_ids = lax.broadcasted_iota(jnp.int32, (count, 128), 0) + first
        start_cos = jnp.broadcast_to(rotary_start[0, 0:1], (count, 128))
        start_sin = jnp.broadcast_to(rotary_start[1, 0:1], (count, 128))
        end = 0
        for slot in range(SLOTS):
            end = end + lengths[rows_of[index], slot]
            number = lax.div(end, jnp.int32(CLIP_UNIT))
            passed = frame_ids >= end
            start_cos = jnp.where(passed, rotary_start[0, pl.ds(number, 1)], start_cos)
            start_sin = jnp.where(passed, rotary_start[1, pl.ds(number, 1)], start_sin)
        frame_cos, frame_sin = rotary[0, pl.ds(first, count)], rotary[1, pl.ds(first, count)]
        lane = lax.broadcasted_iota(jnp.int32, (count, 128), 1)
        cosine = frame_cos * start_cos + frame_sin * start_sin
        sine = frame_sin * start_cos - frame_cos * start_sin
        sign = jnp.where(lane % HEAD_DIM < HEAD_DIM // 2, -direction, direction)
        return cosine, sine * sign

    def window(index, number):
        lead = 1 - (7 - number) // 7
        first = pl.multiple_of(number * WINDOW, WINDOW)
        key_first = pl.multiple_of((number - lead) * WINDOW, WINDOW)
        frame_ids, start_ids = clip_facts(index, first, WINDOW)
        limit = jnp.minimum(frame_ids - start_ids, WINDOW - 1)
        limit = jnp.concatenate([limit, limit], 1)
        row_ids = lax.broadcasted_iota(jnp.int32, (WINDOW, 2 * WINDOW), 0)
        col_ids = lax.broadcasted_iota(jnp.int32, (WINDOW, 2 * WINDOW), 1)
        distance = row_ids - col_ids + lead * WINDOW
        bias = jnp.where((distance >= 0) & (distance <= limit), 0.0, -1e30)
        return pl.ds(first, WINDOW), pl.ds(key_first, 2 * WINDOW), jnp.concatenate([bias, bias], 0)

    def columns(kind, pair=None):
        if pair is None:
            return slice(kind * HEADS_WIDE, kind * HEADS_WIDE + HEADS_WIDE)
        return slice(kind * HEADS_WIDE + pair * 128, kind * HEADS_WIDE + pair * 128 + 128)

    other_weight = sends.start(wo, wo_other, side_dev)
    att_sent, spills, core_sent, side_low, core_low = [], [], [], [], []
    ones = jnp.ones((2 * WINDOW, 128), BF16)
    for index in range(2):
        for part in range(4):
            frame_loads[index * 4 + part].wait()

        @pl.loop(0, ROW_LEN // PIECE)
        def _(step):
            rows = span(step * PIECE, PIECE)
            unit, _spread = norm_of(x0[index, rows].astype(F32))
            low = (unit * gain1[...] + bias1[...]).astype(BF16)
            x1[index, rows] = low
            cosine, sine = angles(index, pl.multiple_of(step * PIECE, PIECE), PIECE, 1.0)
            x2[index, rows, columns(0)] = turned_by(product(low, wq[...], 1, 0), cosine, sine).astype(BF16)
            x2[index, rows, columns(1)] = turned_by(product(low, wk[...], 1, 0), cosine, sine).astype(BF16)
            x2[index, rows, columns(2)] = product(low, wv[...], 1, 0).astype(BF16)

        spills.append(stores.start(x1.at[index], low_spill.at[index]))

        def attend(half, step):
            for inner in range(PIECE // WINDOW):
                rows, key_rows, bias = window(index, half * 4 + step * 2 + inner)
                for pair in range(2):
                    query = split_heads(x2[index, rows, columns(0, pair)])
                    scores = product(query, x2[index, key_rows, columns(1, pair)], 1, 1)
                    scores = scores * HEAD_DIM**-0.5 + bias
                    expo = jnp.exp(scores - jnp.max(scores, -1, keepdims=True)).astype(BF16)
                    values = jnp.concatenate([x2[index, key_rows, columns(2, pair)], ones], 1)
                    result = product(expo, values, 1, 0)
                    x2[index, rows, columns(3, pair)] = (
                        join_heads(result[:, :128]) / join_heads(result[:, 128:])
                    ).astype(BF16)

        for step in range(2):
            if index == 0:
                for half in range(2):
                    attend(half, step)
                    rows = pl.ds(half * QUARTER + step * PIECE, PIECE)
                    att_sent.append(sends.start(x2.at[0, rows, columns(3)], att_other.at[rows], side_dev))
                continue

            for slot in range(2):
                attend(halves[slot], step)
                if step == 0 and slot == 0:
                    sends.arrived(other_weight)
                if slot == 0:
                    sends.arrived(att_sent[2 * step], att_sent[2 * step + 1])
                rows = span(halves[slot] * QUARTER + step * PIECE, PIECE)
                fresh = product(x2[1, rows, columns(3)], wo[...], 1, 0) + product(
                    att_other[rows], wo_other[...], 1, 0
                )
                if slot == 0:
                    x5[1, piece(step)] = fresh.astype(BF16)
                    core_sent.append(sends.start(x5.at[1, piece(step)], core_g.at[1, piece(step)], core_dev))
                else:
                    wide[piece(step)] = fresh
            sends.arrived(core_sent[step])

            @pl.loop(0, PIECE // SMALL)
            def _(small):
                here = span(step * PIECE + small * SMALL, SMALL)
                there = span(QUARTER + step * PIECE + small * SMALL, SMALL)
                branch = wide[here] + core_g[1, here].astype(F32)
                wide[here] = branch
                source = x0[1, span(core * QUARTER + step * PIECE + small * SMALL, SMALL)].astype(F32)
                unit, _spread = norm_of(source + scale1[...] * branch)
                x3[1, there] = (unit * gain2[...] + bias2[...]).astype(BF16)

            rows = at_slot(1, step)
            side_low.append(sends.start(x3.at[1, rows], x3.at[0, rows], side_dev))
            core_low.append(sends.start(x3.at[1, rows], x3.at[1, at_slot(0, step)], core_dev))
        spills.append(stores.start(x2.at[index], head_spill.at[index]))

    spills.append(stores.start(wide, branch_spill))
    for copy in spills + weight_loads:
        copy.wait()
    sends.sent(*core_sent, *att_sent)
    vec[...] = jnp.zeros((8, D), F32)

    def chunk(group, slot, step):
        rows = at_slot(slot, step)
        low = x3[group, rows]
        grad = (scale2[...] * x4[group, rows].astype(F32)).astype(BF16)
        x4[group, rows] = grad
        for tile in range(4):
            cols = slice(tile * 256, tile * 256 + 256)
            gating = product(low, wg_buf[:, cols], 1, 0)
            upward = product(low, wu_buf[:, cols], 1, 0)
            grad_hidden = product(grad, wd_buf[cols], 1, 1)
            sigma = 0.5 * jnp.tanh(0.5 * gating) + 0.5
            active = gating * sigma
            x0[group, rows, cols] = (active * upward).astype(BF16)
            x1[group, rows, cols] = (grad_hidden * upward * (sigma + active * (1.0 - sigma))).astype(BF16)
            x2[group, rows, cols] = (grad_hidden * active).astype(BF16)
        for tile in range(4):
            cols = slice(tile * 256, tile * 256 + 256)
            x5[group, rows, cols] = (
                product(x1[group, rows], wg_buf[cols], 1, 1) + product(x2[group, rows], wu_buf[cols], 1, 1)
            ).astype(BF16)
            x6[group, rows, cols] = product(x0[group, rows], wd_buf[:, cols], 1, 0).astype(BF16)

    core_grad, core_part, side_grad, core_again, side_mlp = {}, {}, [], [], []
    for group, step in ((1, 0), (0, 0), (0, 1), (1, 1)):
        if group == 1:
            sends.arrived(core_low[step])
        else:
            sends.arrived(side_low[step])
            core_again.append(sends.start(x3.at[0, at_slot(1, step)], x3.at[0, at_slot(0, step)], core_dev))
            sends.arrived(core_again[step])
        for slot in range(2):
            if step == 0:
                cot_loads[group, slot].wait()
            chunk(group, slot, step)
            if slot == 0:
                rows = at_slot(0, step)
                core_grad[group, step] = sends.start(x5.at[group, rows], core_g.at[group, piece(step)], core_dev)
                core_part[group, step] = sends.start(x6.at[group, rows], core_m.at[group, piece(step)], core_dev)
        if group == 0:
            rows = at_slot(1, step)
            sends.arrived(core_grad[0, step])
            x5[0, rows] = (x5[0, rows].astype(F32) + core_g[0, piece(step)].astype(F32)).astype(BF16)
            side_grad.append(sends.start(x5.at[0, rows], side_g.at[piece(step)], side_dev))
            sends.arrived(core_part[0, step])
            x6[0, rows] = (x6[0, rows].astype(F32) + core_m[0, piece(step)].astype(F32)).astype(BF16)
            if step == 1:
                side_mlp.append(sends.start(x6.at[0, at_slot(1, 0)], side_m.at[piece(0)], side_dev))

    quarter_loads = [
        loads.start(frames.at[span(model * QUARTER, QUARTER)], wd_buf.at[pl.ds(0, QUARTER)]),
        loads.start(cotangent.at[span(model * QUARTER, QUARTER)], wd_buf.at[pl.ds(QUARTER, QUARTER)]),
    ]
    low_loads = [loads.start(low_spill.at[0], wg_buf), loads.start(low_spill.at[1], wu_buf)]

    def kept(which, half, start, size):
        if which == 0:
            return x6.at[half, pl.ds(start, size)]
        if which == 1:
            return x1.at[0, pl.ds(half * QUARTER + start, size)]
        if which == 2:
            return x3.at[0, pl.ds(half * QUARTER + start, size)]
        return x3.at[1, pl.ds(half * QUARTER + start, size), columns(which - 3)]

    def arriving(level, which):
        return in_mlp[level].at[which] if which < 3 else in_attn[level].at[which - 3]

    data_sent = {}

    def place_blocks(which, tile, total, cols):
        fresh = total.astype(BF16)
        for number in range(QUARTER // block):
            natural = tile * (QUARTER // block) + number
            whole = sum(((natural // bit) % 2) << place for place, bit in enumerate(order_of(which)))
            target = kept(which, whole % 2, (whole // 2) * block, block)
            target[:, cols] = fresh[number * block : number * block + block]

    def send_half(which):
        data_sent[0, which] = sends.start(
            kept(which, 1 - own_bit[order_of(which)[0]], 0, QUARTER),
            arriving(0, which),
            bit_dev[order_of(which)[0]],
        )

    def mlp_grad(which):
        left, right = ((x3, x1), (x3, x2), (x4, x0))[which]
        for tile in range(2):

            @pl.loop(0, 2)
            def _(part):
                cols = span(part * 512, 512)
                total = None
                for group in range(2):
                    fresh = product(left[group, :, tile * 512 : tile * 512 + 512], right[group, :, cols], 0, 0)
                    total = fresh if total is None else total + fresh
                place_blocks(which, tile, total, cols)

        send_half(which)

    def data_step(level, which):
        copy = data_sent[level, which]
        order = order_of(which)
        mine = [own_bit[bit] for bit in order]
        sends.arrived(copy)
        sends.sent(copy)
        size = QUARTER >> level
        source_half = mine[0] if level % 2 == 0 else 1 - mine[0]
        offset = 0 if level == 0 else mine[level] * size
        come = arriving(level, which)
        for number in range(size // block):
            own = kept(which, source_half, offset + number * block, block)[...]
            fresh = own.astype(F32) + come[number * block : number * block + block].astype(F32)
            if level == steps - 1:
                if which < 3:
                    wide[which * block : which * block + block] = fresh
                else:
                    wide[3 * block : 4 * block, columns(which - 3)] = fresh
            else:
                target = kept(
                    which, 1 - source_half, (number % 2) * (size // 2) + (number // 2) * block, block
                )
                target[...] = fresh.astype(BF16)
        if level < steps - 1:
            away = 1 - mine[level + 1]
            data_sent[level + 1, which] = sends.start(
                kept(which, 1 - source_half, away * (size // 2), size // 2),
                arriving(level + 1, which),
                bit_dev[order[level + 1]],
            )

    side_branch, core_branch = [], []

    def own_backward(step):
        sends.arrived(core_grad[1, step], side_grad[step])

        @pl.loop(0, PIECE // SMALL)
        def _(small):
            here = span(step * PIECE + small * SMALL, SMALL)
            there = span(QUARTER + step * PIECE + small * SMALL, SMALL)
            branch = wide[here]
            grad_out = wd_buf[there].astype(F32)
            midway = wd_buf[here].astype(F32) + scale1[...] * branch
            grad_norm = x5[1, there].astype(F32) + core_g[1, here].astype(F32) + side_g[here].astype(F32)
            unit, spread = norm_of(midway)
            vec[2:3] += column_sum(grad_norm * unit)
            vec[3:4] += column_sum(grad_norm)
            grad_mid = grad_out + norm_back(grad_norm, unit, spread, gain2[...])
            vec[4:5] += column_sum(grad_mid * branch)
            x7[1, there] = (scale1[...] * grad_mid).astype(BF16)
            wide[here] = grad_mid

        rows = at_slot(1, step)
        core_branch.append(sends.start(x7.at[1, rows], x7.at[1, at_slot(0, step)], core_dev))
        side_branch.append(sends.start(x7.at[1, rows], x7.at[0, rows], side_dev))

    def row_back(index, between):
        for slot in range(2):

            @pl.loop(0, QUARTER // PIECE)
            def _(step):
                rows = span(halves[slot] * QUARTER + step * PIECE, PIECE)
                x4[index, rows, columns(3)] = product(
                    x7[index, span(slot * QUARTER + step * PIECE, PIECE)], wo[...], 1, 1
                ).astype(BF16)

        dk_sum[...] = jnp.zeros(dk_sum.shape, F32)
        dv_sum[...] = jnp.zeros(dv_sum.shape, F32)

        @pl.loop(0, ROW_LEN // PIECE)
        def _(step):
            for inner in range(PIECE // WINDOW):
                rows, key_rows, bias = window(index, step * 2 + inner)
                for pair in range(2):
                    lanes = slice(pair * 128, pair * 128 + 128)
                    query = split_heads(x2[index, rows, columns(0, pair)])
                    keys = x2[index, key_rows, columns(1, pair)]
                    values = x2[index, key_rows, columns(2, pair)]
                    grad = split_heads(x4[index, rows, columns(3, pair)])
                    scores = product(query, keys, 1, 1) * HEAD_DIM**-0.5 + bias
                    expo = jnp.exp(scores - jnp.max(scores, -1, keepdims=True))
                    inverse = 1.0 / product(expo.astype(BF16), ones, 1, 0)
                    probs = expo * jnp.concatenate([inverse, inverse], 1)
                    grad_probs = product(grad, values, 1, 1)
                    inside = grad.astype(F32) * split_heads(x2[index, rows, columns(3, pair)]).astype(F32)
                    inside = product(inside.astype(BF16), ones[:128], 1, 0)
                    inside = jnp.concatenate([inside, inside], 1)
                    grad_logits = (probs * (grad_probs - inside) * HEAD_DIM**-0.5).astype(BF16)
                    x4[index, rows, columns(0, pair)] = join_heads(product(grad_logits, keys, 1, 0)).astype(BF16)
                    dk_sum[key_rows, lanes] += product(grad_logits, query, 0, 0)
                    dv_sum[key_rows, lanes] += product(probs.astype(BF16), grad, 0, 0)

        between()

        for slot in range(2):

            @pl.loop(0, QUARTER // PIECE)
            def _(step):
                first = pl.multiple_of(halves[slot] * QUARTER + step * PIECE, PIECE)
                rows = pl.ds(first, PIECE)
                cosine, sine = angles(index, first, PIECE, -1.0)
                grad_q = turned_by(x4[index, rows, columns(0)].astype(F32), cosine, sine).astype(BF16)
                grad_k = turned_by(dk_sum[rows].astype(BF16).astype(F32), cosine, sine).astype(BF16)
                grad_v = dv_sum[rows].astype(BF16)
                x4[index, rows, columns(0)] = grad_q
                x4[index, rows, columns(1)] = grad_k
                x4[index, rows, columns(2)] = grad_v
                x5[index, span(slot * QUARTER + step * PIECE, PIECE)] = (
                    product(grad_q, wq[...], 1, 1) + product(grad_k, wk[...], 1, 1) + product(grad_v, wv[...], 1, 1)
                ).astype(BF16)

            if slot == 0:
                return_sent[index] = sends.start(x5.at[index, pl.ds(0, QUARTER)], core_g.at[index], core_dev)

    return_sent = {}

    def attn_grad(which):
        kind = which - 3
        for tile in range(2):
            cols = slice(tile * 512, tile * 512 + 512)
            total = None
            for index in range(2):
                if kind < 3:
                    left = (wg_buf, wu_buf)[index]
                    pairs = [(left[:, cols], x4[index, :, columns(kind)])]
                else:
                    pairs = [
                        (
                            x7[index, pl.ds(slot * QUARTER, QUARTER), cols],
                            x2[index, span(halves[slot] * QUARTER, QUARTER), columns(3)],
                        )
                        for slot in range(2)
                    ]
                for left, right in pairs:
                    fresh = product(left, right, 0, 0)
                    total = fresh if total is None else total + fresh
            place_blocks(which, tile, total, slice(None))
        send_half(which)

    sends.sent(*core_part.values())
    mlp_grad(0)
    for copy in quarter_loads:
        copy.wait()
    own_backward(0)
    mlp_grad(1)
    head_load = loads.start(head_spill, x2)
    own_backward(1)
    sends.sent(*core_low, *side_low, *core_again)
    mlp_grad(2)
    side_mlp.append(sends.start(x6.at[0, at_slot(1, 1)], side_m.at[piece(1)], side_dev))
    sends.arrived(*core_branch)
    head_load.wait()
    sends.sent(*core_grad.values(), *side_grad)
    row_back(1, lambda: None)
    core_frames, side_frames = [], []

    def branch_back(step):
        return [
            loads.start(branch_spill.at[piece(step), pl.ds(part * 256, 256)], dk_sum.at[pl.ds(part * PIECE, PIECE)])
            for part in range(4)
        ]

    def own_frames(step, branch_loads):
        sends.arrived(core_part[1, step], side_mlp[step])
        for part in range(4):
            branch_loads[part].wait()
            cols = slice(part * 256, part * 256 + 256)
            here, there = piece(step), at_slot(1, step)
            mlp_branch = x6[1, there, cols].astype(F32) + core_m[1, here, cols].astype(F32) + side_m[here, cols].astype(F32)
            vec[5:6, cols] += column_sum(wd_buf[there, cols].astype(F32) * mlp_branch)
            midway = wd_buf[here, cols].astype(F32) + scale1[:, cols] * dk_sum[pl.ds(part * PIECE, PIECE)]
            x6[1, there, cols] = (midway + scale2[:, cols] * mlp_branch).astype(BF16)
        core_frames.append(sends.start(x6.at[1, at_slot(1, step)], out_frames.at[own_rows(model, step)], core_dev))

    def side_frame(step):
        side_frames.append(sends.start(x6.at[1, at_slot(1, step)], out_frames.at[own_rows(model, step)], side_dev))

    branch_loads = branch_back(0)
    gathered = []
    for step in range(2):
        sends.arrived(side_branch[step])
        gathered.append(sends.start(x7.at[0, at_slot(1, step)], x7.at[0, at_slot(0, step)], core_dev))
    data_step(0, 0)
    own_frames(0, branch_loads)
    side_frame(0)
    data_step(0, 1)
    sends.arrived(*gathered)

    def second_level(*chosen):
        if steps > 1:
            for which in chosen:
                data_step(1, which)

    row_back(0, lambda: second_level(0))
    sends.arrived(return_sent[0])
    side_return = []
    for step in range(2):
        rows = at_slot(1, step)
        x5[0, rows] = (x5[0, rows].astype(F32) + core_g[0, piece(step)].astype(F32)).astype(BF16)
        side_return.append(sends.start(x5.at[0, rows], side_g.at[piece(step)], side_dev))
    branch_loads = branch_back(1)
    for copy in low_loads:
        copy.wait()
    for which in (6, 3):
        attn_grad(which)
    data_step(0, 2)
    second_level(1)
    for which in (4, 5):
        attn_grad(which)
    own_frames(1, branch_loads)
    final_stores = [stores.start(x6.at[1, pl.ds(QUARTER, QUARTER)], out_frames.at[span(model * QUARTER, QUARTER)])]

    sends.arrived(return_sent[1])
    core_out, side_out = [], []
    for step in range(2):
        sends.arrived(side_return[step])

        @pl.loop(0, PIECE // SMALL)
        def _(small):
            here = span(step * PIECE + small * SMALL, SMALL)
            there = span(QUARTER + step * PIECE + small * SMALL, SMALL)
            grad_norm = x5[1, there].astype(F32) + core_g[1, here].astype(F32) + side_g[here].astype(F32)
            unit, spread = norm_of(wd_buf[here].astype(F32))
            vec[0:1] += column_sum(grad_norm * unit)
            vec[1:2] += column_sum(grad_norm)
            x5[1, there] = (wide[here] + norm_back(grad_norm, unit, spread, gain1[...])).astype(BF16)

        rows = at_slot(1, step)
        side_out.append(sends.start(x5.at[1, rows], frames_grad.at[own_rows(model, step)], side_dev))
        core_out.append(sends.start(x5.at[1, rows], frames_grad.at[own_rows(model, step)], core_dev))
        if step == 0:
            side_frame(1)
            second_level(2)
    final_stores.append(stores.start(x5.at[1, pl.ds(QUARTER, QUARTER)], frames_grad.at[span(model * QUARTER, QUARTER)]))

    vec_devs, vec_sent = partners, []

    def vec_step():
        level = len(vec_sent)
        if level == len(vec_devs):
            return
        if level > 0:
            sends.arrived(vec_sent[-1])
            sends.sent(vec_sent[-1])
            vec[...] += vec_in[level - 1]
        if level < len(vec_devs):
            vec_sent.append(sends.start(vec, vec_in.at[level], vec_devs[level]))

    last = []

    def second_hop(arriving_copy, target, step):
        sends.arrived(arriving_copy)
        rows = own_rows(side_model, step)
        last.append(sends.start(target.at[rows], target.at[rows], core_dev))

    vec_step()
    second_hop(side_frames[0], out_frames, 0)
    for which in (6, 3):
        data_step(0, which)
    vec_step()
    for which in (4, 5):
        data_step(0, which)
    vec_step()
    for level in range(2, steps):
        if level == 2:
            second_level(6, 3)
            vec_step()
            second_level(4, 5)
            vec_step()
        for which in (0, 1, 2):
            data_step(level, which)
        if level == 2:
            second_hop(side_out[0], frames_grad, 0)
        for which in (6, 3, 4, 5):
            data_step(level, which)
    while len(vec_sent) < len(vec_devs):
        vec_step()
    sends.arrived(vec_sent[-1])
    sends.sent(vec_sent[-1])
    vec_out[...] = vec[...] + vec_in[len(vec_devs) - 1]
    for which in range(3):
        final_stores.append(stores.start(wide.at[pl.ds(which * block, block)], mlp_grads_out.at[which]))
    final_stores.append(stores.start(wide.at[pl.ds(3 * block, block)], attn_grads_out))
    second_hop(side_frames[1], out_frames, 1)
    second_hop(side_out[1], frames_grad, 1)
    sends.arrived(*core_frames, *core_out, *last)
    sends.sent(*range(len(sends.made)))
    for copy in final_stores:
        copy.wait()


def layer(parts, lengths, frames, cotangent, wq, wk, wv, wo, wg, wu, wd, gain1, bias1, gain2, bias2, scale1, scale2):
    shape = jax.ShapeDtypeStruct
    sems = pltpu.SemaphoreType.DMA
    block = D // parts
    bits = []
    while 2 ** len(bits) < parts:
        bits.append(2 ** len(bits))
    steps = len(bits)
    rotary, rotary_start = rotary_constants()
    whole = pltpu.VMEM((2, ROW_LEN, D), BF16)
    row = pltpu.VMEM((2, QUARTER, D), BF16)
    single = pltpu.VMEM((QUARTER, D), BF16)
    square = pltpu.VMEM((D, D), BF16)
    sums = pltpu.VMEM((ROW_LEN, HEADS_WIDE), F32)
    ins_mlp = [pltpu.VMEM((3, QUARTER >> level, D), BF16) for level in range(steps)]
    ins_attn = [pltpu.VMEM((4, QUARTER >> level, HEADS_WIDE), BF16) for level in range(steps)]
    vmem, hbm = pl.BlockSpec(memory_space=pltpu.VMEM), pl.BlockSpec(memory_space=pl.ANY)
    smem = pl.BlockSpec(memory_space=pltpu.SMEM)
    send_count = 56 + 8 * steps
    return pl.pallas_call(
        functools.partial(layer_kernel, bits),
        out_shape=(
            shape((2 * ROW_LEN, D), BF16),
            shape((2 * ROW_LEN, D), BF16),
            shape((block, 4 * HEADS_WIDE), F32),
            shape((3, block, D), F32),
            shape((8, D), F32),
            shape((2, ROW_LEN, D), BF16),
            shape((2, ROW_LEN, D), BF16),
            shape((QUARTER, D), F32),
        ),
        in_specs=[smem, hbm, hbm] + [vmem] * 4 + [hbm] * 3 + [vmem] * 8,
        out_specs=(hbm, hbm, hbm, hbm, vmem, hbm, hbm, hbm),
        scratch_shapes=[
            *[whole] * 8,
            pltpu.VMEM((HEADS_WIDE, D), BF16),
            pltpu.VMEM((ROW_LEN, HEADS_WIDE), BF16),
            row, row, single, single,
            pltpu.VMEM((QUARTER, D), F32),
            sums, sums, square, square, square,
            pltpu.VMEM((8, D), F32),
            pltpu.VMEM((steps + 2, 8, D), F32),
            *ins_mlp, *ins_attn,
            sems((32,)), sems((16,)), sems((send_count,)), sems((send_count,)),
        ],
        compiler_params=pltpu.CompilerParams(
            collective_id=1, has_side_effects=True, vmem_limit_bytes=64 * MIB
        ),
        name="layer",
    )(lengths, frames, cotangent, wq, wk, wv, wo, wg, wu, wd, gain1, bias1, gain2, bias2, scale1, scale2, rotary, rotary_start)


def deliver_kernel(
    frames_in, grad_in, attn_in, mlp_in, frames_to, grad_to, q_to, k_to, v_to, o_to, gate_to, up_to, down_to,
    frames_buf, grad_buf, attn_buf, mlp_buf, o_turned, down_turned, load_sems, store_sems,
):
    loads, stores = Copies(load_sems), Copies(store_sems)
    attn_load, mlp_load = loads.start(attn_in, attn_buf), loads.start(mlp_in, mlp_buf)
    count = frames_in.shape[0] // 4
    moves, waits = [], []
    for source, buf, target in ((frames_in, frames_buf, frames_to), (grad_in, grad_buf, grad_to)):
        for part in range(4):
            rows = pl.ds(part * count, count)
            moves.append((loads.start(source.at[rows], buf.at[rows]), buf.at[rows], target.at[rows]))
    attn_load.wait()
    for kind, target in enumerate((q_to, k_to, v_to)):
        waits.append(stores.start(attn_buf.at[:, pl.ds(kind * HEADS_WIDE, HEADS_WIDE)], target))
    mlp_load.wait()
    waits.append(stores.start(mlp_buf.at[0], gate_to))
    waits.append(stores.start(mlp_buf.at[1], up_to))
    for load, source, target in moves:
        load.wait()
        waits.append(stores.start(source, target))
    o_turned[...] = attn_buf[:, 3 * HEADS_WIDE :].T
    waits.append(stores.start(o_turned, o_to))
    down_turned[...] = mlp_buf[2].T
    waits.append(stores.start(down_turned, down_to))
    for copy in waits:
        copy.wait()


def deliver(frames_in, grad_in, attn_in, mlp_in):
    shape = jax.ShapeDtypeStruct
    block = attn_in.shape[0]
    hbm = pl.BlockSpec(memory_space=pl.ANY)
    small, large = (block, HEADS_WIDE), (block, D)
    return pl.pallas_call(
        deliver_kernel,
        out_shape=(
            shape(frames_in.shape, BF16), shape(grad_in.shape, BF16),
            shape(small, F32), shape(small, F32), shape(small, F32), shape(small[::-1], F32),
            shape(large, F32), shape(large, F32), shape(large[::-1], F32),
        ),
        in_specs=[hbm] * 4,
        out_specs=(hbm,) * 9,
        scratch_shapes=[
            pltpu.VMEM(frames_in.shape, BF16), pltpu.VMEM(grad_in.shape, BF16),
            pltpu.VMEM((block, D), F32), pltpu.VMEM((3, block, D), F32),
            pltpu.VMEM(small[::-1], F32), pltpu.VMEM(large[::-1], F32),
            pltpu.SemaphoreType.DMA((10,)), pltpu.SemaphoreType.DMA((15,)),
        ],
        compiler_params=pltpu.CompilerParams(vmem_limit_bytes=62 * MIB),
        name="deliver",
    )(frames_in, grad_in, attn_in, mlp_in)


def per_device(
    parts, frames, clip_lengths, query_weight, key_weight, value_weight, output_weight, gate_weight, up_weight,
    down_weight, attn_gain, attn_bias, mlp_gain, mlp_bias, attn_scale, mlp_scale, cotangent,
):
    out_frames, frames_grad, attn_part, mlp_part, vec = layer(
        parts, clip_lengths, frames, cotangent, query_weight, key_weight, value_weight, output_weight,
        gate_weight, up_weight, down_weight,
        *[vector.reshape(1, D) for vector in (attn_gain, attn_bias, mlp_gain, mlp_bias, attn_scale, mlp_scale)],
    )[:5]
    block = D // parts
    vec = lax.dynamic_slice_in_dim(vec, lax.axis_index("dp") * block, block, 1)
    arrays = deliver(out_frames, frames_grad, attn_part, mlp_part)
    return tuple(arrays) + tuple(vec[kind] for kind in range(6))


def solution(mesh):
    rows, whole = P("dp", None), P()
    in_weight, out_weight = P(None, "mp"), P("mp", None)
    in_specs = (
        (rows, rows, in_weight, in_weight, in_weight, out_weight, in_weight, in_weight, out_weight)
        + (whole,) * 6
        + (rows,)
    )
    scattered, turned = P("dp", "mp"), P("mp", "dp")
    out_specs = (
        rows, rows, scattered, scattered, scattered, turned, scattered, scattered, turned,
    ) + (P("dp"),) * 6
    return jax.shard_map(
        functools.partial(per_device, mesh.shape["dp"]),
        mesh=mesh,
        in_specs=in_specs,
        out_specs=out_specs,
        check_vma=False,
    )
```

```python
import functools

import jax
import jax.numpy as jnp
import numpy as np
from jax import lax
from jax.experimental import pallas as pl
from jax.experimental.pallas import tpu as pltpu
from jax.sharding import PartitionSpec as P

HEAD_DIM = 64
WINDOW = 128
ROW_LEN = 1024
QUARTER = 512
PIECE = 256
SMALL = 64
SLOTS = 8
CLIP_UNIT = 125
D = 1024
HEADS_WIDE = 256
F32 = jnp.float32
BF16 = jnp.bfloat16
MESH = pl.DeviceIdType.MESH
MIB = 2**20


def product(left, right, left_dim, right_dim):
    return lax.dot_general(
        left, right, (((left_dim,), (right_dim,)), ((), ())), preferred_element_type=F32
    )


def rotary_constants():
    half_dim = HEAD_DIM // 2
    inverse = 10000.0 ** (-np.arange(half_dim) / half_dim)
    inverse = np.concatenate([inverse] * 4)[None, :]
    frame_angle = np.arange(ROW_LEN)[:, None] * inverse
    start_angle = (CLIP_UNIT * np.arange(SLOTS + 1))[:, None] * inverse
    filler = np.zeros((16 - SLOTS - 1, 128))
    starts = np.stack(
        [np.concatenate([np.cos(start_angle), filler]), np.concatenate([np.sin(start_angle), filler])]
    )
    frame = np.stack([np.cos(frame_angle), np.sin(frame_angle)])
    return jnp.asarray(frame, F32), jnp.asarray(starts, F32)


class Copies:
    def __init__(self, sems):
        self.sems, self.count = sems, 0

    def start(self, source, target):
        copy = pltpu.make_async_copy(source, target, self.sems.at[self.count])
        self.count += 1
        copy.start()
        return copy


class Sends:
    def __init__(self, send_sems, recv_sems):
        self.send_sems, self.recv_sems, self.made = send_sems, recv_sems, []

    def start(self, source, target, partner):
        index = len(self.made)
        copy = pltpu.make_async_remote_copy(
            src_ref=source,
            dst_ref=target,
            send_sem=self.send_sems.at[index],
            recv_sem=self.recv_sems.at[index],
            device_id=partner,
            device_id_type=MESH,
        )
        copy.start()
        self.made.append([copy, False])
        return len(self.made) - 1

    def sent(self, *numbers):
        for number in numbers:
            if not self.made[number][1]:
                self.made[number][0].wait_send()
                self.made[number][1] = True

    def arrived(self, *numbers):
        for number in numbers:
            self.made[number][0].wait_recv()


def turned_by(field, cosine, sine):
    lane = lax.broadcasted_iota(jnp.int32, (1, 128), 1)
    lower = lane % HEAD_DIM < HEAD_DIM // 2
    halves = []
    for pair in range(field.shape[1] // 128):
        part = field[:, pair * 128 : pair * 128 + 128]
        swapped = jnp.where(lower, pltpu.roll(part, 96, 1), pltpu.roll(part, 32, 1))
        halves.append(part * cosine + swapped * sine)
    return jnp.concatenate(halves, 1)


def norm_of(source):
    centre = jnp.mean(source, -1, keepdims=True)
    centred = source - centre
    spread = lax.rsqrt(jnp.mean(centred * centred, -1, keepdims=True) + 1e-05)
    return centred * spread, spread


def norm_back(grad, unit, spread, gain):
    scaled = grad * gain
    inner = scaled - jnp.mean(scaled, -1, keepdims=True) - unit * jnp.mean(scaled * unit, -1, keepdims=True)
    return inner * spread


def column_sum(field):
    return jnp.sum(field, 0, keepdims=True)


def split_heads(pair):
    lane = lax.broadcasted_iota(jnp.int32, pair.shape, 1)
    zero = jnp.zeros_like(pair)
    return jnp.concatenate(
        [jnp.where(lane < HEAD_DIM, pair, zero), jnp.where(lane >= HEAD_DIM, pair, zero)], 0
    )


def join_heads(stacked):
    rows = stacked.shape[0] // 2
    lane = lax.broadcasted_iota(jnp.int32, (rows, 128), 1)
    return jnp.where(lane < HEAD_DIM, stacked[:rows], stacked[rows:])


def span(start, size):
    return pl.ds(pl.multiple_of(start, size), size)


def layer_kernel(
    bits,
    lengths, frames, cotangent, wq, wk, wv, wo, wg, wu, wd,
    gain1, bias1, gain2, bias2, scale1, scale2, rotary, rotary_start,
    out_frames, frames_grad, attn_grads_out, mlp_grads_out, vec_out, low_spill, head_spill, branch_spill,
    x0, x1, x2, x3, x4, x5, x6, x7, wo_other, att_other, core_g, core_m, side_g, side_m, wide, dk_sum, dv_sum,
    wg_buf, wu_buf, wd_buf, vec, vec_in, *rest,
):
    steps = len(bits)
    in_mlp, in_attn = rest[:steps], rest[steps : 2 * steps]
    load_sems, store_sems, send_sems, recv_sems = rest[2 * steps :]
    data, model = lax.axis_index("dp"), lax.axis_index("mp")
    core, side = model % 2, model // 2
    side_model = model + 2 - 4 * side
    core_dev, side_dev = (data, model + 1 - 2 * core), (data, side_model)
    own_bit = {bit: (data // bit) % 2 for bit in bits}
    bit_dev = {bit: (data + bit * (1 - 2 * own_bit[bit]), model) for bit in bits}
    data_dev = [bit_dev[bit] for bit in bits]

    def order_of(which):
        if which in (1, 4, 6) and steps > 1:
            return [bits[1], bits[0]] + bits[2:]
        return bits

    loads, stores, sends = Copies(load_sems), Copies(store_sems), Sends(send_sems, recv_sems)
    block = D // 2**steps

    rows_of = (1 - side, side)
    halves = (1 - core, core)

    def quarter_rows(group, slot):
        return span(rows_of[group] * ROW_LEN + halves[slot] * QUARTER, QUARTER)

    def own_rows(owner, step):
        return span(owner * QUARTER + step * PIECE, PIECE)

    def at_slot(slot, step):
        return pl.ds(slot * QUARTER + step * PIECE, PIECE)

    def piece(step):
        return pl.ds(step * PIECE, PIECE)

    frame_loads = []
    for index in range(2):
        for part in range(4):
            frame_loads.append(
                loads.start(
                    frames.at[span(rows_of[index] * ROW_LEN + part * PIECE, PIECE)],
                    x0.at[index, pl.ds(part * PIECE, PIECE)],
                )
            )
    weight_loads = [loads.start(wg, wg_buf), loads.start(wu, wu_buf), loads.start(wd, wd_buf)]
    cot_loads = {}
    for group in range(2):
        for slot in range(2):
            cot_loads[group, slot] = loads.start(
                cotangent.at[quarter_rows(group, slot)], x4.at[group, pl.ds(slot * QUARTER, QUARTER)]
            )
    barrier = pltpu.get_barrier_semaphore()
    partners = [core_dev, side_dev] + data_dev
    for partner in partners:
        pl.semaphore_signal(barrier, inc=1, device_id=partner, device_id_type=MESH)
    pl.semaphore_wait(barrier, len(partners))

    def clip_facts(index, first, count):
        frame_ids = lax.broadcasted_iota(jnp.int32, (count, 128), 0) + first
        start_ids = jnp.zeros((count, 128), jnp.int32)
        end = 0
        for slot in range(SLOTS):
            length = lengths[rows_of[index], slot]
            end = end + length
            start_ids = start_ids + jnp.where(frame_ids >= end, length, 0)
        return frame_ids, start_ids

    def angles(index, first, count, direction):
        frame_ids = lax.broadcasted_iota(jnp.int32, (count, 128), 0) + first
        start_cos = jnp.broadcast_to(rotary_start[0, 0:1], (count, 128))
        start_sin = jnp.broadcast_to(rotary_start[1, 0:1], (count, 128))
        end = 0
        for slot in range(SLOTS):
            end = end + lengths[rows_of[index], slot]
            number = lax.div(end, jnp.int32(CLIP_UNIT))
            passed = frame_ids >= end
            start_cos = jnp.where(passed, rotary_start[0, pl.ds(number, 1)], start_cos)
            start_sin = jnp.where(passed, rotary_start[1, pl.ds(number, 1)], start_sin)
        frame_cos, frame_sin = rotary[0, pl.ds(first, count)], rotary[1, pl.ds(first, count)]
        lane = lax.broadcasted_iota(jnp.int32, (count, 128), 1)
        cosine = frame_cos * start_cos + frame_sin * start_sin
        sine = frame_sin * start_cos - frame_cos * start_sin
        sign = jnp.where(lane % HEAD_DIM < HEAD_DIM // 2, -direction, direction)
        return cosine, sine * sign

    def window(index, number):
        lead = 1 - (7 - number) // 7
        first = pl.multiple_of(number * WINDOW, WINDOW)
        key_first = pl.multiple_of((number - lead) * WINDOW, WINDOW)
        frame_ids, start_ids = clip_facts(index, first, WINDOW)
        limit = jnp.minimum(frame_ids - start_ids, WINDOW - 1)
        limit = jnp.concatenate([limit, limit], 1)
        row_ids = lax.broadcasted_iota(jnp.int32, (WINDOW, 2 * WINDOW), 0)
        col_ids = lax.broadcasted_iota(jnp.int32, (WINDOW, 2 * WINDOW), 1)
        distance = row_ids - col_ids + lead * WINDOW
        bias = jnp.where((distance >= 0) & (distance <= limit), 0.0, -1e30)
        return pl.ds(first, WINDOW), pl.ds(key_first, 2 * WINDOW), jnp.concatenate([bias, bias], 0)

    def columns(kind, pair=None):
        if pair is None:
            return slice(kind * HEADS_WIDE, kind * HEADS_WIDE + HEADS_WIDE)
        return slice(kind * HEADS_WIDE + pair * 128, kind * HEADS_WIDE + pair * 128 + 128)

    other_weight = sends.start(wo, wo_other, side_dev)
    att_sent, spills, core_sent, side_low, core_low = [], [], [], [], []
    ones = jnp.ones((2 * WINDOW, 128), BF16)
    for index in range(2):
        for part in range(4):
            frame_loads[index * 4 + part].wait()

        @pl.loop(0, ROW_LEN // PIECE)
        def _(step):
            rows = span(step * PIECE, PIECE)
            unit, _spread = norm_of(x0[index, rows].astype(F32))
            low = (unit * gain1[...] + bias1[...]).astype(BF16)
            x1[index, rows] = low
            cosine, sine = angles(index, pl.multiple_of(step * PIECE, PIECE), PIECE, 1.0)
            x2[index, rows, columns(0)] = turned_by(product(low, wq[...], 1, 0), cosine, sine).astype(BF16)
            x2[index, rows, columns(1)] = turned_by(product(low, wk[...], 1, 0), cosine, sine).astype(BF16)
            x2[index, rows, columns(2)] = product(low, wv[...], 1, 0).astype(BF16)

        spills.append(stores.start(x1.at[index], low_spill.at[index]))

        def attend(half, step):
            for inner in range(PIECE // WINDOW):
                rows, key_rows, bias = window(index, half * 4 + step * 2 + inner)
                for pair in range(2):
                    query = split_heads(x2[index, rows, columns(0, pair)])
                    scores = product(query, x2[index, key_rows, columns(1, pair)], 1, 1)
                    scores = scores * HEAD_DIM**-0.5 + bias
                    expo = jnp.exp(scores - jnp.max(scores, -1, keepdims=True)).astype(BF16)
                    values = jnp.concatenate([x2[index, key_rows, columns(2, pair)], ones], 1)
                    result = product(expo, values, 1, 0)
                    x2[index, rows, columns(3, pair)] = (
                        join_heads(result[:, :128]) / join_heads(result[:, 128:])
                    ).astype(BF16)

        for step in range(2):
            if index == 0:
                for half in range(2):
                    attend(half, step)
                    rows = pl.ds(half * QUARTER + step * PIECE, PIECE)
                    att_sent.append(sends.start(x2.at[0, rows, columns(3)], att_other.at[rows], side_dev))
                continue

            for slot in range(2):
                attend(halves[slot], step)
                if step == 0 and slot == 0:
                    sends.arrived(other_weight)
                if slot == 0:
                    sends.arrived(att_sent[2 * step], att_sent[2 * step + 1])
                rows = span(halves[slot] * QUARTER + step * PIECE, PIECE)
                fresh = product(x2[1, rows, columns(3)], wo[...], 1, 0) + product(
                    att_other[rows], wo_other[...], 1, 0
                )
                if slot == 0:
                    x5[1, piece(step)] = fresh.astype(BF16)
                    core_sent.append(sends.start(x5.at[1, piece(step)], core_g.at[1, piece(step)], core_dev))
                else:
                    wide[piece(step)] = fresh
            sends.arrived(core_sent[step])

            @pl.loop(0, PIECE // SMALL)
            def _(small):
                here = span(step * PIECE + small * SMALL, SMALL)
                there = span(QUARTER + step * PIECE + small * SMALL, SMALL)
                branch = wide[here] + core_g[1, here].astype(F32)
                wide[here] = branch
                source = x0[1, span(core * QUARTER + step * PIECE + small * SMALL, SMALL)].astype(F32)
                unit, _spread = norm_of(source + scale1[...] * branch)
                x3[1, there] = (unit * gain2[...] + bias2[...]).astype(BF16)

            rows = at_slot(1, step)
            side_low.append(sends.start(x3.at[1, rows], x3.at[0, rows], side_dev))
            core_low.append(sends.start(x3.at[1, rows], x3.at[1, at_slot(0, step)], core_dev))
        spills.append(stores.start(x2.at[index], head_spill.at[index]))

    spills.append(stores.start(wide, branch_spill))
    for copy in spills + weight_loads:
        copy.wait()
    sends.sent(*core_sent, *att_sent)
    vec[...] = jnp.zeros((8, D), F32)

    def chunk(group, slot, step):
        rows = at_slot(slot, step)
        low = x3[group, rows]
        grad = (scale2[...] * x4[group, rows].astype(F32)).astype(BF16)
        x4[group, rows] = grad
        for tile in range(4):
            cols = slice(tile * 256, tile * 256 + 256)
            gating = product(low, wg_buf[:, cols], 1, 0)
            upward = product(low, wu_buf[:, cols], 1, 0)
            grad_hidden = product(grad, wd_buf[cols], 1, 1)
            sigma = 0.5 * jnp.tanh(0.5 * gating) + 0.5
            active = gating * sigma
            x0[group, rows, cols] = (active * upward).astype(BF16)
            x1[group, rows, cols] = (grad_hidden * upward * (sigma + active * (1.0 - sigma))).astype(BF16)
            x2[group, rows, cols] = (grad_hidden * active).astype(BF16)
        for tile in range(4):
            cols = slice(tile * 256, tile * 256 + 256)
            x5[group, rows, cols] = (
                product(x1[group, rows], wg_buf[cols], 1, 1) + product(x2[group, rows], wu_buf[cols], 1, 1)
            ).astype(BF16)
            x6[group, rows, cols] = product(x0[group, rows], wd_buf[:, cols], 1, 0).astype(BF16)

    core_grad, core_part, side_grad, core_again, side_mlp = {}, {}, [], [], []
    for group, step in ((1, 0), (0, 0), (0, 1), (1, 1)):
        if group == 1:
            sends.arrived(core_low[step])
        else:
            sends.arrived(side_low[step])
            core_again.append(sends.start(x3.at[0, at_slot(1, step)], x3.at[0, at_slot(0, step)], core_dev))
            sends.arrived(core_again[step])
        for slot in range(2):
            if step == 0:
                cot_loads[group, slot].wait()
            chunk(group, slot, step)
            if slot == 0:
                rows = at_slot(0, step)
                core_grad[group, step] = sends.start(x5.at[group, rows], core_g.at[group, piece(step)], core_dev)
                core_part[group, step] = sends.start(x6.at[group, rows], core_m.at[group, piece(step)], core_dev)
        if group == 0:
            rows = at_slot(1, step)
            sends.arrived(core_grad[0, step])
            x5[0, rows] = (x5[0, rows].astype(F32) + core_g[0, piece(step)].astype(F32)).astype(BF16)
            side_grad.append(sends.start(x5.at[0, rows], side_g.at[piece(step)], side_dev))
            sends.arrived(core_part[0, step])
            x6[0, rows] = (x6[0, rows].astype(F32) + core_m[0, piece(step)].astype(F32)).astype(BF16)
            if step == 1:
                side_mlp.append(sends.start(x6.at[0, at_slot(1, 0)], side_m.at[piece(0)], side_dev))

    quarter_loads = [
        loads.start(frames.at[span(model * QUARTER, QUARTER)], wd_buf.at[pl.ds(0, QUARTER)]),
        loads.start(cotangent.at[span(model * QUARTER, QUARTER)], wd_buf.at[pl.ds(QUARTER, QUARTER)]),
    ]
    low_loads = [loads.start(low_spill.at[0], wg_buf), loads.start(low_spill.at[1], wu_buf)]

    def kept(which, half, start, size):
        if which == 0:
            return x6.at[half, pl.ds(start, size)]
        if which == 1:
            return x1.at[0, pl.ds(half * QUARTER + start, size)]
        if which == 2:
            return x3.at[0, pl.ds(half * QUARTER + start, size)]
        return x3.at[1, pl.ds(half * QUARTER + start, size), columns(which - 3)]

    def arriving(level, which):
        return in_mlp[level].at[which] if which < 3 else in_attn[level].at[which - 3]

    data_sent = {}

    def place_blocks(which, tile, total, cols):
        fresh = total.astype(BF16)
        for number in range(QUARTER // block):
            natural = tile * (QUARTER // block) + number
            whole = sum(((natural // bit) % 2) << place for place, bit in enumerate(order_of(which)))
            target = kept(which, whole % 2, (whole // 2) * block, block)
            target[:, cols] = fresh[number * block : number * block + block]

    def send_half(which):
        data_sent[0, which] = sends.start(
            kept(which, 1 - own_bit[order_of(which)[0]], 0, QUARTER),
            arriving(0, which),
            bit_dev[order_of(which)[0]],
        )

    def mlp_grad(which):
        left, right = ((x3, x1), (x3, x2), (x4, x0))[which]
        for tile in range(2):

            @pl.loop(0, 2)
            def _(part):
                cols = span(part * 512, 512)
                total = None
                for group in range(2):
                    fresh = product(left[group, :, tile * 512 : tile * 512 + 512], right[group, :, cols], 0, 0)
                    total = fresh if total is None else total + fresh
                place_blocks(which, tile, total, cols)

        send_half(which)

    def data_step(level, which):
        copy = data_sent[level, which]
        order = order_of(which)
        mine = [own_bit[bit] for bit in order]
        sends.arrived(copy)
        sends.sent(copy)
        size = QUARTER >> level
        source_half = mine[0] if level % 2 == 0 else 1 - mine[0]
        offset = 0 if level == 0 else mine[level] * size
        come = arriving(level, which)
        for number in range(size // block):
            own = kept(which, source_half, offset + number * block, block)[...]
            fresh = own.astype(F32) + come[number * block : number * block + block].astype(F32)
            if level == steps - 1:
                if which < 3:
                    wide[which * block : which * block + block] = fresh
                else:
                    wide[3 * block : 4 * block, columns(which - 3)] = fresh
            else:
                target = kept(
                    which, 1 - source_half, (number % 2) * (size // 2) + (number // 2) * block, block
                )
                target[...] = fresh.astype(BF16)
        if level < steps - 1:
            away = 1 - mine[level + 1]
            data_sent[level + 1, which] = sends.start(
                kept(which, 1 - source_half, away * (size // 2), size // 2),
                arriving(level + 1, which),
                bit_dev[order[level + 1]],
            )

    side_branch, core_branch = [], []

    def own_backward(step):
        sends.arrived(core_grad[1, step], side_grad[step])

        @pl.loop(0, PIECE // SMALL)
        def _(small):
            here = span(step * PIECE + small * SMALL, SMALL)
            there = span(QUARTER + step * PIECE + small * SMALL, SMALL)
            branch = wide[here]
            grad_out = wd_buf[there].astype(F32)
            midway = wd_buf[here].astype(F32) + scale1[...] * branch
            grad_norm = x5[1, there].astype(F32) + core_g[1, here].astype(F32) + side_g[here].astype(F32)
            unit, spread = norm_of(midway)
            vec[2:3] += column_sum(grad_norm * unit)
            vec[3:4] += column_sum(grad_norm)
            grad_mid = grad_out + norm_back(grad_norm, unit, spread, gain2[...])
            vec[4:5] += column_sum(grad_mid * branch)
            x7[1, there] = (scale1[...] * grad_mid).astype(BF16)
            wide[here] = grad_mid

        rows = at_slot(1, step)
        core_branch.append(sends.start(x7.at[1, rows], x7.at[1, at_slot(0, step)], core_dev))
        side_branch.append(sends.start(x7.at[1, rows], x7.at[0, rows], side_dev))

    def row_back(index, between):
        for slot in range(2):

            @pl.loop(0, QUARTER // PIECE)
            def _(step):
                rows = span(halves[slot] * QUARTER + step * PIECE, PIECE)
                x4[index, rows, columns(3)] = product(
                    x7[index, span(slot * QUARTER + step * PIECE, PIECE)], wo[...], 1, 1
                ).astype(BF16)

        dk_sum[...] = jnp.zeros(dk_sum.shape, F32)
        dv_sum[...] = jnp.zeros(dv_sum.shape, F32)

        @pl.loop(0, ROW_LEN // PIECE)
        def _(step):
            for inner in range(PIECE // WINDOW):
                rows, key_rows, bias = window(index, step * 2 + inner)
                for pair in range(2):
                    lanes = slice(pair * 128, pair * 128 + 128)
                    query = split_heads(x2[index, rows, columns(0, pair)])
                    keys = x2[index, key_rows, columns(1, pair)]
                    values = x2[index, key_rows, columns(2, pair)]
                    grad = split_heads(x4[index, rows, columns(3, pair)])
                    scores = product(query, keys, 1, 1) * HEAD_DIM**-0.5 + bias
                    expo = jnp.exp(scores - jnp.max(scores, -1, keepdims=True))
                    inverse = 1.0 / product(expo.astype(BF16), ones, 1, 0)
                    probs = expo * jnp.concatenate([inverse, inverse], 1)
                    grad_probs = product(grad, values, 1, 1)
                    inside = grad.astype(F32) * split_heads(x2[index, rows, columns(3, pair)]).astype(F32)
                    inside = product(inside.astype(BF16), ones[:128], 1, 0)
                    inside = jnp.concatenate([inside, inside], 1)
                    grad_logits = (probs * (grad_probs - inside) * HEAD_DIM**-0.5).astype(BF16)
                    x4[index, rows, columns(0, pair)] = join_heads(product(grad_logits, keys, 1, 0)).astype(BF16)
                    dk_sum[key_rows, lanes] += product(grad_logits, query, 0, 0)
                    dv_sum[key_rows, lanes] += product(probs.astype(BF16), grad, 0, 0)

        between()

        for slot in range(2):

            @pl.loop(0, QUARTER // PIECE)
            def _(step):
                first = pl.multiple_of(halves[slot] * QUARTER + step * PIECE, PIECE)
                rows = pl.ds(first, PIECE)
                cosine, sine = angles(index, first, PIECE, -1.0)
                grad_q = turned_by(x4[index, rows, columns(0)].astype(F32), cosine, sine).astype(BF16)
                grad_k = turned_by(dk_sum[rows].astype(BF16).astype(F32), cosine, sine).astype(BF16)
                grad_v = dv_sum[rows].astype(BF16)
                x4[index, rows, columns(0)] = grad_q
                x4[index, rows, columns(1)] = grad_k
                x4[index, rows, columns(2)] = grad_v
                x5[index, span(slot * QUARTER + step * PIECE, PIECE)] = (
                    product(grad_q, wq[...], 1, 1) + product(grad_k, wk[...], 1, 1) + product(grad_v, wv[...], 1, 1)
                ).astype(BF16)

            if slot == 0:
                return_sent[index] = sends.start(x5.at[index, pl.ds(0, QUARTER)], core_g.at[index], core_dev)

    return_sent = {}

    def attn_grad(which):
        kind = which - 3
        for tile in range(2):
            cols = slice(tile * 512, tile * 512 + 512)
            total = None
            for index in range(2):
                if kind < 3:
                    left = (wg_buf, wu_buf)[index]
                    pairs = [(left[:, cols], x4[index, :, columns(kind)])]
                else:
                    pairs = [
                        (
                            x7[index, pl.ds(slot * QUARTER, QUARTER), cols],
                            x2[index, span(halves[slot] * QUARTER, QUARTER), columns(3)],
                        )
                        for slot in range(2)
                    ]
                for left, right in pairs:
                    fresh = product(left, right, 0, 0)
                    total = fresh if total is None else total + fresh
            place_blocks(which, tile, total, slice(None))
        send_half(which)

    sends.sent(*core_part.values())
    mlp_grad(0)
    for copy in quarter_loads:
        copy.wait()
    own_backward(0)
    mlp_grad(1)
    head_load = loads.start(head_spill, x2)
    own_backward(1)
    sends.sent(*core_low, *side_low, *core_again)
    mlp_grad(2)
    side_mlp.append(sends.start(x6.at[0, at_slot(1, 1)], side_m.at[piece(1)], side_dev))
    sends.arrived(*core_branch)
    head_load.wait()
    sends.sent(*core_grad.values(), *side_grad)
    row_back(1, lambda: None)
    core_frames, side_frames = [], []

    def branch_back(step):
        return [
            loads.start(branch_spill.at[piece(step), pl.ds(part * 256, 256)], dk_sum.at[pl.ds(part * PIECE, PIECE)])
            for part in range(4)
        ]

    def own_frames(step, branch_loads):
        sends.arrived(core_part[1, step], side_mlp[step])
        for part in range(4):
            branch_loads[part].wait()
            cols = slice(part * 256, part * 256 + 256)
            here, there = piece(step), at_slot(1, step)
            mlp_branch = x6[1, there, cols].astype(F32) + core_m[1, here, cols].astype(F32) + side_m[here, cols].astype(F32)
            vec[5:6, cols] += column_sum(wd_buf[there, cols].astype(F32) * mlp_branch)
            midway = wd_buf[here, cols].astype(F32) + scale1[:, cols] * dk_sum[pl.ds(part * PIECE, PIECE)]
            x6[1, there, cols] = (midway + scale2[:, cols] * mlp_branch).astype(BF16)
        core_frames.append(sends.start(x6.at[1, at_slot(1, step)], out_frames.at[own_rows(model, step)], core_dev))

    def side_frame(step):
        side_frames.append(sends.start(x6.at[1, at_slot(1, step)], out_frames.at[own_rows(model, step)], side_dev))

    branch_loads = branch_back(0)
    gathered = []
    for step in range(2):
        sends.arrived(side_branch[step])
        gathered.append(sends.start(x7.at[0, at_slot(1, step)], x7.at[0, at_slot(0, step)], core_dev))
    data_step(0, 0)
    own_frames(0, branch_loads)
    side_frame(0)
    data_step(0, 1)
    sends.arrived(*gathered)

    def second_level(*chosen):
        if steps > 1:
            for which in chosen:
                data_step(1, which)

    attn_grad(6)
    row_back(0, lambda: second_level(0))
    sends.arrived(return_sent[0])
    side_return = []
    for step in range(2):
        rows = at_slot(1, step)
        x5[0, rows] = (x5[0, rows].astype(F32) + core_g[0, piece(step)].astype(F32)).astype(BF16)
        side_return.append(sends.start(x5.at[0, rows], side_g.at[piece(step)], side_dev))
    branch_loads = branch_back(1)
    for copy in low_loads:
        copy.wait()
    attn_grad(3)
    data_step(0, 2)
    second_level(1)
    for which in (4, 5):
        attn_grad(which)
    own_frames(1, branch_loads)
    final_stores = [stores.start(x6.at[1, pl.ds(QUARTER, QUARTER)], out_frames.at[span(model * QUARTER, QUARTER)])]

    sends.arrived(return_sent[1])
    core_out, side_out = [], []
    for step in range(2):
        sends.arrived(side_return[step])

        @pl.loop(0, PIECE // SMALL)
        def _(small):
            here = span(step * PIECE + small * SMALL, SMALL)
            there = span(QUARTER + step * PIECE + small * SMALL, SMALL)
            grad_norm = x5[1, there].astype(F32) + core_g[1, here].astype(F32) + side_g[here].astype(F32)
            unit, spread = norm_of(wd_buf[here].astype(F32))
            vec[0:1] += column_sum(grad_norm * unit)
            vec[1:2] += column_sum(grad_norm)
            x5[1, there] = (wide[here] + norm_back(grad_norm, unit, spread, gain1[...])).astype(BF16)

        rows = at_slot(1, step)
        side_out.append(sends.start(x5.at[1, rows], frames_grad.at[own_rows(model, step)], side_dev))
        core_out.append(sends.start(x5.at[1, rows], frames_grad.at[own_rows(model, step)], core_dev))
        if step == 0:
            side_frame(1)
            second_level(2)
    final_stores.append(stores.start(x5.at[1, pl.ds(QUARTER, QUARTER)], frames_grad.at[span(model * QUARTER, QUARTER)]))

    vec_devs, vec_sent = partners, []

    def vec_step():
        level = len(vec_sent)
        if level == len(vec_devs):
            return
        if level > 0:
            sends.arrived(vec_sent[-1])
            sends.sent(vec_sent[-1])
            vec[...] += vec_in[level - 1]
        if level < len(vec_devs):
            vec_sent.append(sends.start(vec, vec_in.at[level], vec_devs[level]))

    last = []

    def second_hop(arriving_copy, target, step):
        sends.arrived(arriving_copy)
        rows = own_rows(side_model, step)
        last.append(sends.start(target.at[rows], target.at[rows], core_dev))

    vec_step()
    second_hop(side_frames[0], out_frames, 0)
    for which in (6, 3):
        data_step(0, which)
    vec_step()
    for which in (4, 5):
        data_step(0, which)
    vec_step()
    for level in range(2, steps):
        if level == 2:
            second_level(6, 3)
            vec_step()
            second_level(4, 5)
            vec_step()
        for which in (0, 1, 2):
            data_step(level, which)
        if level == 2:
            second_hop(side_out[0], frames_grad, 0)
        for which in (6, 3, 4, 5):
            data_step(level, which)
    while len(vec_sent) < len(vec_devs):
        vec_step()
    sends.arrived(vec_sent[-1])
    sends.sent(vec_sent[-1])
    vec_out[...] = vec[...] + vec_in[len(vec_devs) - 1]
    for which in range(3):
        final_stores.append(stores.start(wide.at[pl.ds(which * block, block)], mlp_grads_out.at[which]))
    final_stores.append(stores.start(wide.at[pl.ds(3 * block, block)], attn_grads_out))
    second_hop(side_frames[1], out_frames, 1)
    second_hop(side_out[1], frames_grad, 1)
    sends.arrived(*core_frames, *core_out, *last)
    sends.sent(*range(len(sends.made)))
    for copy in final_stores:
        copy.wait()


def layer(parts, lengths, frames, cotangent, wq, wk, wv, wo, wg, wu, wd, gain1, bias1, gain2, bias2, scale1, scale2):
    shape = jax.ShapeDtypeStruct
    sems = pltpu.SemaphoreType.DMA
    block = D // parts
    bits = []
    while 2 ** len(bits) < parts:
        bits.append(2 ** len(bits))
    steps = len(bits)
    rotary, rotary_start = rotary_constants()
    whole = pltpu.VMEM((2, ROW_LEN, D), BF16)
    row = pltpu.VMEM((2, QUARTER, D), BF16)
    single = pltpu.VMEM((QUARTER, D), BF16)
    square = pltpu.VMEM((D, D), BF16)
    sums = pltpu.VMEM((ROW_LEN, HEADS_WIDE), F32)
    ins_mlp = [pltpu.VMEM((3, QUARTER >> level, D), BF16) for level in range(steps)]
    ins_attn = [pltpu.VMEM((4, QUARTER >> level, HEADS_WIDE), BF16) for level in range(steps)]
    vmem, hbm = pl.BlockSpec(memory_space=pltpu.VMEM), pl.BlockSpec(memory_space=pl.ANY)
    smem = pl.BlockSpec(memory_space=pltpu.SMEM)
    send_count = 56 + 8 * steps
    return pl.pallas_call(
        functools.partial(layer_kernel, bits),
        out_shape=(
            shape((2 * ROW_LEN, D), BF16),
            shape((2 * ROW_LEN, D), BF16),
            shape((block, 4 * HEADS_WIDE), F32),
            shape((3, block, D), F32),
            shape((8, D), F32),
            shape((2, ROW_LEN, D), BF16),
            shape((2, ROW_LEN, D), BF16),
            shape((QUARTER, D), F32),
        ),
        in_specs=[smem, hbm, hbm] + [vmem] * 4 + [hbm] * 3 + [vmem] * 8,
        out_specs=(hbm, hbm, hbm, hbm, vmem, hbm, hbm, hbm),
        scratch_shapes=[
            *[whole] * 8,
            pltpu.VMEM((HEADS_WIDE, D), BF16),
            pltpu.VMEM((ROW_LEN, HEADS_WIDE), BF16),
            row, row, single, single,
            pltpu.VMEM((QUARTER, D), F32),
            sums, sums, square, square, square,
            pltpu.VMEM((8, D), F32),
            pltpu.VMEM((steps + 2, 8, D), F32),
            *ins_mlp, *ins_attn,
            sems((32,)), sems((16,)), sems((send_count,)), sems((send_count,)),
        ],
        compiler_params=pltpu.CompilerParams(
            collective_id=1, has_side_effects=True, vmem_limit_bytes=64 * MIB
        ),
        name="layer",
    )(lengths, frames, cotangent, wq, wk, wv, wo, wg, wu, wd, gain1, bias1, gain2, bias2, scale1, scale2, rotary, rotary_start)


def deliver_kernel(
    frames_in, grad_in, attn_in, mlp_in, frames_to, grad_to, q_to, k_to, v_to, o_to, gate_to, up_to, down_to,
    frames_buf, grad_buf, attn_buf, mlp_buf, o_turned, down_turned, load_sems, store_sems,
):
    loads, stores = Copies(load_sems), Copies(store_sems)
    attn_load, mlp_load = loads.start(attn_in, attn_buf), loads.start(mlp_in, mlp_buf)
    count = frames_in.shape[0] // 4
    moves, waits = [], []
    for source, buf, target in ((frames_in, frames_buf, frames_to), (grad_in, grad_buf, grad_to)):
        for part in range(4):
            rows = pl.ds(part * count, count)
            moves.append((loads.start(source.at[rows], buf.at[rows]), buf.at[rows], target.at[rows]))
    attn_load.wait()
    for kind, target in enumerate((q_to, k_to, v_to)):
        waits.append(stores.start(attn_buf.at[:, pl.ds(kind * HEADS_WIDE, HEADS_WIDE)], target))
    mlp_load.wait()
    waits.append(stores.start(mlp_buf.at[0], gate_to))
    waits.append(stores.start(mlp_buf.at[1], up_to))
    for load, source, target in moves:
        load.wait()
        waits.append(stores.start(source, target))
    o_turned[...] = attn_buf[:, 3 * HEADS_WIDE :].T
    waits.append(stores.start(o_turned, o_to))
    down_turned[...] = mlp_buf[2].T
    waits.append(stores.start(down_turned, down_to))
    for copy in waits:
        copy.wait()


def deliver(frames_in, grad_in, attn_in, mlp_in):
    shape = jax.ShapeDtypeStruct
    block = attn_in.shape[0]
    hbm = pl.BlockSpec(memory_space=pl.ANY)
    small, large = (block, HEADS_WIDE), (block, D)
    return pl.pallas_call(
        deliver_kernel,
        out_shape=(
            shape(frames_in.shape, BF16), shape(grad_in.shape, BF16),
            shape(small, F32), shape(small, F32), shape(small, F32), shape(small[::-1], F32),
            shape(large, F32), shape(large, F32), shape(large[::-1], F32),
        ),
        in_specs=[hbm] * 4,
        out_specs=(hbm,) * 9,
        scratch_shapes=[
            pltpu.VMEM(frames_in.shape, BF16), pltpu.VMEM(grad_in.shape, BF16),
            pltpu.VMEM((block, D), F32), pltpu.VMEM((3, block, D), F32),
            pltpu.VMEM(small[::-1], F32), pltpu.VMEM(large[::-1], F32),
            pltpu.SemaphoreType.DMA((10,)), pltpu.SemaphoreType.DMA((15,)),
        ],
        compiler_params=pltpu.CompilerParams(vmem_limit_bytes=62 * MIB),
        name="deliver",
    )(frames_in, grad_in, attn_in, mlp_in)


def per_device(
    parts, frames, clip_lengths, query_weight, key_weight, value_weight, output_weight, gate_weight, up_weight,
    down_weight, attn_gain, attn_bias, mlp_gain, mlp_bias, attn_scale, mlp_scale, cotangent,
):
    out_frames, frames_grad, attn_part, mlp_part, vec = layer(
        parts, clip_lengths, frames, cotangent, query_weight, key_weight, value_weight, output_weight,
        gate_weight, up_weight, down_weight,
        *[vector.reshape(1, D) for vector in (attn_gain, attn_bias, mlp_gain, mlp_bias, attn_scale, mlp_scale)],
    )[:5]
    block = D // parts
    vec = lax.dynamic_slice_in_dim(vec, lax.axis_index("dp") * block, block, 1)
    arrays = deliver(out_frames, frames_grad, attn_part, mlp_part)
    return tuple(arrays) + tuple(vec[kind] for kind in range(6))


def solution(mesh):
    rows, whole = P("dp", None), P()
    in_weight, out_weight = P(None, "mp"), P("mp", None)
    in_specs = (
        (rows, rows, in_weight, in_weight, in_weight, out_weight, in_weight, in_weight, out_weight)
        + (whole,) * 6
        + (rows,)
    )
    scattered, turned = P("dp", "mp"), P("mp", "dp")
    out_specs = (
        rows, rows, scattered, scattered, scattered, turned, scattered, scattered, turned,
    ) + (P("dp"),) * 6
    return jax.shard_map(
        functools.partial(per_device, mesh.shape["dp"]),
        mesh=mesh,
        in_specs=in_specs,
        out_specs=out_specs,
        check_vma=False,
    )
```
